32 devices in a mesh: shard: 4 (over y, x), replica: 8 (over z, core).
Axes of the slice: x: 2, y: 2, z: 4, core: 2. Of those that a mesh axis runs over, the one named last changes fastest.
Arguments:
- hidden_in: bfloat16 [1024, 16, 1600], P('shard', 'replica'), may hold values from -6 to 6
- out_grad: bfloat16 [1024, 16, 1600], P('shard', 'replica'), may hold values from -6 to 6
- segments: int32 [1024, 16], P(None, 'replica'), may hold values from 0 to 17, as said below
- ln1_gain: float32 [1600], replicated, may hold values from 0.1 to 1.9
- ln1_bias: float32 [1600], replicated, may hold values from -1.5 to 1.5
- qkv_weight: bfloat16 [4800, 1600], P('shard'), may hold values from -0.15625 to 0.15625
- q_bias: float32 [1600], replicated, may hold values from -2.5 to 2.5
- v_bias: float32 [1600], replicated, may hold values from -2.5 to 2.5
- output_projection_weight: bfloat16 [1600, 1600], P('shard'), may hold values from -0.875 to 0.875
- out_bias: float32 [1600], replicated, may hold values from -1.5 to 1.5
- ln2_gain: float32 [1600], replicated, may hold values from 0.1 to 1.9
- ln2_bias: float32 [1600], replicated, may hold values from -1.5 to 1.5
- up_weight: bfloat16 [6400, 1600], P('shard'), may hold values from -0.15625 to 0.15625
- up_bias: float32 [6400], replicated, may hold values from -2.5 to 2.5
- down_weight: bfloat16 [1600, 6400], P('shard'), may hold values from -0.078125 to 0.078125
- down_bias: float32 [1600], replicated, may hold values from -1.5 to 1.5
Outputs:
- block_out: bfloat16 [1024, 16, 1600], P('shard', 'replica')
- input_grad: float32 [1024, 16, 1600], P('shard', 'replica')
- ln1_gain_grad: float32 [1600], replicated
- ln1_bias_grad: float32 [1600], replicated
- qkv_weight_grad: float32 [4800, 1600], P('shard')
- q_bias_grad: float32 [1600], replicated
- v_bias_grad: float32 [1600], replicated
- out_weight_grad: float32 [1600, 1600], P('shard')
- out_bias_grad: float32 [1600], replicated
- ln2_gain_grad: float32 [1600], replicated
- ln2_bias_grad: float32 [1600], replicated
- up_weight_grad: float32 [6400, 1600], P('shard')
- up_bias_grad: float32 [6400], replicated
- down_weight_grad: float32 [1600, 6400], P('shard')
- down_bias_grad: float32 [1600], replicated
The draws below stay inside these ranges and needn't reach their ends.
Inputs may be any that keep to these rules, and one draw needn't show every extreme that they name: `segments`: in each sequence the numbers start at 0 and rise by 0 or 1 from one position to the next; every document but a sequence's last has 60 to 800 tokens; of the 2 sequences of one index of replica, one is a single document.
All inputs are finite; a program needn't handle non-finite values.
Results may differ from the reference program's by a relative error of at most 0.019.
Values may be sent and summed in bfloat16 or wider, within the bound.
No kernel may reach another device: no remote copies, remote signals or barrier semaphores. Data moves between devices by JAX's collectives and lax.ppermute only.
A program may use at most 448 MiB of HBM per device.

```python
import jax
import jax.numpy as jnp
from jax import lax

D = 1600
HEADS = 25
HDIM = 64
FF = 6400
LENGTH = 1024
MINDOC = 60
MAX_DOC_TOKENS = 800
SEQS = 2
NSEQ = 16


def draw_segments(key, part):
    key = jax.random.fold_in(key, 7)
    len_key, pick_key = jax.random.split(key)
    doc_count = LENGTH // MINDOC + 1
    doc_lengths = jax.random.randint(len_key, (NSEQ, doc_count), MINDOC, MAX_DOC_TOKENS + 1)
    groups = NSEQ // SEQS
    selected_rows = jax.random.randint(pick_key, (groups,), 0, SEQS)
    row_ids = jnp.arange(NSEQ)
    densest = (selected_rows[0] + 1) % SEQS
    doc_lengths = jnp.where((row_ids == densest)[:, None], MINDOC, doc_lengths)
    doc_ends = jnp.cumsum(doc_lengths, axis=1)
    places = jnp.arange(LENGTH)
    seg_ids = jnp.sum((doc_ends[:, None, :] <= places[None, :, None]).astype(jnp.int32), axis=2)
    single = row_ids % SEQS == selected_rows[row_ids // SEQS]
    seg_ids = jnp.where(single[:, None], 0, seg_ids)
    return seg_ids.T.astype(jnp.int32)


def block_levels(rng, extent, cuts, low, high):
    level, own = 1.0, jax.random.fold_in(rng, 6)
    for axis_at, shards_of in cuts:
        draws = jnp.exp(jax.random.uniform(jax.random.fold_in(own, axis_at), (shards_of,), jnp.float32, low / len(cuts), high / len(cuts)))
        level = level * jnp.repeat(draws, extent[axis_at] // shards_of).reshape([-1 if axis == axis_at else 1 for axis in range(len(extent))])
    return level


def bell_draw(key, dims, scale, bound, cuts=(), kind=jnp.bfloat16):
    loudness = block_levels(key, dims, cuts, -0.22, 0.18) if cuts else 1.0
    values = jax.random.normal(key, dims, jnp.float32) * scale * loudness
    return jnp.minimum(jnp.maximum(values, -bound), bound).astype(kind)


def setup_inputs(seed: int = 0) -> dict:
    seeds = jax.random.split(jax.random.key(seed), 17)
    hidden_in = bell_draw(seeds[0], (LENGTH, NSEQ, D), 1.0, 6.0, ((0, 4), (1, 8)))
    out_grad = bell_draw(seeds[1], (LENGTH, NSEQ, D), 1.0, 6.0, ((0, 4), (1, 8)))
    segments = draw_segments(jax.random.fold_in(seeds[16], 71), 0)
    ln1_gain = jnp.clip(1.0 + 0.18 * jax.random.normal(seeds[3], (D,), jnp.float32), 0.1, 1.9)
    ln1_bias = bell_draw(seeds[4], (D,), 0.3, 1.5, (), jnp.float32)
    qkv_weight = bell_draw(seeds[5], (3 * D, D), D ** -0.5, 0.15625, ((0, 4),))
    q_bias = bell_draw(seeds[6], (D,), 0.5, 2.5, (), jnp.float32)
    v_bias = bell_draw(seeds[7], (D,), 0.5, 2.5, (), jnp.float32)
    output_projection_weight = bell_draw(seeds[8], (D, D), (D // 32) ** -0.5, 0.875, ((0, 4),))
    out_bias = bell_draw(seeds[9], (D,), 0.3, 1.5, (), jnp.float32)
    ln2_gain = jnp.clip(1.0 + 0.18 * jax.random.normal(seeds[10], (D,), jnp.float32), 0.1, 1.9)
    ln2_bias = bell_draw(seeds[11], (D,), 0.3, 1.5, (), jnp.float32)
    up_weight = bell_draw(seeds[12], (FF, D), D ** -0.5, 0.15625, ((0, 4),))
    up_bias = bell_draw(seeds[13], (FF,), 0.5, 2.5, (), jnp.float32)
    down_weight = bell_draw(seeds[14], (D, FF), FF ** -0.5, 0.078125, ((0, 4),))
    down_bias = bell_draw(seeds[15], (D,), 0.3, 1.5, (), jnp.float32)
    return {"hidden_in": hidden_in, "out_grad": out_grad, "segments": segments, "ln1_gain": ln1_gain, "ln1_bias": ln1_bias, "qkv_weight": qkv_weight, "q_bias": q_bias, "v_bias": v_bias, "output_projection_weight": output_projection_weight, "out_bias": out_bias, "ln2_gain": ln2_gain, "ln2_bias": ln2_bias, "up_weight": up_weight, "up_bias": up_bias, "down_weight": down_weight, "down_bias": down_bias}


@jax.custom_vjp
def low(v):
    return lax.optimization_barrier(v.astype(jnp.bfloat16)).astype(jnp.float32)

@jax.custom_vjp
def low_back(v):
    return v

def low_keep(v):
    return (low(v), None)

def low_pass(kept, grad):
    return (grad,)

def back_keep(v):
    return (v, None)

def back_low(kept, grad):
    return (low(grad),)
low.defvjp(low_keep, low_pass)
low_back.defvjp(back_keep, back_low)

def layer_norm(value_rows, gain_vec, shift_vec):
    centre = value_rows - lax.optimization_barrier(jnp.mean(value_rows, axis=-1, keepdims=True))
    spread = lax.optimization_barrier(jnp.mean(centre * centre, axis=-1, keepdims=True))
    return centre * lax.rsqrt(spread + 1e-05) * gain_vec + shift_vec

def project(value_rows, weight_matrix):
    return jnp.einsum('zyv,xv->zyx', value_rows, weight_matrix, precision=lax.Precision.HIGHEST)

def forward(param_set, tokens, seg_ids):
    ln1_gain, ln1_bias, qkv_weight, q_bias, v_bias, output_projection_weight, out_bias, ln2_gain, ln2_bias, up_weight, up_bias, down_weight, down_bias = param_set
    seq_count, seq_len, width = tokens.shape
    normed = low(layer_norm(tokens, ln1_gain, ln1_bias))
    joined = project(normed, qkv_weight)
    queries = low(low_back(joined[..., :width] + q_bias))
    keys_all = low(low_back(joined[..., width:2 * width]))
    values_all = low(low_back(joined[..., 2 * width:] + v_bias))
    places = jnp.arange(seq_len)
    allowed = (seg_ids[:, :, None] == seg_ids[:, None, :]) & (places[None, :, None] >= places[None, None, :])

    def split_heads(array):
        return array.reshape(seq_count, seq_len, HEADS, HDIM).transpose(2, 0, 1, 3)

    def one_head(operands):
        head_q, head_k, head_v = operands
        scores = low_back(jnp.einsum('sqd,skd->sqk', head_q, head_k, precision=lax.Precision.HIGHEST) * 0.125)
        scores = jnp.where(allowed, scores, -1e+30)
        exp_terms = jnp.exp(scores - lax.optimization_barrier(jnp.max(scores, axis=-1, keepdims=True)))
        soft = exp_terms / lax.optimization_barrier(jnp.sum(exp_terms, axis=-1, keepdims=True))
        return jnp.einsum('sqk,skd->sqd', low(soft), head_v, precision=lax.Precision.HIGHEST)
    mixed = lax.map(jax.checkpoint(one_head), (split_heads(queries), split_heads(keys_all), split_heads(values_all)))
    mixed = low(low_back(mixed.transpose(1, 2, 0, 3).reshape(seq_count, seq_len, width)))
    branch = low_back(project(mixed, output_projection_weight) + out_bias)
    middle = tokens + branch
    normed_two = low(layer_norm(middle, ln2_gain, ln2_bias))
    pre_act = low_back(project(normed_two, up_weight) + up_bias)
    activ = low(jax.nn.gelu(pre_act, approximate=True))
    return middle + low_back(project(activ, down_weight) + down_bias)

def reference(hidden_in, out_grad, segments, ln1_gain, ln1_bias, qkv_weight, q_bias, v_bias, output_projection_weight, out_bias, ln2_gain, ln2_bias, up_weight, up_bias, down_weight, down_bias):
    param_set = tuple((param_item.astype(jnp.float32) for param_item in (ln1_gain, ln1_bias, qkv_weight, q_bias, v_bias, output_projection_weight, out_bias, ln2_gain, ln2_bias, up_weight, up_bias, down_weight, down_bias)))

    def blocks(array):
        return array.astype(jnp.float32).transpose(1, 0, 2).reshape(NSEQ // SEQS, SEQS, LENGTH, D)
    seg_blocks = segments.T.reshape(NSEQ // SEQS, SEQS, LENGTH)

    def scan_step(totals, block):
        token_blk, cotangent, seg_ids = block
        result, pull = jax.vjp(lambda params_now, tokens_now: forward(params_now, tokens_now, seg_ids), param_set, token_blk)
        grads, token_grad = pull(cotangent)
        totals = jax.tree.map(lambda running, addend: running + addend, totals, grads)
        return (totals, (result.astype(jnp.bfloat16), token_grad))
    totals, (results, token_grads) = lax.scan(scan_step, jax.tree.map(jnp.zeros_like, param_set), (blocks(hidden_in), blocks(out_grad), seg_blocks))

    def unblock(array):
        return array.reshape(NSEQ, LENGTH, D).transpose(1, 0, 2)
    return (unblock(results), unblock(token_grads), totals[0], totals[1], totals[2], totals[3], totals[4], totals[5], totals[6], totals[7], totals[8], totals[9], totals[10], totals[11], totals[12])
```

```python
import functools

import jax
import jax.numpy as jnp
from jax import lax
from jax.experimental import pallas as pl
from jax.experimental.pallas import tpu as pltpu
from jax.sharding import PartitionSpec as P

HEADS = 25
HDIM = 64
OWN_HEADS = HEADS // 2 + 1
FIRST_HEAD = HEADS // 2
OWN = OWN_HEADS * HDIM
BLOCK = 256
AXES = ("shard", "replica")
BF16 = jnp.bfloat16
F32 = jnp.float32


def dot(left, right, left_dim, right_dim):
    return lax.dot_general(
        left, right, (((left_dim,), (right_dim,)), ((), ())), preferred_element_type=F32
    )


def norm_parts(rows):
    centre = rows - jnp.mean(rows, axis=-1, keepdims=True)
    scale = lax.rsqrt(jnp.mean(centre * centre, axis=-1, keepdims=True) + 1e-05)
    return centre * scale, scale


def norm_back(grad, unit, scale, gain):
    inner = grad * gain
    mean_inner = jnp.mean(inner, axis=-1, keepdims=True)
    mean_cross = jnp.mean(inner * unit, axis=-1, keepdims=True)
    return scale * (inner - mean_inner - unit * mean_cross)


def gelu_pair(value):
    root = 0.7978845608028654
    cube = 0.044715
    square = value * value
    tanh = jnp.tanh(root * value * (1.0 + cube * square))
    half = 0.5 * (1.0 + tanh)
    slope = half + 0.5 * value * (1.0 - tanh * tanh) * root * (1.0 + 3.0 * cube * square)
    return value * half, slope


def fill_mask(seg_row, seg_col, mask, blocks):
    for q_at in range(blocks):
        for k_at in range(q_at + 1):
            keys = seg_col[pl.ds(k_at * BLOCK, BLOCK), :]
            queries = seg_row[:, pl.ds(q_at * BLOCK, BLOCK)]
            seen = keys == queries
            if k_at == q_at:
                k_place = lax.broadcasted_iota(jnp.int32, (BLOCK, BLOCK), 0)
                q_place = lax.broadcasted_iota(jnp.int32, (BLOCK, BLOCK), 1)
                seen = seen & (k_place <= q_place)
            mask[pl.ds(k_at * BLOCK, BLOCK), pl.ds(q_at * BLOCK, BLOCK)] = jnp.where(
                seen, 0.0, -1e30
            )


def forward_kernel(seg_row, seg_col, q_ref, k_ref, v_ref, o_ref, lse_ref, mask):
    length = q_ref.shape[1]
    blocks = length // BLOCK

    @pl.when(pl.program_id(0) == 0)
    def _():
        fill_mask(seg_row, seg_col, mask, blocks)

    keys = k_ref[...].T
    for q_at in range(blocks):
        span = (q_at + 1) * BLOCK
        here = pl.ds(q_at * BLOCK, BLOCK)
        scores = dot(keys[:span], q_ref[:, here], 1, 0) + mask[:span, here]
        peak = jnp.max(scores, axis=0, keepdims=True)
        terms = jnp.exp(scores - peak)
        total = jnp.sum(terms, axis=0, keepdims=True)
        mixed = dot(v_ref[:, :span], terms.astype(BF16), 1, 0)
        o_ref[:, here] = (mixed / total).astype(BF16)
        lse_ref[0, :, here] = peak + jnp.log(total)


def backward_kernel(
    seg_row, seg_col, q_ref, k_ref, v_ref, o_ref, g_ref, lse_ref, dq_ref, dk_ref, dv_ref, mask, acc
):
    length = q_ref.shape[1]
    blocks = length // BLOCK

    @pl.when(pl.program_id(0) == 0)
    def _():
        fill_mask(seg_row, seg_col, mask, blocks)

    keys = k_ref[...].T
    values = v_ref[...].T
    delta = jnp.sum(g_ref[...].astype(F32) * o_ref[...].astype(F32), axis=0, keepdims=True)
    lse = lse_ref[0]
    for k_at in range(blocks):
        low = k_at * BLOCK
        here = pl.ds(low, BLOCK)
        rest = pl.ds(low, length - low)
        scores = dot(keys[low : low + BLOCK], q_ref[:, rest], 1, 0) + mask[here, rest]
        soft = jnp.exp(scores - lse[:, low:])
        soft_grad = dot(values[low : low + BLOCK], g_ref[:, rest], 1, 0)
        score_grad = (soft * (soft_grad - delta[:, low:])).astype(BF16)
        dv_ref[:, here] = dot(g_ref[:, rest], soft.astype(BF16), 1, 1).astype(BF16)
        dk_ref[:, here] = dot(q_ref[:, rest], score_grad, 1, 1).astype(BF16)
        grad_q = dot(k_ref[:, here], score_grad, 1, 0)
        if k_at == 0:
            acc[...] = grad_q
        else:
            acc[:, rest] += grad_q
    dq_ref[...] = (acc[...] * 0.125).astype(BF16)


def head_spec(first, length):
    return pl.BlockSpec((HDIM, length), lambda head: (first + head, 0))


def whole_spec(shape):
    return pl.BlockSpec(shape, lambda head: (0,) * len(shape))


def attention(seg, joined):
    length = seg.shape[0]
    lse_spec = pl.BlockSpec((1, 1, length), lambda head: (head, 0, 0))
    pairs = OWN_HEADS * length * length
    return pl.pallas_call(
        forward_kernel,
        grid=(OWN_HEADS,),
        in_specs=[whole_spec((1, length)), whole_spec((length, 1))]
        + [head_spec(part * OWN_HEADS, length) for part in range(3)],
        out_specs=[head_spec(0, length), lse_spec],
        out_shape=[
            jax.ShapeDtypeStruct((OWN, length), BF16),
            jax.ShapeDtypeStruct((OWN_HEADS, 1, length), F32),
        ],
        scratch_shapes=[pltpu.VMEM((length, length), F32)],
        compiler_params=pltpu.CompilerParams(vmem_limit_bytes=40 * 2**20),
        cost_estimate=pl.CostEstimate(
            flops=16 * pairs * HDIM, bytes_accessed=8 * OWN * length, transcendentals=pairs
        ),
        name="attention_forward",
    )(seg.reshape(1, length), seg.reshape(length, 1), joined, joined, joined)


def attention_back(seg, joined, mixed, grad, lse):
    length = seg.shape[0]
    lse_spec = pl.BlockSpec((1, 1, length), lambda head: (head, 0, 0))
    pairs = OWN_HEADS * length * length
    return pl.pallas_call(
        backward_kernel,
        grid=(OWN_HEADS,),
        in_specs=[whole_spec((1, length)), whole_spec((length, 1))]
        + [head_spec(part * OWN_HEADS, length) for part in range(3)]
        + [head_spec(0, length), head_spec(0, length), lse_spec],
        out_specs=[head_spec(0, length)] * 3,
        out_shape=[jax.ShapeDtypeStruct((OWN, length), BF16)] * 3,
        scratch_shapes=[pltpu.VMEM((length, length), F32), pltpu.VMEM((HDIM, length), F32)],
        compiler_params=pltpu.CompilerParams(vmem_limit_bytes=48 * 2**20),
        cost_estimate=pl.CostEstimate(
            flops=40 * pairs * HDIM, bytes_accessed=16 * OWN * length, transcendentals=pairs
        ),
        name="attention_backward",
    )(seg.reshape(1, length), seg.reshape(length, 1), joined, joined, joined, mixed, grad, lse)


class Moves:
    def __init__(self, shard_count, replica_count):
        self.shard_count = shard_count
        self.replica_count = replica_count
        self.shard = lax.axis_index("shard")
        replica = lax.axis_index("replica")
        self.core = replica % 2
        self.column = replica // 2
        self.square = shard_count == 4 and replica_count == 8

    def move(self, array, route):
        pairs = []
        for shard in range(self.shard_count):
            for column in range(self.replica_count // 2):
                for core in range(2):
                    target = route(shard, column, core)
                    if target is not None:
                        to_shard, to_column, to_core = target
                        pairs.append(
                            (
                                shard * self.replica_count + 2 * column + core,
                                to_shard * self.replica_count + 2 * to_column + to_core,
                            )
                        )
        return lax.ppermute(array, AXES, pairs)

    def over_x(self, array):
        return self.move(array, lambda s, z, c: (s ^ 1, z, c))

    def over_y(self, array):
        return self.move(array, lambda s, z, c: (s ^ 2, z, c))

    def over_core(self, array):
        return self.move(array, lambda s, z, c: (s, z, 1 - c))

    def gather(self, piece):
        if not self.square:
            return lax.all_gather(piece, "shard", axis=0, tiled=False)
        rows = piece.shape[0] // 2
        from_x = self.over_x(piece)
        from_y = self.over_y(piece)
        far_low = self.over_x(from_y[:rows])
        far_high = self.over_y(from_x[rows:])
        out = jnp.zeros((4,) + piece.shape, piece.dtype)
        zero = (0,) * (piece.ndim - 1)
        out = lax.dynamic_update_slice(out, piece[None], (self.shard, 0) + zero)
        out = lax.dynamic_update_slice(out, from_x[None], (self.shard ^ 1, 0) + zero)
        out = lax.dynamic_update_slice(out, from_y[None], (self.shard ^ 2, 0) + zero)
        out = lax.dynamic_update_slice(out, far_low[None], (self.shard ^ 3, 0) + zero)
        out = lax.dynamic_update_slice(out, far_high[None], (self.shard ^ 3, rows) + zero)
        return out

    def pick(self, parts, index):
        return lax.dynamic_index_in_dim(parts, index, 0, keepdims=False)

    def scatter(self, parts):
        if not self.square:
            return lax.psum_scatter(parts, "shard", scatter_dimension=0, tiled=False)
        rows = parts.shape[1] // 2
        me = self.shard

        def part(index, high):
            begin = (index, rows if high else 0) + (0,) * (parts.ndim - 2)
            size = (1, parts.shape[1] - rows if high else rows) + parts.shape[2:]
            return lax.dynamic_slice(parts, begin, size)[0]

        low_far, low_y = self.over_x(part(me ^ 3, False)), self.over_x(part(me ^ 1, False))
        high_far, high_x = self.over_y(part(me ^ 3, True)), self.over_y(part(me ^ 2, True))
        low = self.over_y(part(me ^ 2, False) + low_far)
        high = self.over_x(part(me ^ 1, True) + high_far)
        return jnp.concatenate(
            [(part(me, False) + low_y) + low, (part(me, True) + high_x) + high], axis=0
        )

    def total(self, array):
        if not self.square:
            groups = [
                [2 * column + core for column in range(self.replica_count // 2)]
                for core in range(2)
            ]
            return lax.psum(array, "replica", axis_index_groups=groups)
        inward = {0: 1, 3: 2}
        across = {1: 2, 2: 1}
        outward = {1: 0, 2: 3}

        def hop(array, table):
            return self.move(array, lambda s, z, c: (s, table[z], c) if z in table else None)

        pair = array + hop(array, inward)
        full = pair + hop(pair, across)
        middle = (self.column == 1) | (self.column == 2)
        return jnp.where(middle, full, hop(full, outward))

    def owners(self, step, seqs):
        return lambda s, z, c: (seqs * c + (s + step) % seqs, z, s // seqs)

    def to_chips(self, local):
        seqs = local.shape[1]
        came = []
        for step in range(seqs):
            sent = lax.dynamic_index_in_dim(local, (self.shard + step) % seqs, 1, keepdims=False)
            came.append(self.move(sent, self.owners(step, seqs)))
        at = self.shard % seqs
        ring = came[::-1] * 2
        ring = jnp.concatenate(ring[: 2 * seqs - 1], axis=0)
        rows = local.shape[0]
        return lax.dynamic_slice_in_dim(ring, (seqs - 1 - at) * rows, seqs * rows, 0)

    def from_chips(self, half, seqs):
        rows = half.shape[0] // seqs
        at = self.shard % seqs
        outs = []
        for step in range(seqs):
            route = self.owners(step, seqs)
            back = {}
            for s in range(self.shard_count):
                for z in range(self.replica_count // 2):
                    for c in range(2):
                        back[route(s, z, c)] = (s, z, c)
            sent = lax.dynamic_slice_in_dim(half, ((at - step) % seqs) * rows, rows, 0)
            outs.append(self.move(sent, lambda s, z, c: back[(s, z, c)]))
        stacked = jnp.stack(outs, axis=1)
        doubled = jnp.concatenate([stacked, stacked[:, : seqs - 1]], axis=1)
        return lax.dynamic_slice_in_dim(doubled, (seqs - at) % seqs, seqs, 1)

    def both(self, half):
        other = self.over_core(half)
        first = self.core == 0
        return jnp.concatenate(
            [jnp.where(first, half, other), jnp.where(first, other, half)], axis=0
        )


def shards(
    shard_count,
    replica_count,
    hidden_in,
    out_grad,
    segments,
    ln1_gain,
    ln1_bias,
    qkv_weight,
    q_bias,
    v_bias,
    output_projection_weight,
    out_bias,
    ln2_gain,
    ln2_bias,
    up_weight,
    up_bias,
    down_weight,
    down_bias,
):
    moves = Moves(shard_count, replica_count)
    core = moves.core
    seqs = hidden_in.shape[1]
    width = hidden_in.shape[2]
    length = segments.shape[0]
    half_rows = length // 2
    ff = up_bias.shape[0]
    ff_part = ff // shard_count
    ff_half = ff_part // 2
    first_row = core * FIRST_HEAD * HDIM
    own_cols = functools.partial(lax.dynamic_slice_in_dim, slice_size=OWN)

    tokens_half = moves.to_chips(hidden_in)
    qkv_rows = qkv_weight.shape[0] // 2
    qkv_half = moves.gather(lax.dynamic_slice_in_dim(qkv_weight, core * qkv_rows, qkv_rows, 0))
    qkv_other = moves.over_core(qkv_half)
    qkv_full = jnp.where(
        core == 0,
        jnp.concatenate([qkv_half, qkv_other], axis=1),
        jnp.concatenate([qkv_other, qkv_half], axis=1),
    ).reshape(3 * width, width)
    w_out = moves.gather(own_cols(output_projection_weight, first_row, axis=1))
    w_up = moves.gather(lax.dynamic_slice_in_dim(up_weight, core * ff_half, ff_half, 0))
    down_cols = lax.dynamic_index_in_dim(
        down_weight.reshape(-1, shard_count, 2, ff_half), core, 2, keepdims=False
    ).reshape(-1, ff // 2)
    w_down = moves.gather(down_cols)
    w_up = w_up.reshape(ff // 2, width)
    w_down = w_down.reshape(width, ff // 2)
    twice = (core == 1) & (jnp.arange(OWN) < HDIM)
    w_out = jnp.where(twice[None, :], 0, w_out.reshape(width, OWN)).astype(BF16)
    up_bias_own = lax.dynamic_index_in_dim(
        up_bias.reshape(shard_count, 2, ff_half), core, 1, keepdims=False
    ).reshape(-1)
    w_qkv = jnp.concatenate(
        [own_cols(qkv_full, part * width + first_row, axis=0) for part in range(3)], axis=0
    )
    seg_pair = jnp.stack([segments, moves.over_core(segments)])
    home = moves.shard // seqs
    seg = lax.dynamic_index_in_dim(
        lax.dynamic_index_in_dim(seg_pair, (home != core).astype(jnp.int32), 0, keepdims=False),
        moves.shard % seqs,
        1,
        keepdims=False,
    )
    grad_out = moves.both(moves.to_chips(out_grad))

    tokens = moves.both(tokens_half).astype(F32)
    unit_one, scale_one = norm_parts(tokens)
    normed = (unit_one * ln1_gain + ln1_bias).astype(BF16)
    zeros = jnp.zeros((OWN,), F32)
    joined_bias = jnp.concatenate(
        [own_cols(q_bias, first_row, axis=0), zeros, own_cols(v_bias, first_row, axis=0)]
    )
    joined = (dot(w_qkv, normed, 1, 1) + joined_bias[:, None]).astype(BF16)
    row_scale = jnp.where(jnp.arange(3 * OWN) < OWN, 0.125, 1.0).astype(BF16)
    joined = joined * row_scale[:, None]
    mixed, lse = attention(seg, joined)
    branch = dot(mixed, w_out, 0, 1)
    middle = tokens + (branch + moves.over_core(branch.astype(BF16)).astype(F32)) + out_bias
    unit_two, scale_two = norm_parts(middle)
    normed_two = (unit_two * ln2_gain + ln2_bias).astype(BF16)
    activ, slope = gelu_pair(dot(normed_two, w_up, 1, 1) + up_bias_own)
    activ = activ.astype(BF16)
    slope = slope.astype(BF16)
    down = dot(activ, w_down, 1, 1)
    half_of = functools.partial(lax.dynamic_slice_in_dim, slice_size=half_rows, axis=0)
    mine, theirs = core * half_rows, (1 - core) * half_rows
    down_other = moves.over_core(half_of(down.astype(BF16), theirs)).astype(F32)
    result_half = half_of(middle, mine) + (half_of(down, mine) + down_other) + down_bias
    result = moves.from_chips(result_half.astype(BF16), seqs)

    down_grad = dot(grad_out, activ, 0, 0).astype(BF16)
    grad_act = dot(grad_out, w_down, 1, 0)
    grad_pre = (grad_act * slope.astype(F32)).astype(BF16)
    up_grad = dot(grad_pre, normed_two, 0, 0).astype(BF16)
    grad_norm_two = dot(grad_pre, w_up, 1, 0)
    grad_norm_two = grad_norm_two + moves.over_core(grad_norm_two.astype(BF16)).astype(F32)
    grad_out_f = grad_out.astype(F32)
    grad_middle = grad_out_f + norm_back(grad_norm_two, unit_two, scale_two, ln2_gain)
    grad_branch = grad_middle.astype(BF16)
    out_grad_own = dot(grad_branch, mixed, 0, 1).astype(BF16)
    grad_mixed = dot(w_out, grad_branch, 0, 1).astype(BF16)

    down_sum = moves.total(moves.scatter(down_grad.reshape(shard_count, -1, ff // 2)))
    up_sum = moves.total(moves.scatter(up_grad.reshape(shard_count, ff_half, width)))
    out_sum = moves.total(moves.scatter(out_grad_own.reshape(shard_count, -1, OWN)))

    grad_q, grad_k, grad_v = attention_back(seg, joined, mixed, grad_mixed, lse)
    grad_own = jnp.stack([grad_q, grad_k, grad_v])
    grad_other = moves.over_core(grad_own)
    low = jnp.where(core == 0, grad_own, grad_other)
    high = jnp.where(core == 0, grad_other, grad_own)
    grad_joined = jnp.concatenate([low, high[:, HDIM:]], axis=1).reshape(3 * width, length)
    half_width = width // 2
    qkv_grad = dot(
        grad_joined, lax.dynamic_slice_in_dim(normed, core * half_width, half_width, 1), 1, 0
    ).astype(BF16)
    qkv_sum = moves.total(moves.scatter(qkv_grad.reshape(shard_count, -1, half_width)))
    grad_norm_one = dot(
        lax.dynamic_slice_in_dim(grad_joined, mine, half_rows, 1), qkv_full, 0, 0
    )
    unit_half = half_of(unit_one, mine)
    input_half = half_of(grad_middle, mine) + norm_back(
        grad_norm_one, unit_half, half_of(scale_one, mine), ln1_gain
    )
    input_grad = moves.from_chips(input_half.astype(BF16), seqs).astype(F32)

    once = (core == 0).astype(F32)
    up_bias_grad = jnp.sum(grad_pre.astype(F32), axis=0).reshape(shard_count, 1, ff_half)
    up_bias_grad = up_bias_grad * (jnp.arange(2)[None, :, None] == core).astype(F32)
    early = lax.psum(
        jnp.concatenate(
            [
                up_bias_grad.reshape(-1),
                once * jnp.sum(grad_norm_two * unit_two, axis=0),
                once * jnp.sum(grad_norm_two, axis=0),
                once * jnp.sum(grad_out_f, axis=0),
                once * jnp.sum(grad_branch.astype(F32), axis=0),
            ]
        ),
        AXES,
    )
    up_bias_grad, rest = early[:ff], early[ff:]
    ln2_gain_grad, ln2_bias_grad, down_bias_grad, out_bias_grad = rest.reshape(4, width)
    bias_sums = jnp.sum(grad_joined.astype(F32), axis=1).reshape(3, width)
    late = lax.psum(
        jnp.concatenate(
            [
                jnp.sum(grad_norm_one * unit_half, axis=0),
                jnp.sum(grad_norm_one, axis=0),
                once * bias_sums[0],
                once * bias_sums[2],
            ]
        ),
        AXES,
    )
    ln1_gain_grad, ln1_bias_grad, q_bias_grad, v_bias_grad = late.reshape(4, width)

    first = core == 0

    def join(own, axis):
        other = moves.over_core(own)
        low, high = jnp.where(first, own, other), jnp.where(first, other, own)
        return low.astype(F32), high.astype(F32), axis

    def laid(own, axis):
        low, high, axis = join(own, axis)
        return jnp.concatenate([low, high], axis=axis)

    down_low, down_high, _ = join(down_sum.reshape(-1, shard_count, ff_half), 2)
    down_total = jnp.stack([down_low, down_high], axis=2).reshape(-1, ff)
    up_total = laid(up_sum, 0)
    qkv_total = laid(qkv_sum, 1)
    out_low, out_high, _ = join(out_sum, 1)
    out_total = jnp.concatenate([out_low, out_high[:, HDIM:]], axis=1)
    return (
        result,
        input_grad,
        ln1_gain_grad,
        ln1_bias_grad,
        qkv_total,
        q_bias_grad,
        v_bias_grad,
        out_total,
        out_bias_grad,
        ln2_gain_grad,
        ln2_bias_grad,
        up_total,
        up_bias_grad,
        down_total,
        down_bias_grad,
    )


def solution(mesh):
    rows = P("shard", None)
    tokens = P("shard", "replica", None)
    in_specs = (
        tokens,
        tokens,
        P(None, "replica"),
        P(),
        P(),
        rows,
        P(),
        P(),
        rows,
        P(),
        P(),
        P(),
        rows,
        P(),
        rows,
        P(),
    )
    out_specs = (
        tokens,
        tokens,
        P(),
        P(),
        rows,
        P(),
        P(),
        rows,
        P(),
        P(),
        P(),
        rows,
        P(),
        rows,
        P(),
    )
    body = functools.partial(shards, mesh.shape["shard"], mesh.shape["replica"])
    return jax.shard_map(body, mesh=mesh, in_specs=in_specs, out_specs=out_specs, check_vma=False)
```

```python
import functools

import jax
import jax.numpy as jnp
from jax import lax
from jax.experimental import pallas as pl
from jax.experimental.pallas import tpu as pltpu
from jax.sharding import PartitionSpec as P

HEADS = 25
HDIM = 64
OWN_HEADS = HEADS // 2 + 1
FIRST_HEAD = HEADS // 2
OWN = OWN_HEADS * HDIM
BLOCK = 256
AXES = ("shard", "replica")
BF16 = jnp.bfloat16
F32 = jnp.float32


def dot(left, right, left_dim, right_dim):
    return lax.dot_general(
        left, right, (((left_dim,), (right_dim,)), ((), ())), preferred_element_type=F32
    )


COST_SCALE = 8


def cost(flops, bytes_accessed):
    return pl.CostEstimate(
        flops=int(flops * COST_SCALE),
        bytes_accessed=int(bytes_accessed * COST_SCALE),
        transcendentals=0,
    )


def norm_parts(rows):
    centre = rows - jnp.mean(rows, axis=0, keepdims=True)
    scale = lax.rsqrt(jnp.mean(centre * centre, axis=0, keepdims=True) + 1e-05)
    return centre * scale, scale


def norm_back(grad, unit, scale, gain):
    inner = grad * gain
    mean_inner = jnp.mean(inner, axis=0, keepdims=True)
    mean_cross = jnp.mean(inner * unit, axis=0, keepdims=True)
    return scale * (inner - mean_inner - unit * mean_cross)


def gelu_pair(value):
    root = 0.7978845608028654
    cube = 0.044715
    square = value * value
    tanh = jnp.tanh(root * value * (1.0 + cube * square))
    half = 0.5 * (1.0 + tanh)
    slope = half + 0.5 * value * (1.0 - tanh * tanh) * root * (1.0 + 3.0 * cube * square)
    return value * half, slope


def fill_mask(seg_row, seg_col, mask, blocks):
    for q_at in range(blocks):
        for k_at in range(q_at + 1):
            keys = seg_col[pl.ds(k_at * BLOCK, BLOCK), :]
            queries = seg_row[:, pl.ds(q_at * BLOCK, BLOCK)]
            seen = keys == queries
            if k_at == q_at:
                k_place = lax.broadcasted_iota(jnp.int32, (BLOCK, BLOCK), 0)
                q_place = lax.broadcasted_iota(jnp.int32, (BLOCK, BLOCK), 1)
                seen = seen & (k_place <= q_place)
            mask[pl.ds(k_at * BLOCK, BLOCK), pl.ds(q_at * BLOCK, BLOCK)] = jnp.where(
                seen, 0.0, -1e30
            )


def forward_kernel(seg_row, seg_col, q_ref, k_ref, v_ref, *refs):
    o_ref, lse_ref, mask = refs[-3:]
    length = q_ref.shape[1]
    blocks = length // BLOCK

    @pl.when(pl.program_id(0) == 0)
    def _():
        fill_mask(seg_row, seg_col, mask, blocks)

    keys = k_ref[...].T
    for q_at in range(blocks):
        span = (q_at + 1) * BLOCK
        here = pl.ds(q_at * BLOCK, BLOCK)
        scores = dot(keys[:span], q_ref[:, here], 1, 0) + mask[:span, here]
        peak = jnp.max(scores, axis=0, keepdims=True)
        terms = jnp.exp(scores - peak)
        total = jnp.sum(terms, axis=0, keepdims=True)
        mixed = dot(v_ref[:, :span], terms.astype(BF16), 1, 0)
        o_ref[:, here] = (mixed / total).astype(BF16)
        lse_ref[0, :, here] = peak + jnp.log(total)


def backward_kernel(seg_row, seg_col, q_ref, k_ref, v_ref, o_ref, g_ref, lse_ref, *refs):
    grads, mask, acc = refs[-3:]
    length = q_ref.shape[1]
    blocks = length // BLOCK

    @pl.when(pl.program_id(0) == 0)
    def _():
        fill_mask(seg_row, seg_col, mask, blocks)

    keys = k_ref[...].T
    values = v_ref[...].T
    delta = jnp.sum(g_ref[...].astype(F32) * o_ref[...].astype(F32), axis=0, keepdims=True)
    lse = lse_ref[0]
    for k_at in range(blocks):
        low = k_at * BLOCK
        here = pl.ds(low, BLOCK)
        rest = pl.ds(low, length - low)
        scores = dot(keys[low : low + BLOCK], q_ref[:, rest], 1, 0) + mask[here, rest]
        soft = jnp.exp(scores - lse[:, low:])
        soft_grad = dot(values[low : low + BLOCK], g_ref[:, rest], 1, 0)
        score_grad = (soft * (soft_grad - delta[:, low:])).astype(BF16)
        grads[2, :, here] = dot(g_ref[:, rest], soft.astype(BF16), 1, 1).astype(BF16)
        grads[1, :, here] = dot(q_ref[:, rest], score_grad, 1, 1).astype(BF16)
        grad_q = dot(k_ref[:, here], score_grad, 1, 0)
        if k_at == 0:
            acc[...] = grad_q
        else:
            acc[:, rest] += grad_q
    grads[0] = (acc[...] * 0.125).astype(BF16)


def head_spec(first, length):
    return pl.BlockSpec((HDIM, length), lambda head: (first + head, 0))


def whole_spec(shape):
    return pl.BlockSpec(shape, lambda head: (0,) * len(shape))


def attention(seg, joined, wait):
    length = seg.shape[0]
    lse_spec = pl.BlockSpec((1, 1, length), lambda head: (head, 0, 0))
    pairs = OWN_HEADS * length * length
    return pl.pallas_call(
        forward_kernel,
        grid=(OWN_HEADS,),
        in_specs=[whole_spec((1, length)), whole_spec((length, 1))]
        + [head_spec(part * OWN_HEADS, length) for part in range(3)]
        + [pl.BlockSpec(memory_space=pl.ANY)] * len(wait),
        out_specs=[head_spec(0, length), lse_spec],
        out_shape=[
            jax.ShapeDtypeStruct((OWN, length), BF16),
            jax.ShapeDtypeStruct((OWN_HEADS, 1, length), F32),
        ],
        scratch_shapes=[pltpu.VMEM((length, length), F32)],
        compiler_params=pltpu.CompilerParams(vmem_limit_bytes=40 * 2**20),
        cost_estimate=cost(16 * pairs * HDIM, 8 * OWN * length),
        name="attention_forward",
    )(seg.reshape(1, length), seg.reshape(length, 1), joined, joined, joined, *wait)


def attention_back(seg, joined, mixed, grad, lse, wait):
    length = seg.shape[0]
    lse_spec = pl.BlockSpec((1, 1, length), lambda head: (head, 0, 0))
    pairs = OWN_HEADS * length * length
    return pl.pallas_call(
        backward_kernel,
        grid=(OWN_HEADS,),
        in_specs=[whole_spec((1, length)), whole_spec((length, 1))]
        + [head_spec(part * OWN_HEADS, length) for part in range(3)]
        + [head_spec(0, length), head_spec(0, length), lse_spec]
        + [pl.BlockSpec(memory_space=pl.ANY)] * len(wait),
        out_specs=pl.BlockSpec((3, HDIM, length), lambda head: (0, head, 0)),
        out_shape=jax.ShapeDtypeStruct((3, OWN, length), BF16),
        scratch_shapes=[pltpu.VMEM((length, length), F32), pltpu.VMEM((HDIM, length), F32)],
        compiler_params=pltpu.CompilerParams(vmem_limit_bytes=48 * 2**20),
        cost_estimate=cost(40 * pairs * HDIM, 16 * OWN * length),
        name="attention_backward",
    )(
        seg.reshape(1, length),
        seg.reshape(length, 1),
        joined,
        joined,
        joined,
        mixed,
        grad,
        lse,
        *wait,
    )


def product(left, rights, form, block, finish=None, extras=(), outs=((None, BF16),), name="product",
            wait=()):
    rights = rights if isinstance(rights, (list, tuple)) else [rights]
    many = len(rights)
    left_dim, right_dim = (0 if form == "tn" else 1), (1 if form == "nt" else 0)
    m, k = left.shape[1 - left_dim], left.shape[left_dim]
    size = rights[0].shape[1 - right_dim]
    n = size * many
    block = min(block, m)

    def body(left_ref, *refs):
        extra_refs = refs[many : many + len(extras)]
        out_refs = refs[many + len(extras) + len(wait) :]
        for at in range(many):
            value = dot(left_ref[...], refs[at][...], left_dim, right_dim)
            values = (value,)
            if finish is not None:
                values = finish(value, at, *extra_refs)
            for ref, part in zip(out_refs, values):
                if part is not None:
                    width = part.shape[1]
                    begin = at * width % ref.shape[1]
                    ref[:, begin : begin + width] = part.astype(ref.dtype)

    if form == "tn":
        left_spec = pl.BlockSpec((k, block), lambda i: (0, i))
    else:
        left_spec = pl.BlockSpec((block, k), lambda i: (i, 0))
    sizes = [(columns or n, kind) for columns, kind in outs]
    results = pl.pallas_call(
        body,
        grid=(pl.cdiv(m, block),),
        in_specs=[left_spec]
        + [
            pl.BlockSpec(right.shape, lambda i: (0, 0), pipeline_mode=pl.Buffered(1))
            for right in rights
        ]
        + [pl.BlockSpec((block, extra.shape[1]), lambda i: (i, 0)) for extra in extras]
        + [pl.BlockSpec(memory_space=pl.ANY)] * len(wait),
        out_specs=[pl.BlockSpec((block, columns), lambda i: (i, 0)) for columns, _ in sizes],
        out_shape=[jax.ShapeDtypeStruct((m, columns), kind) for columns, kind in sizes],
        compiler_params=pltpu.CompilerParams(vmem_limit_bytes=56 * 2**20),
        cost_estimate=cost(2 * m * n * k, 2 * (m * k + n * k + m * n)),
        name=name,
    )(left, *rights, *extras, *wait)
    return results if len(outs) > 1 else results[0]


def lane_sums(value):
    return sum(value[:, at : at + 128] for at in range(0, value.shape[1], 128))


def lay(places, near, far, parts):
    count, columns = near[0].shape
    size = count // parts
    kind = near[0].dtype

    def body(places_ref, *refs):
        step = pl.program_id(0)
        outs = refs[5:]
        for at in range(3):

            @pl.when(step == at)
            def _(at=at):
                for index, out in enumerate(outs):
                    out[...] = refs[at][index * size : (index + 1) * size]

        @pl.when(step == 3)
        def _():
            start = 0
            for ref in refs[3:5]:
                rows = ref.shape[0]
                for index, out in enumerate(outs):
                    low, high = max(start, index * size), min(start + rows, (index + 1) * size)
                    if low < high:
                        out[low - index * size : high - index * size] = ref[
                            low - start : high - start
                        ]
                start += rows

    pieces = list(near) + list(far)
    return pl.pallas_call(
        body,
        grid_spec=pltpu.PrefetchScalarGridSpec(
            num_scalar_prefetch=1,
            grid=(4,),
            in_specs=[
                pl.BlockSpec(piece.shape, lambda i, p: (0, 0), pipeline_mode=pl.Buffered(1))
                for piece in pieces
            ],
            out_specs=[pl.BlockSpec((size, columns), lambda i, p: (p[i], 0))] * parts,
        ),
        out_shape=[jax.ShapeDtypeStruct((4 * size, columns), kind)] * parts,
        compiler_params=pltpu.CompilerParams(vmem_limit_bytes=56 * 2**20),
        cost_estimate=cost(0, 16 * count * columns),
        name="lay",
    )(places, *pieces)


def lay_heads(core, places, mine, others, count):
    rows, width = mine[0].shape
    over = 2 * rows - count

    def body(core_ref, places_ref, *refs):
        heads_ref, block = refs[10:]
        step = pl.program_id(0)

        def halves(refs, begin, size, at, skip):
            if at < 3:
                block[begin : begin + size - skip] = refs[at][skip:]
            else:
                cut = refs[3].shape[0]
                block[begin : begin + cut - skip] = refs[3][skip:]
                block[begin + cut - skip : begin + size - skip] = refs[4][...]

        for which in range(2):

            @pl.when(core_ref[0] == which)
            def _(which=which):
                low, high = (refs[:5], refs[5:10]) if which == 0 else (refs[5:10], refs[:5])
                for at in range(4):

                    @pl.when(step == at)
                    def _(at=at):
                        halves(low, 0, rows, at, 0)
                        halves(high, rows, rows, at, over)

                for shard in range(4):

                    @pl.when(places_ref[step] == shard)
                    def _(shard=shard):
                        for part in range(3):
                            begin = part * width + which * FIRST_HEAD * HDIM
                            first = max(begin, shard * count)
                            last = min(begin + OWN, (shard + 1) * count)
                            if first < last:
                                heads_ref[
                                    part * OWN + first - begin : part * OWN + last - begin
                                ] = block[first - shard * count : last - shard * count]

    pieces = list(mine) + list(others)
    return pl.pallas_call(
        body,
        grid_spec=pltpu.PrefetchScalarGridSpec(
            num_scalar_prefetch=2,
            grid=(4,),
            in_specs=[
                pl.BlockSpec(piece.shape, lambda i, c, p: (0, 0), pipeline_mode=pl.Buffered(1))
                for piece in pieces
            ],
            out_specs=pl.BlockSpec(
                (3 * OWN, width), lambda i, c, p: (0, 0), pipeline_mode=pl.Buffered(1)
            ),
            scratch_shapes=[pltpu.VMEM((count, width), BF16)],
        ),
        out_shape=jax.ShapeDtypeStruct((3 * OWN, width), BF16),
        compiler_params=pltpu.CompilerParams(vmem_limit_bytes=56 * 2**20),
        cost_estimate=cost(0, 16 * count * width),
        name="lay_heads",
    )(core, places, *pieces)


def join_heads(core, own, other):
    length = own.shape[1]
    rows = 2 * OWN - HDIM

    def body(core_ref, own_ref, other_ref, out):
        for which in range(2):

            @pl.when(core_ref[0] == which)
            def _(which=which):
                low, high = (own_ref, other_ref) if which == 0 else (other_ref, own_ref)
                out[:OWN] = low[...]
                out[OWN:] = high[HDIM:]

    block = pl.BlockSpec((OWN, length), lambda i, c: (i, 0))
    return pl.pallas_call(
        body,
        grid_spec=pltpu.PrefetchScalarGridSpec(
            num_scalar_prefetch=1,
            grid=(3,),
            in_specs=[block, block],
            out_specs=pl.BlockSpec((rows, length), lambda i, c: (i, 0)),
        ),
        out_shape=jax.ShapeDtypeStruct((3 * rows, length), BF16),
        compiler_params=pltpu.CompilerParams(vmem_limit_bytes=56 * 2**20),
        cost_estimate=cost(0, 12 * rows * length),
        name="join_heads",
    )(core, own, other)


def product_parts(order, pairs, cut, wait):
    many = len(pairs)
    lefts = [side_of(left) for left, _ in pairs]
    rights = [side_of(right) for _, right in pairs]
    count = lefts[0][0].shape[0] // 4
    depth = sum(piece.shape[1] for piece in lefts[0])
    columns = rights[0][0].shape[0]
    rest = columns - cut
    filled = to_tiles(rest)
    starts = [0]
    for sides in lefts + rights:
        starts.append(starts[-1] + len(sides))

    def body(order_ref, *refs):
        send_x, send_y, keep_x, keep_y = refs[starts[-1] + len(wait) :]
        step = pl.program_id(0)
        targets = ((send_x, send_y), (send_x, keep_y), (keep_x, send_y), (keep_x, keep_y))
        for pair in range(many):

            @pl.when(step // 4 == pair)
            def _(pair=pair):
                left = refs[starts[pair] : starts[pair + 1]]
                right = refs[starts[many + pair] : starts[many + pair + 1]]
                value = side_product(left, right).astype(BF16)
                for at, (along_x, along_y) in enumerate(targets):

                    @pl.when(step % 4 == at)
                    def _(along_x=along_x, along_y=along_y):
                        along_x[...] = value[:, :cut]
                        along_y[:, :rest] = value[:, cut:]
                        if filled > rest:
                            along_y[:, rest:] = jnp.zeros((count, filled - rest), BF16)

    def left_spec(pair, piece):
        return pl.BlockSpec(
            (count, piece.shape[1]), lambda i, o: (o[jnp.clip(i - 4 * pair, 0, 3)], 0)
        )

    def out_spec(size, second):
        return pl.BlockSpec(
            (count, size), lambda i, o: (jnp.where(i % 4 >= second, many, 0) + i // 4, 0)
        )

    return pl.pallas_call(
        body,
        grid_spec=pltpu.PrefetchScalarGridSpec(
            num_scalar_prefetch=1,
            grid=(4 * many,),
            in_specs=[left_spec(pair, piece) for pair in range(many) for piece in lefts[pair]]
            + [
                pl.BlockSpec(piece.shape, lambda i, o: (0, 0), pipeline_mode=pl.Buffered(1))
                for right in rights
                for piece in right
            ]
            + [pl.BlockSpec(memory_space=pl.ANY)] * len(wait),
            out_specs=[
                out_spec(cut, 1),
                out_spec(filled, 2),
                out_spec(cut, 3),
                out_spec(filled, 3),
            ],
        ),
        out_shape=[
            jax.ShapeDtypeStruct((2 * many * count, size), BF16)
            for size in (cut, filled, cut, filled)
        ],
        compiler_params=pltpu.CompilerParams(vmem_limit_bytes=56 * 2**20),
        cost_estimate=cost(8 * many * count * depth * columns, 8 * many * count * (depth + columns)),
        name="product_parts",
    )(order, *[piece for sides in lefts + rights for piece in sides], *wait)


def side_of(side):
    return list(side) if isinstance(side, (list, tuple)) else [side]


def side_product(left, right):
    if len(left) == len(right) == 1:
        return dot(left[0][...], right[0][...], 1, 1)
    total = None
    size = left[0].shape[1] if len(left) > 1 else right[0].shape[1]
    for at in range(max(len(left), len(right))):
        here = slice(at * size, (at + 1) * size)
        one = left[at][...] if len(left) > 1 else left[0][:, here]
        two = right[at][...] if len(right) > 1 else right[0][:, here]
        value = dot(one, two, 1, 1)
        total = value if total is None else total + value
    return total


def to_tiles(count):
    return -(-count // 128) * 128


def fold(keep_x, came_x, last_x, keep_y, came_y, last_y, columns):
    rows, cut = last_x.shape
    filled = last_y.shape[1]
    rest = columns - cut
    block = 400
    steps = rows // block

    def body(*refs):
        out = refs[6]
        for first, begin, size in ((0, 0, cut), (3, cut, rest)):
            value = refs[first][:, :size].astype(F32) + refs[first + 1][:, :size].astype(F32)
            value = value + refs[first + 2][:, :size].astype(F32)
            out[:, begin : begin + size] = value.astype(BF16)

    def specs(size):
        second = pl.BlockSpec((block, size), lambda i: (steps + i, 0))
        return [second, second, pl.BlockSpec((block, size), lambda i: (i, 0))]

    return pl.pallas_call(
        body,
        grid=(steps,),
        in_specs=specs(cut) + specs(filled),
        out_specs=pl.BlockSpec((block, columns), lambda i: (i, 0)),
        out_shape=jax.ShapeDtypeStruct((rows, columns), BF16),
        compiler_params=pltpu.CompilerParams(vmem_limit_bytes=56 * 2**20),
        cost_estimate=cost(0, 8 * rows * columns),
        name="fold",
    )(keep_x, came_x, last_x, keep_y, came_y, last_y)


def finish_up(quarter, parts):
    rows, width = parts[0].shape

    def body(quarter_ref, *refs):
        for at in range(4):

            @pl.when(pl.program_id(0) == at)
            def _(at=at):
                refs[4][...] = refs[at][...].astype(F32)

    return pl.pallas_call(
        body,
        grid_spec=pltpu.PrefetchScalarGridSpec(
            num_scalar_prefetch=1,
            grid=(4,),
            in_specs=[
                pl.BlockSpec((rows, width), lambda i, q: (0, 0), pipeline_mode=pl.Buffered(1))
            ]
            * 4,
            out_specs=pl.BlockSpec((rows, width), lambda i, q: (q[0] ^ i, 0)),
        ),
        out_shape=jax.ShapeDtypeStruct((4 * rows, width), F32),
        compiler_params=pltpu.CompilerParams(vmem_limit_bytes=56 * 2**20),
        cost_estimate=cost(0, 24 * rows * width),
        name="finish_up",
    )(quarter, *parts)


def finish_down(quarter, parts, shard_count):
    rows, width = parts[0].shape
    strip = width // shard_count
    block = 80 if rows % 80 == 0 else 40
    steps = rows // block

    def body(quarter_ref, *refs):
        for which in range(4):

            @pl.when(quarter_ref[0] == which)
            def _(which=which):
                for shard in range(shard_count):
                    for at in range(4):
                        begin = (4 * shard + at) * strip
                        refs[4][:, begin : begin + strip] = refs[which ^ at][
                            :, shard * strip : (shard + 1) * strip
                        ].astype(F32)

    return pl.pallas_call(
        body,
        grid_spec=pltpu.PrefetchScalarGridSpec(
            num_scalar_prefetch=1,
            grid=(steps,),
            in_specs=[pl.BlockSpec((block, width), lambda i, q: (i, 0))] * 4,
            out_specs=pl.BlockSpec((block, 4 * width), lambda i, q: (i, 0)),
        ),
        out_shape=jax.ShapeDtypeStruct((rows, 4 * width), F32),
        compiler_params=pltpu.CompilerParams(vmem_limit_bytes=56 * 2**20),
        cost_estimate=cost(0, 24 * rows * width),
        name="finish_down",
    )(quarter, *parts)


def finish_sides(core, even, parts):
    rows, width = parts[0].shape
    cut = FIRST_HEAD * HDIM

    def body(core_ref, even_ref, *refs):
        for which in range(2):
            for at in range(2):

                @pl.when((core_ref[0] == which) & (pl.program_id(0) == at))
                def _(which=which, at=at):
                    own, other = refs[at], refs[2 + at]
                    low, high = (own, other) if which == 0 else (other, own)
                    refs[4][:, :cut] = low[:, :cut].astype(F32)
                    refs[4][:, cut:] = high[:, :OWN].astype(F32)

    return pl.pallas_call(
        body,
        grid_spec=pltpu.PrefetchScalarGridSpec(
            num_scalar_prefetch=2,
            grid=(2,),
            in_specs=[
                pl.BlockSpec((rows, width), lambda i, c, e: (0, 0), pipeline_mode=pl.Buffered(1))
            ]
            * 4,
            out_specs=pl.BlockSpec((rows, cut + OWN), lambda i, c, e: (e[0] ^ i, 0)),
        ),
        out_shape=jax.ShapeDtypeStruct((2 * rows, cut + OWN), F32),
        compiler_params=pltpu.CompilerParams(vmem_limit_bytes=56 * 2**20),
        cost_estimate=cost(0, 16 * rows * width),
        name="finish_sides",
    )(core, even, *parts)


def to_sixteen(count):
    return -(-count // 16) * 16


class Moves:
    def __init__(self, shard_count, replica_count):
        self.shard_count = shard_count
        self.replica_count = replica_count
        self.shard = lax.axis_index("shard")
        replica = lax.axis_index("replica")
        self.core = replica % 2
        self.column = replica // 2
        self.square = shard_count == 4 and replica_count == 8
        self.core_ref = self.core.astype(jnp.int32)[None]
        me = self.shard
        self.places = jnp.stack([me, me ^ 1, me ^ 2, me ^ 3]).astype(jnp.int32)
        self.order = jnp.stack([me ^ 3, me ^ 1, me ^ 2, me]).astype(jnp.int32)

    def move(self, array, route):
        pairs, stays = [], []
        for shard in range(self.shard_count):
            for column in range(self.replica_count // 2):
                for core in range(2):
                    target = route(shard, column, core)
                    if target == (shard, column, core):
                        stays.append((shard, core))
                    elif target is not None:
                        to_shard, to_column, to_core = target
                        pairs.append(
                            (
                                shard * self.replica_count + 2 * column + core,
                                to_shard * self.replica_count + 2 * to_column + to_core,
                            )
                        )
        came = lax.ppermute(array, AXES, pairs)
        if not stays:
            return came
        table = [(s, c) in stays for s in range(self.shard_count) for c in range(2)]
        return jnp.where(jnp.asarray(table)[2 * self.shard + self.core], array, came)

    def over_x(self, array):
        return self.move(array, lambda s, z, c: (s ^ 1, z, c))

    def over_y(self, array):
        return self.move(array, lambda s, z, c: (s ^ 2, z, c))

    def over_z(self, array, step):
        return self.move(array, lambda s, z, c: (s, z ^ step, c))

    def over_core(self, array):
        return self.move(array, lambda s, z, c: (s, z, 1 - c))

    def gather_near(self, piece):
        if not self.square:
            return (piece,)
        return piece, self.over_x(piece), self.over_y(piece)

    def gather_far(self, near):
        if not self.square:
            return ()
        count = near[0].shape[0]
        rows = to_sixteen(count // 2)
        return self.over_x(near[2][:rows]), self.over_y(near[1][rows:])

    def lay(self, near, far, parts=1):
        if self.square:
            return lay(self.places, near, far, parts)
        size = near[0].shape[0] // parts
        return [
            lax.all_gather(near[0][at * size : (at + 1) * size], "shard", axis=0, tiled=True)
            for at in range(parts)
        ]

    def scatter(self, pairs, cut, columns, wait=()):
        if not self.square:
            sums = []
            for left, right in pairs:
                left = jnp.concatenate(side_of(left), axis=1)
                right = jnp.concatenate(side_of(right), axis=1)
                value = product(left, right, "nt", 400)
                sums.append(lax.psum_scatter(value, "shard", scatter_dimension=0, tiled=True))
            sums = jnp.concatenate(sums, axis=0)
            return sums, [], [], []
        send_x, send_y, keep_x, keep_y = product_parts(self.order, pairs, cut, wait)
        half = send_x.shape[0] // 2
        came_x, came_y = self.over_x(send_x), self.over_y(send_y)
        last_x = self.over_y(keep_x[:half] + came_x[:half])
        last_y = self.over_x(keep_y[:half] + came_y[:half])
        folded = fold(keep_x, came_x, last_x, keep_y, came_y, last_y, columns)
        return folded, [send_x], [came_x, came_y], [last_x, last_y]

    def total(self, array):
        if not self.square:
            groups = [
                [2 * column + core for column in range(self.replica_count // 2)]
                for core in range(2)
            ]
            return (lax.psum(array, "replica", axis_index_groups=groups),)
        rows = array.shape[0] // 2
        even = self.column % 2
        keep = lax.dynamic_slice_in_dim(array, even * rows, rows, 0)
        send = lax.dynamic_slice_in_dim(array, (1 - even) * rows, rows, 0)
        pair = keep + self.over_z(send, 1)
        full = pair + self.over_z(pair, 2)
        return full, self.over_z(full, 1)

    def sides(self, sums):
        if self.square:
            parts = list(sums) + [self.over_core(half) for half in sums]
            return finish_sides(self.core_ref, (self.column % 2).astype(jnp.int32)[None], parts)
        own = sums[0]
        other = self.over_core(own)
        first = self.core == 0
        low, high = jnp.where(first, own, other), jnp.where(first, other, own)
        return jnp.concatenate([low[:, : FIRST_HEAD * HDIM], high[:, :OWN]], axis=1).astype(F32)

    def total_alike(self, array):
        if not self.square:
            groups = [
                [2 * column + core for column in range(even, self.replica_count // 2, 2)]
                for even in range(2)
                for core in range(2)
            ]
            return lax.psum(array, "replica", axis_index_groups=groups)
        return array + self.over_z(array, 2)

    def total_small(self, array):
        if not self.square:
            return lax.psum(array, AXES)
        array = array + self.over_core(array)
        array = array + self.over_x(array)
        array = array + self.over_y(array)
        array = array + self.over_z(array, 1)
        return array + self.over_z(array, 2)

    def owners(self, step, seqs):
        return lambda s, z, c: (seqs * c + (s + step) % seqs, z, s // seqs)

    def to_chips(self, local, turn):
        seqs, _, count = local.shape
        came = []
        for step in range(seqs):
            at = (self.shard + step) % seqs + turn
            sent = lax.dynamic_index_in_dim(local, at, 0, keepdims=False)
            came.append(self.move(sent, self.owners(step, seqs)))
        at = self.shard % seqs
        if seqs == 2:
            first = at == 0
            return jnp.concatenate(
                [jnp.where(first, came[0], came[1]), jnp.where(first, came[1], came[0])], axis=1
            )
        ring = jnp.concatenate((came[::-1] * 2)[: 2 * seqs - 1], axis=1)
        return lax.dynamic_slice_in_dim(ring, (seqs - 1 - at) * count, seqs * count, 1)

    def from_chips(self, half, seqs):
        count = half.shape[1] // seqs
        at = self.shard % seqs
        outs = []
        for step in range(seqs):
            route = self.owners(step, seqs)
            back = {}
            for s in range(self.shard_count):
                for z in range(self.replica_count // 2):
                    for c in range(2):
                        back[route(s, z, c)] = (s, z, c)
            sent = lax.dynamic_slice_in_dim(half, ((at - step) % seqs) * count, count, 1)
            outs.append(self.move(sent, lambda s, z, c: back[(s, z, c)]))
        if seqs == 2:
            first = at == 0
            return jnp.stack(
                [jnp.where(first, outs[0], outs[1]), jnp.where(first, outs[1], outs[0])]
            )
        stacked = jnp.stack(outs)
        doubled = jnp.concatenate([stacked, stacked[: seqs - 1]], axis=0)
        return lax.dynamic_slice_in_dim(doubled, (seqs - at) % seqs, seqs, 0)

    def both(self, half):
        other = self.over_core(half)
        first = self.core == 0
        return jnp.concatenate(
            [jnp.where(first, half, other), jnp.where(first, other, half)], axis=1
        )

    def spread(self, half):
        across = self.over_z(half, 1)
        return [half, across, self.over_core(half), self.over_core(across)]

    def collect(self, here, there):
        half = here.shape[1] // 2
        came = self.over_core(there)
        across = self.over_z(here[:, half:] + came[:, half:], 1)
        return here[:, :half].astype(F32) + came[:, :half].astype(F32) + across.astype(F32)


def shards(
    shard_count,
    replica_count,
    hidden_in,
    out_grad,
    segments,
    ln1_gain,
    ln1_bias,
    qkv_weight,
    q_bias,
    v_bias,
    output_projection_weight,
    out_bias,
    ln2_gain,
    ln2_bias,
    up_weight,
    up_bias,
    down_weight,
    down_bias,
):
    moves = Moves(shard_count, replica_count)
    core = moves.core
    quarter = 2 * (moves.column % 2) + core
    seqs = hidden_in.shape[1]
    width = hidden_in.shape[2]
    length = segments.shape[0]
    half_len = length // 2
    ff = up_bias.shape[0]
    strip = ff // shard_count // 4
    first_row = core * FIRST_HEAD * HDIM
    rows_of = functools.partial(lax.dynamic_slice_in_dim, slice_size=OWN, axis=0)
    half_of = functools.partial(lax.dynamic_slice_in_dim, slice_size=half_len, axis=1)
    mine, theirs = core * half_len, (1 - core) * half_len

    def column(vector):
        return vector[:, None]

    def after(*arrays):
        return sum(jnp.isnan(array[0, 0]).astype(jnp.int32) for array in arrays)

    qkv_count = qkv_weight.shape[0]
    qkv_rows = to_sixteen(qkv_count // 2)
    qkv_over = 2 * qkv_rows - qkv_count
    qkv_near = moves.gather_near(
        lax.dynamic_slice_in_dim(qkv_weight, core * (qkv_count - qkv_rows), qkv_rows, 0)
    )
    turn = after(*qkv_near[1:]) if moves.square else 0
    tokens_half = moves.to_chips(hidden_in.transpose(1, 2, 0), turn)
    qkv_far = moves.gather_far(qkv_near)
    turn = after(*qkv_far) if moves.square else 0
    twice = (core == 1) & (jnp.arange(OWN) < HDIM)
    out_near = moves.gather_near(
        jnp.where(
            twice[None, :],
            0,
            lax.dynamic_slice_in_dim(output_projection_weight, first_row + turn, OWN, 1),
        ).astype(BF16)
    )
    grad_half = moves.to_chips(out_grad.transpose(1, 2, 0), turn)
    ff_near = moves.gather_near(
        jnp.concatenate(
            [
                lax.dynamic_slice_in_dim(up_weight, quarter * strip + turn, strip, 0),
                jnp.concatenate(
                    [
                        lax.dynamic_slice_in_dim(
                            down_weight, (4 * shard + quarter) * strip, strip, 1
                        )
                        for shard in range(shard_count)
                    ],
                    axis=1,
                ),
            ],
            axis=0,
        )
    )
    out_far = moves.gather_far(out_near)
    (w_out,) = moves.lay(out_near, out_far)
    ff_far = moves.gather_far(ff_near)
    w_up, w_down = moves.lay(ff_near, ff_far, 2)
    if moves.square:
        qkv_own = list(qkv_near) + list(qkv_far)
        qkv_other = [moves.over_core(piece) for piece in qkv_own]
        w_qkv = lay_heads(moves.core_ref, moves.places, qkv_own, qkv_other, qkv_count)
    else:
        (qkv_half,) = moves.lay(qkv_near, qkv_far)
        qkv_other = moves.over_core(qkv_half)
        low = jnp.where(core == 0, qkv_half, qkv_other)
        high = jnp.where(core == 0, qkv_other, qkv_half)
        qkv_full = jnp.concatenate(
            [
                block[shard * qkv_rows + skip : (shard + 1) * qkv_rows]
                for shard in range(shard_count)
                for block, skip in ((low, 0), (high, qkv_over))
            ],
            axis=0,
        )
        w_qkv = jnp.concatenate(
            [rows_of(qkv_full, part * width + first_row) for part in range(3)], axis=0
        )
    up_bias_own = lax.dynamic_index_in_dim(
        up_bias.reshape(shard_count, 4, strip), quarter, 1, keepdims=False
    ).reshape(-1)
    seg_pair = jnp.stack([segments, moves.over_core(segments)])
    home = moves.shard // seqs
    seg = lax.dynamic_index_in_dim(
        lax.dynamic_index_in_dim(seg_pair, (home != core).astype(jnp.int32), 0, keepdims=False),
        moves.shard % seqs,
        1,
        keepdims=False,
    )

    tokens = tokens_half.astype(F32)
    unit_one, scale_one = norm_parts(tokens)
    normed = moves.both((unit_one * column(ln1_gain) + column(ln1_bias)).astype(BF16))
    zeros = jnp.zeros((OWN,), F32)
    joined_bias = jnp.concatenate([rows_of(q_bias, first_row), zeros, rows_of(v_bias, first_row)])
    row_scale = jnp.where(jnp.arange(3 * OWN) < OWN, 0.125, 1.0).astype(F32)
    joined = product(
        w_qkv,
        normed,
        "nn",
        416,
        lambda value, at, bias, scale: (
            (value + bias[...]).astype(BF16).astype(F32) * scale[...],
        ),
        (column(joined_bias), column(row_scale)),
        name="project_qkv",
    )
    mixed, lse = attention(seg, joined, [*out_near[1:], grad_half])
    grad_out = moves.spread(grad_half)
    branch = product(
        w_out, mixed, "nn", 400, name="project_out", wait=[*ff_near[1:], grad_out[1]]
    )
    branch_half = half_of(branch, mine).astype(F32)
    branch_half = branch_half + moves.over_core(half_of(branch, theirs)).astype(F32)
    middle = tokens + branch_half + column(out_bias)
    unit_two, scale_two = norm_parts(middle)
    normed_two = moves.spread((unit_two * column(ln2_gain) + column(ln2_bias)).astype(BF16))
    activ, slope = product(
        w_up,
        normed_two,
        "nn",
        320,
        lambda value, at, bias: gelu_pair(value + bias[...]),
        (column(up_bias_own),),
        ((None, BF16), (None, BF16)),
        name="project_up",
        wait=grad_out,
    )

    ff_cut = 896 if width == 1600 else width // 256 * 128
    down_part, down_made, down_first, down_last = moves.scatter(
        [(grad_out, activ)], ff_cut, width
    )

    def through_gelu(value, at, slope_ref):
        size = value.shape[1]
        slope_here = slope_ref[:, at * size : (at + 1) * size].astype(F32)
        grad = (value * slope_here).astype(BF16)
        return grad, lane_sums(grad.astype(F32))

    def in_halves(value, at):
        half = value.shape[1] // 2
        return value[:, :half], value[:, half:]

    grad_pre, grad_pre_sums = product(
        w_down,
        grad_out,
        "tn",
        256,
        through_gelu,
        (slope,),
        ((None, BF16), (512, F32)),
        name="back_down",
        wait=down_made,
    )
    halves = ((length, BF16), (length, BF16))
    grad_norm_two = moves.collect(
        *product(w_up, grad_pre, "tn", 256, in_halves, (), halves, name="back_up")
    )
    up_part, up_made, up_first, up_last = moves.scatter([(grad_pre, normed_two)], ff_cut, width)
    down_here, down_there = product(
        w_down, activ, "nn", 320, in_halves, (), halves, name="project_down", wait=up_made
    )
    down_half = moves.collect(down_here, down_there)
    grad_out_f = grad_half.astype(F32)
    grad_middle = grad_out_f + norm_back(grad_norm_two, unit_two, scale_two, column(ln2_gain))
    grad_branch_half = grad_middle.astype(BF16)
    grad_branch = moves.both(grad_branch_half)
    grad_mixed = product(
        w_out, grad_branch, "tn", OWN, name="back_out", wait=[down_here, *down_first, *down_last]
    )
    padded = to_tiles(OWN)
    out_part, out_made, out_first, out_last = moves.scatter([(grad_branch, mixed)], 512, padded)
    down_sum = moves.total_alike(down_part)
    up_sum = moves.total_alike(up_part)
    out_sum = moves.total(out_part)
    result = moves.from_chips((middle + down_half + column(down_bias)).astype(BF16), seqs)

    grad_own = attention_back(
        seg, joined, mixed, grad_mixed, lse, [*out_made, *up_first]
    ).reshape(3 * OWN, length)
    grad_other = moves.over_core(grad_own)
    grad_norm_one = product(
        w_qkv, grad_own, "tn", 256, name="back_qkv", wait=[*out_first, *up_last]
    )
    if moves.square:
        grad_joined = join_heads(moves.core_ref, grad_own, grad_other)
    else:
        low = jnp.where(core == 0, grad_own, grad_other)
        high = jnp.where(core == 0, grad_other, grad_own)
        grad_joined = jnp.concatenate(
            [
                piece
                for part in range(3)
                for piece in (
                    low[part * OWN : (part + 1) * OWN],
                    high[part * OWN + HDIM : (part + 1) * OWN],
                )
            ],
            axis=0,
        )
    qkv_part, _, _, _ = moves.scatter(
        [(grad_joined, rows_of(normed, first_row))], 512, padded, [*out_last]
    )
    qkv_sum = moves.total(qkv_part)
    grad_norm_one = half_of(grad_norm_one, mine).astype(F32) + moves.over_core(
        half_of(grad_norm_one, theirs)
    ).astype(F32)
    input_half = grad_middle + norm_back(grad_norm_one, unit_one, scale_one, column(ln1_gain))
    input_grad = moves.from_chips(input_half.astype(BF16), seqs).astype(F32)

    up_bias_grad = jnp.sum(grad_pre_sums, axis=1).reshape(shard_count, 1, strip)
    up_bias_grad = up_bias_grad * (jnp.arange(4)[None, :, None] == quarter).astype(F32)
    head_sums = jnp.sum(grad_own.astype(F32), axis=1).reshape(3, OWN)
    bias_sums = lax.dynamic_update_slice(
        jnp.zeros((3, width), F32), head_sums, (jnp.int32(0), first_row)
    )
    small = moves.total_small(
        jnp.concatenate(
            [
                up_bias_grad.reshape(-1),
                jnp.sum(grad_norm_two * unit_two, axis=1),
                jnp.sum(grad_norm_two, axis=1),
                jnp.sum(grad_out_f, axis=1),
                jnp.sum(grad_branch_half.astype(F32), axis=1),
                jnp.sum(grad_norm_one * unit_one, axis=1),
                jnp.sum(grad_norm_one, axis=1),
                bias_sums[0],
                bias_sums[2],
            ]
        ).reshape(-1, 128)
    ).reshape(-1)
    up_bias_grad, rest = small[:ff], small[ff:]
    (
        ln2_gain_grad,
        ln2_bias_grad,
        down_bias_grad,
        out_bias_grad,
        ln1_gain_grad,
        ln1_bias_grad,
        q_bias_grad,
        v_bias_grad,
    ) = rest.reshape(8, width)

    def quarters(own):
        across = moves.over_z(own, 1)
        return [own, moves.over_core(own), across, moves.over_core(across)]

    quarter_ref = quarter.astype(jnp.int32)[None]
    down_total = finish_down(quarter_ref, quarters(down_sum), shard_count)
    up_total = finish_up(quarter_ref, quarters(up_sum))

    return (
        result.transpose(2, 0, 1),
        input_grad.transpose(2, 0, 1),
        ln1_gain_grad,
        ln1_bias_grad,
        moves.sides(qkv_sum),
        q_bias_grad,
        v_bias_grad,
        moves.sides(out_sum),
        out_bias_grad,
        ln2_gain_grad,
        ln2_bias_grad,
        up_total,
        up_bias_grad,
        down_total,
        down_bias_grad,
    )


def solution(mesh):
    rows = P("shard", None)
    tokens = P("shard", "replica", None)
    in_specs = (
        tokens,
        tokens,
        P(None, "replica"),
        P(),
        P(),
        rows,
        P(),
        P(),
        rows,
        P(),
        P(),
        P(),
        rows,
        P(),
        rows,
        P(),
    )
    out_specs = (
        tokens,
        tokens,
        P(),
        P(),
        rows,
        P(),
        P(),
        rows,
        P(),
        P(),
        P(),
        rows,
        P(),
        rows,
        P(),
    )
    body = functools.partial(shards, mesh.shape["shard"], mesh.shape["replica"])
    return jax.shard_map(body, mesh=mesh, in_specs=in_specs, out_specs=out_specs, check_vma=False)
```

```python
import functools

import jax
import jax.numpy as jnp
from jax import lax
from jax.experimental import pallas as pl
from jax.experimental.pallas import tpu as pltpu
from jax.sharding import PartitionSpec as P

HEADS = 25
HDIM = 64
OWN_HEADS = HEADS // 2 + 1
FIRST_HEAD = HEADS // 2
OWN = OWN_HEADS * HDIM
BLOCK = 256
AXES = ("shard", "replica")
BF16 = jnp.bfloat16
F32 = jnp.float32


def dot(left, right, left_dim, right_dim):
    return lax.dot_general(
        left, right, (((left_dim,), (right_dim,)), ((), ())), preferred_element_type=F32
    )


COST_SCALE = 8


def cost(flops, bytes_accessed):
    return pl.CostEstimate(
        flops=int(flops * COST_SCALE),
        bytes_accessed=int(bytes_accessed * COST_SCALE),
        transcendentals=0,
    )


def norm_parts(rows):
    centre = rows - jnp.mean(rows, axis=0, keepdims=True)
    scale = lax.rsqrt(jnp.mean(centre * centre, axis=0, keepdims=True) + 1e-05)
    return centre * scale, scale


def norm_back(grad, unit, scale, gain):
    inner = grad * gain
    mean_inner = jnp.mean(inner, axis=0, keepdims=True)
    mean_cross = jnp.mean(inner * unit, axis=0, keepdims=True)
    return scale * (inner - mean_inner - unit * mean_cross)


def gelu_pair(value):
    root = 0.7978845608028654
    cube = 0.044715
    square = value * value
    tanh = jnp.tanh(root * value * (1.0 + cube * square))
    half = 0.5 * (1.0 + tanh)
    slope = half + 0.5 * value * (1.0 - tanh * tanh) * root * (1.0 + 3.0 * cube * square)
    return value * half, slope


def fill_mask(seg_row, seg_col, mask, blocks):
    for q_at in range(blocks):
        for k_at in range(q_at + 1):
            keys = seg_col[pl.ds(k_at * BLOCK, BLOCK), :]
            queries = seg_row[:, pl.ds(q_at * BLOCK, BLOCK)]
            seen = keys == queries
            if k_at == q_at:
                k_place = lax.broadcasted_iota(jnp.int32, (BLOCK, BLOCK), 0)
                q_place = lax.broadcasted_iota(jnp.int32, (BLOCK, BLOCK), 1)
                seen = seen & (k_place <= q_place)
            mask[pl.ds(k_at * BLOCK, BLOCK), pl.ds(q_at * BLOCK, BLOCK)] = jnp.where(
                seen, 0.0, -1e30
            )


def forward_kernel(seg_row, seg_col, q_ref, k_ref, v_ref, *refs):
    o_ref, lse_ref, mask = refs[-3:]
    length = q_ref.shape[1]
    blocks = length // BLOCK

    @pl.when(pl.program_id(0) == 0)
    def _():
        fill_mask(seg_row, seg_col, mask, blocks)

    keys = k_ref[...].T
    for q_at in range(blocks):
        span = (q_at + 1) * BLOCK
        here = pl.ds(q_at * BLOCK, BLOCK)
        scores = dot(keys[:span], q_ref[:, here], 1, 0) + mask[:span, here]
        peak = jnp.max(scores, axis=0, keepdims=True)
        terms = jnp.exp(scores - peak)
        total = jnp.sum(terms, axis=0, keepdims=True)
        mixed = dot(v_ref[:, :span], terms.astype(BF16), 1, 0)
        o_ref[:, here] = (mixed / total).astype(BF16)
        lse_ref[0, :, here] = peak + jnp.log(total)


def backward_kernel(seg_row, seg_col, q_ref, k_ref, v_ref, o_ref, g_ref, lse_ref, *refs):
    grads, mask, acc = refs[-3:]
    length = q_ref.shape[1]
    blocks = length // BLOCK

    @pl.when(pl.program_id(0) == 0)
    def _():
        fill_mask(seg_row, seg_col, mask, blocks)

    keys = k_ref[...].T
    values = v_ref[...].T
    delta = jnp.sum(g_ref[...].astype(F32) * o_ref[...].astype(F32), axis=0, keepdims=True)
    lse = lse_ref[0]
    for k_at in range(blocks):
        low = k_at * BLOCK
        here = pl.ds(low, BLOCK)
        rest = pl.ds(low, length - low)
        scores = dot(keys[low : low + BLOCK], q_ref[:, rest], 1, 0) + mask[here, rest]
        soft = jnp.exp(scores - lse[:, low:])
        soft_grad = dot(values[low : low + BLOCK], g_ref[:, rest], 1, 0)
        score_grad = (soft * (soft_grad - delta[:, low:])).astype(BF16)
        grads[2, :, here] = dot(g_ref[:, rest], soft.astype(BF16), 1, 1).astype(BF16)
        grads[1, :, here] = dot(q_ref[:, rest], score_grad, 1, 1).astype(BF16)
        grad_q = dot(k_ref[:, here], score_grad, 1, 0)
        if k_at == 0:
            acc[...] = grad_q
        else:
            acc[:, rest] += grad_q
    grads[0] = (acc[...] * 0.125).astype(BF16)


def head_spec(first, length):
    return pl.BlockSpec((HDIM, length), lambda head: (first + head, 0))


def whole_spec(shape):
    return pl.BlockSpec(shape, lambda head: (0,) * len(shape))


def attention(seg, joined, wait):
    length = seg.shape[0]
    lse_spec = pl.BlockSpec((1, 1, length), lambda head: (head, 0, 0))
    pairs = OWN_HEADS * length * length
    return pl.pallas_call(
        forward_kernel,
        grid=(OWN_HEADS,),
        in_specs=[whole_spec((1, length)), whole_spec((length, 1))]
        + [head_spec(part * OWN_HEADS, length) for part in range(3)]
        + [pl.BlockSpec(memory_space=pl.ANY)] * len(wait),
        out_specs=[head_spec(0, length), lse_spec],
        out_shape=[
            jax.ShapeDtypeStruct((OWN, length), BF16),
            jax.ShapeDtypeStruct((OWN_HEADS, 1, length), F32),
        ],
        scratch_shapes=[pltpu.VMEM((length, length), F32)],
        compiler_params=pltpu.CompilerParams(vmem_limit_bytes=40 * 2**20),
        cost_estimate=cost(16 * pairs * HDIM, 8 * OWN * length),
        name="attention_forward",
    )(seg.reshape(1, length), seg.reshape(length, 1), joined, joined, joined, *wait)


def attention_back(seg, joined, mixed, grad, lse, wait):
    length = seg.shape[0]
    lse_spec = pl.BlockSpec((1, 1, length), lambda head: (head, 0, 0))
    pairs = OWN_HEADS * length * length
    return pl.pallas_call(
        backward_kernel,
        grid=(OWN_HEADS,),
        in_specs=[whole_spec((1, length)), whole_spec((length, 1))]
        + [head_spec(part * OWN_HEADS, length) for part in range(3)]
        + [head_spec(0, length), head_spec(0, length), lse_spec]
        + [pl.BlockSpec(memory_space=pl.ANY)] * len(wait),
        out_specs=pl.BlockSpec((3, HDIM, length), lambda head: (0, head, 0)),
        out_shape=jax.ShapeDtypeStruct((3, OWN, length), BF16),
        scratch_shapes=[pltpu.VMEM((length, length), F32), pltpu.VMEM((HDIM, length), F32)],
        compiler_params=pltpu.CompilerParams(vmem_limit_bytes=48 * 2**20),
        cost_estimate=cost(40 * pairs * HDIM, 16 * OWN * length),
        name="attention_backward",
    )(
        seg.reshape(1, length),
        seg.reshape(length, 1),
        joined,
        joined,
        joined,
        mixed,
        grad,
        lse,
        *wait,
    )


def product(left, rights, form, block, finish=None, extras=(), outs=((None, BF16),), name="product",
            wait=()):
    rights = rights if isinstance(rights, (list, tuple)) else [rights]
    many = len(rights)
    left_dim, right_dim = (0 if form == "tn" else 1), (1 if form == "nt" else 0)
    m, k = left.shape[1 - left_dim], left.shape[left_dim]
    size = rights[0].shape[1 - right_dim]
    n = size * many
    block = min(block, m)

    def body(left_ref, *refs):
        extra_refs = refs[many : many + len(extras)]
        out_refs = refs[many + len(extras) + len(wait) :]
        for at in range(many):
            value = dot(left_ref[...], refs[at][...], left_dim, right_dim)
            values = (value,)
            if finish is not None:
                values = finish(value, at, *extra_refs)
            for ref, part in zip(out_refs, values):
                if part is not None:
                    width = part.shape[1]
                    begin = at * width % ref.shape[1]
                    ref[:, begin : begin + width] = part.astype(ref.dtype)

    if form == "tn":
        left_spec = pl.BlockSpec((k, block), lambda i: (0, i))
    else:
        left_spec = pl.BlockSpec((block, k), lambda i: (i, 0))
    sizes = [(columns or n, kind) for columns, kind in outs]
    results = pl.pallas_call(
        body,
        grid=(pl.cdiv(m, block),),
        in_specs=[left_spec]
        + [
            pl.BlockSpec(right.shape, lambda i: (0, 0), pipeline_mode=pl.Buffered(1))
            for right in rights
        ]
        + [pl.BlockSpec((block, extra.shape[1]), lambda i: (i, 0)) for extra in extras]
        + [pl.BlockSpec(memory_space=pl.ANY)] * len(wait),
        out_specs=[pl.BlockSpec((block, columns), lambda i: (i, 0)) for columns, _ in sizes],
        out_shape=[jax.ShapeDtypeStruct((m, columns), kind) for columns, kind in sizes],
        compiler_params=pltpu.CompilerParams(vmem_limit_bytes=56 * 2**20),
        cost_estimate=cost(2 * m * n * k, 2 * (m * k + n * k + m * n)),
        name=name,
    )(left, *rights, *extras, *wait)
    return results if len(outs) > 1 else results[0]


def lane_sums(value):
    return sum(value[:, at : at + 128] for at in range(0, value.shape[1], 128))


def lay(places, near, far, parts):
    count, columns = near[0].shape
    size = count // parts
    kind = near[0].dtype

    def body(places_ref, *refs):
        step = pl.program_id(0)
        outs = refs[5:]
        for at in range(3):

            @pl.when(step == at)
            def _(at=at):
                for index, out in enumerate(outs):
                    out[...] = refs[at][index * size : (index + 1) * size]

        @pl.when(step == 3)
        def _():
            start = 0
            for ref in refs[3:5]:
                rows = ref.shape[0]
                for index, out in enumerate(outs):
                    low, high = max(start, index * size), min(start + rows, (index + 1) * size)
                    if low < high:
                        out[low - index * size : high - index * size] = ref[
                            low - start : high - start
                        ]
                start += rows

    pieces = list(near) + list(far)
    return pl.pallas_call(
        body,
        grid_spec=pltpu.PrefetchScalarGridSpec(
            num_scalar_prefetch=1,
            grid=(4,),
            in_specs=[
                pl.BlockSpec(piece.shape, lambda i, p: (0, 0), pipeline_mode=pl.Buffered(1))
                for piece in pieces
            ],
            out_specs=[pl.BlockSpec((size, columns), lambda i, p: (p[i], 0))] * parts,
        ),
        out_shape=[jax.ShapeDtypeStruct((4 * size, columns), kind)] * parts,
        compiler_params=pltpu.CompilerParams(vmem_limit_bytes=56 * 2**20),
        cost_estimate=cost(0, 16 * count * columns),
        name="lay",
    )(places, *pieces)


def lay_heads(core, places, mine, others, counts, taken, wait):
    width = mine[0].shape[1]
    split = mine[3].shape[0]
    cut = FIRST_HEAD * HDIM

    def body(core_ref, places_ref, *refs):
        heads_ref, out_ref, block, out_block = refs[-4:]
        step = pl.program_id(0)

        def copy(halves, at, begin, end, target, row):
            if at < 3:
                target[row : row + end - begin] = halves[at][begin:end]
                return
            if begin < split:
                middle = min(end, split)
                target[row : row + middle - begin] = halves[3][begin:middle]
            if end > split:
                middle = max(begin, split)
                target[row + middle - begin : row + end - begin] = halves[4][
                    middle - split : end - split
                ]

        for which in range(2):

            @pl.when(core_ref[0] == which)
            def _(which=which):
                low, high = (refs[:5], refs[5:10]) if which == 0 else (refs[5:10], refs[:5])
                for at in range(4):

                    @pl.when(step == at)
                    def _(at=at):
                        begin = 0
                        for target, rows, count in zip((block, out_block), taken, counts):
                            copy(low, at, begin, begin + rows, target, 0)
                            over = 2 * rows - count
                            copy(high, at, begin + over, begin + rows, target, rows)
                            begin += rows

                out_ref[...] = out_block[:, which * cut : which * cut + OWN]
                if which == 1:
                    out_ref[:, :HDIM] = jnp.zeros((counts[1], HDIM), BF16)
                for shard in range(4):

                    @pl.when(places_ref[step] == shard)
                    def _(shard=shard):
                        for part in range(3):
                            begin = part * width + which * cut
                            first = max(begin, shard * counts[0])
                            last = min(begin + OWN, (shard + 1) * counts[0])
                            if first < last:
                                heads_ref[
                                    part * OWN + first - begin : part * OWN + last - begin
                                ] = block[first - shard * counts[0] : last - shard * counts[0]]

    pieces = list(mine) + list(others)
    return pl.pallas_call(
        body,
        grid_spec=pltpu.PrefetchScalarGridSpec(
            num_scalar_prefetch=2,
            grid=(4,),
            in_specs=[
                pl.BlockSpec(piece.shape, lambda i, c, p: (0, 0), pipeline_mode=pl.Buffered(1))
                for piece in pieces
            ]
            + [pl.BlockSpec(memory_space=pl.ANY)] * len(wait),
            out_specs=[
                pl.BlockSpec(
                    (3 * OWN, width), lambda i, c, p: (0, 0), pipeline_mode=pl.Buffered(1)
                ),
                pl.BlockSpec((counts[1], OWN), lambda i, c, p: (p[i], 0)),
            ],
            scratch_shapes=[pltpu.VMEM((count, width), BF16) for count in counts],
        ),
        out_shape=[
            jax.ShapeDtypeStruct((3 * OWN, width), BF16),
            jax.ShapeDtypeStruct((4 * counts[1], OWN), BF16),
        ],
        compiler_params=pltpu.CompilerParams(vmem_limit_bytes=56 * 2**20),
        cost_estimate=cost(0, 16 * counts[0] * width),
        name="lay_heads",
    )(core, places, *pieces, *wait)


def join_heads(core, own, other):
    length = own.shape[1]
    rows = 2 * OWN - HDIM

    def body(core_ref, own_ref, other_ref, out):
        for which in range(2):

            @pl.when(core_ref[0] == which)
            def _(which=which):
                low, high = (own_ref, other_ref) if which == 0 else (other_ref, own_ref)
                out[:OWN] = low[...]
                out[OWN:] = high[HDIM:]

    block = pl.BlockSpec((OWN, length), lambda i, c: (i, 0))
    return pl.pallas_call(
        body,
        grid_spec=pltpu.PrefetchScalarGridSpec(
            num_scalar_prefetch=1,
            grid=(3,),
            in_specs=[block, block],
            out_specs=pl.BlockSpec((rows, length), lambda i, c: (i, 0)),
        ),
        out_shape=jax.ShapeDtypeStruct((3 * rows, length), BF16),
        compiler_params=pltpu.CompilerParams(vmem_limit_bytes=56 * 2**20),
        cost_estimate=cost(0, 12 * rows * length),
        name="join_heads",
    )(core, own, other)


def product_parts(order, pairs, cut, wait):
    many = len(pairs)
    lefts = [side_of(left) for left, _ in pairs]
    rights = [side_of(right) for _, right in pairs]
    count = lefts[0][0].shape[0] // 4
    depth = sum(piece.shape[1] for piece in lefts[0])
    columns = rights[0][0].shape[0]
    rest = columns - cut
    filled = to_tiles(rest)
    starts = [0]
    for sides in lefts + rights:
        starts.append(starts[-1] + len(sides))

    def body(order_ref, *refs):
        send_x, send_y, keep_x, keep_y = refs[starts[-1] + len(wait) :]
        step = pl.program_id(0)
        targets = ((send_x, send_y), (send_x, keep_y), (keep_x, send_y), (keep_x, keep_y))
        for pair in range(many):

            @pl.when(step // 4 == pair)
            def _(pair=pair):
                left = refs[starts[pair] : starts[pair + 1]]
                right = refs[starts[many + pair] : starts[many + pair + 1]]
                value = side_product(left, right).astype(BF16)
                for at, (along_x, along_y) in enumerate(targets):

                    @pl.when(step % 4 == at)
                    def _(along_x=along_x, along_y=along_y):
                        along_x[...] = value[:, :cut]
                        along_y[:, :rest] = value[:, cut:]
                        if filled > rest:
                            along_y[:, rest:] = jnp.zeros((count, filled - rest), BF16)

    def left_spec(pair, piece):
        return pl.BlockSpec(
            (count, piece.shape[1]), lambda i, o: (o[jnp.clip(i - 4 * pair, 0, 3)], 0)
        )

    def out_spec(size, second):
        return pl.BlockSpec(
            (count, size), lambda i, o: (jnp.where(i % 4 >= second, many, 0) + i // 4, 0)
        )

    return pl.pallas_call(
        body,
        grid_spec=pltpu.PrefetchScalarGridSpec(
            num_scalar_prefetch=1,
            grid=(4 * many,),
            in_specs=[left_spec(pair, piece) for pair in range(many) for piece in lefts[pair]]
            + [
                pl.BlockSpec(piece.shape, lambda i, o: (0, 0), pipeline_mode=pl.Buffered(1))
                for right in rights
                for piece in right
            ]
            + [pl.BlockSpec(memory_space=pl.ANY)] * len(wait),
            out_specs=[
                out_spec(cut, 1),
                out_spec(filled, 2),
                out_spec(cut, 3),
                out_spec(filled, 3),
            ],
        ),
        out_shape=[
            jax.ShapeDtypeStruct((2 * many * count, size), BF16)
            for size in (cut, filled, cut, filled)
        ],
        compiler_params=pltpu.CompilerParams(vmem_limit_bytes=56 * 2**20),
        cost_estimate=cost(8 * many * count * depth * columns, 8 * many * count * (depth + columns)),
        name="product_parts",
    )(order, *[piece for sides in lefts + rights for piece in sides], *wait)


def side_of(side):
    return list(side) if isinstance(side, (list, tuple)) else [side]


def side_product(left, right):
    if len(left) == len(right) == 1:
        return dot(left[0][...], right[0][...], 1, 1)
    total = None
    size = left[0].shape[1] if len(left) > 1 else right[0].shape[1]
    for at in range(max(len(left), len(right))):
        here = slice(at * size, (at + 1) * size)
        one = left[at][...] if len(left) > 1 else left[0][:, here]
        two = right[at][...] if len(right) > 1 else right[0][:, here]
        value = dot(one, two, 1, 1)
        total = value if total is None else total + value
    return total


def to_tiles(count):
    return -(-count // 128) * 128


def fold(keep_x, came_x, last_x, keep_y, came_y, last_y, columns):
    rows, cut = last_x.shape
    filled = last_y.shape[1]
    rest = columns - cut
    block = 400
    steps = rows // block

    def body(*refs):
        out = refs[6]
        for first, begin, size in ((0, 0, cut), (3, cut, rest)):
            value = refs[first][:, :size].astype(F32) + refs[first + 1][:, :size].astype(F32)
            value = value + refs[first + 2][:, :size].astype(F32)
            out[:, begin : begin + size] = value.astype(BF16)

    def specs(size):
        second = pl.BlockSpec((block, size), lambda i: (steps + i, 0))
        return [second, second, pl.BlockSpec((block, size), lambda i: (i, 0))]

    return pl.pallas_call(
        body,
        grid=(steps,),
        in_specs=specs(cut) + specs(filled),
        out_specs=pl.BlockSpec((block, columns), lambda i: (i, 0)),
        out_shape=jax.ShapeDtypeStruct((rows, columns), BF16),
        compiler_params=pltpu.CompilerParams(vmem_limit_bytes=56 * 2**20),
        cost_estimate=cost(0, 8 * rows * columns),
        name="fold",
    )(keep_x, came_x, last_x, keep_y, came_y, last_y)


def finish_up(quarter, parts):
    rows, width = parts[0].shape

    def body(quarter_ref, *refs):
        for at in range(4):

            @pl.when(pl.program_id(0) == at)
            def _(at=at):
                refs[4][...] = refs[at][...].astype(F32)

    return pl.pallas_call(
        body,
        grid_spec=pltpu.PrefetchScalarGridSpec(
            num_scalar_prefetch=1,
            grid=(4,),
            in_specs=[
                pl.BlockSpec((rows, width), lambda i, q: (0, 0), pipeline_mode=pl.Buffered(1))
            ]
            * 4,
            out_specs=pl.BlockSpec((rows, width), lambda i, q: (q[0] ^ i, 0)),
        ),
        out_shape=jax.ShapeDtypeStruct((4 * rows, width), F32),
        compiler_params=pltpu.CompilerParams(vmem_limit_bytes=56 * 2**20),
        cost_estimate=cost(0, 24 * rows * width),
        name="finish_up",
    )(quarter, *parts)


def finish_down(quarter, parts, shard_count):
    rows, width = parts[0].shape
    strip = width // shard_count
    block = 80 if rows % 80 == 0 else 40
    steps = rows // block

    def body(quarter_ref, *refs):
        for which in range(4):

            @pl.when(quarter_ref[0] == which)
            def _(which=which):
                for shard in range(shard_count):
                    for at in range(4):
                        begin = (4 * shard + at) * strip
                        refs[4][:, begin : begin + strip] = refs[which ^ at][
                            :, shard * strip : (shard + 1) * strip
                        ].astype(F32)

    return pl.pallas_call(
        body,
        grid_spec=pltpu.PrefetchScalarGridSpec(
            num_scalar_prefetch=1,
            grid=(steps,),
            in_specs=[pl.BlockSpec((block, width), lambda i, q: (i, 0))] * 4,
            out_specs=pl.BlockSpec((block, 4 * width), lambda i, q: (i, 0)),
        ),
        out_shape=jax.ShapeDtypeStruct((rows, 4 * width), F32),
        compiler_params=pltpu.CompilerParams(vmem_limit_bytes=56 * 2**20),
        cost_estimate=cost(0, 24 * rows * width),
        name="finish_down",
    )(quarter, *parts)


def finish_sides(core, even, parts):
    rows, width = parts[0].shape
    cut = FIRST_HEAD * HDIM

    def body(core_ref, even_ref, *refs):
        for which in range(2):
            for at in range(2):

                @pl.when((core_ref[0] == which) & (pl.program_id(0) == at))
                def _(which=which, at=at):
                    own, other = refs[at], refs[2 + at]
                    low, high = (own, other) if which == 0 else (other, own)
                    refs[4][:, :cut] = low[:, :cut].astype(F32)
                    refs[4][:, cut:] = high[:, :OWN].astype(F32)

    return pl.pallas_call(
        body,
        grid_spec=pltpu.PrefetchScalarGridSpec(
            num_scalar_prefetch=2,
            grid=(2,),
            in_specs=[
                pl.BlockSpec((rows, width), lambda i, c, e: (0, 0), pipeline_mode=pl.Buffered(1))
            ]
            * 4,
            out_specs=pl.BlockSpec((rows, cut + OWN), lambda i, c, e: (e[0] ^ i, 0)),
        ),
        out_shape=jax.ShapeDtypeStruct((2 * rows, cut + OWN), F32),
        compiler_params=pltpu.CompilerParams(vmem_limit_bytes=56 * 2**20),
        cost_estimate=cost(0, 16 * rows * width),
        name="finish_sides",
    )(core, even, *parts)


def to_sixteen(count):
    return -(-count // 16) * 16


def late(arrays, events):
    arrays = list(arrays)
    events = [event for event in events if event is not None]
    if not events:
        return arrays
    return lax.optimization_barrier((*arrays, *events))[: len(arrays)]


class Moves:
    def __init__(self, shard_count, replica_count):
        self.shard_count = shard_count
        self.replica_count = replica_count
        self.shard = lax.axis_index("shard")
        replica = lax.axis_index("replica")
        self.core = replica % 2
        self.column = replica // 2
        self.square = shard_count == 4 and replica_count == 8
        self.core_ref = self.core.astype(jnp.int32)[None]
        me = self.shard
        self.places = jnp.stack([me, me ^ 1, me ^ 2, me ^ 3]).astype(jnp.int32)
        self.order = jnp.stack([me ^ 3, me ^ 1, me ^ 2, me]).astype(jnp.int32)

    def move(self, array, route):
        pairs, stays = [], []
        for shard in range(self.shard_count):
            for column in range(self.replica_count // 2):
                for core in range(2):
                    target = route(shard, column, core)
                    if target == (shard, column, core):
                        stays.append((shard, core))
                    elif target is not None:
                        to_shard, to_column, to_core = target
                        pairs.append(
                            (
                                shard * self.replica_count + 2 * column + core,
                                to_shard * self.replica_count + 2 * to_column + to_core,
                            )
                        )
        came = lax.ppermute(array, AXES, pairs)
        if not stays:
            return came
        table = [(s, c) in stays for s in range(self.shard_count) for c in range(2)]
        return jnp.where(jnp.asarray(table)[2 * self.shard + self.core], array, came)

    def over_x(self, array):
        return self.move(array, lambda s, z, c: (s ^ 1, z, c))

    def over_y(self, array):
        return self.move(array, lambda s, z, c: (s ^ 2, z, c))

    def over_z(self, array, step):
        return self.move(array, lambda s, z, c: (s, z ^ step, c))

    def over_core(self, array):
        return self.move(array, lambda s, z, c: (s, z, 1 - c))

    def lay(self, near, far, parts=1):
        if self.square:
            return lay(self.places, near, far, parts)
        size = near[0].shape[0] // parts
        return [
            lax.all_gather(near[0][at * size : (at + 1) * size], "shard", axis=0, tiled=True)
            for at in range(parts)
        ]

    def scatter_first(self, pairs, cut, wait=()):
        if not self.square:
            return [
                product(
                    jnp.concatenate(side_of(left), axis=1),
                    jnp.concatenate(side_of(right), axis=1),
                    "nt",
                    400,
                )
                for left, right in pairs
            ]
        return product_parts(self.order, pairs, cut, wait)

    def scatter_near(self, parts, wait=()):
        if not self.square:
            return parts, []
        send_x, send_y = late(parts[:2], wait)
        return parts, [self.over_x(send_x), self.over_y(send_y)]

    def scatter_far(self, near, wait=()):
        parts, came = near
        if not self.square:
            return near, []
        keep_x, keep_y = parts[2:]
        half = keep_x.shape[0] // 2
        came_x, came_y = late(came, wait)
        last_x = self.over_y(keep_x[:half] + came_x[:half])
        last_y = self.over_x(keep_y[:half] + came_y[:half])
        return near, [last_x, last_y]

    def scatter_last(self, far, columns):
        (parts, came), last = far
        if not self.square:
            sums = [
                lax.psum_scatter(part, "shard", scatter_dimension=0, tiled=True) for part in parts
            ]
            return jnp.concatenate(sums, axis=0)
        return fold(parts[2], came[0], last[0], parts[3], came[1], last[1], columns)

    def total_pair(self, array):
        if not self.square:
            return array
        rows = array.shape[0] // 2
        even = self.column % 2
        keep = lax.dynamic_slice_in_dim(array, even * rows, rows, 0)
        send = lax.dynamic_slice_in_dim(array, (1 - even) * rows, rows, 0)
        return keep + self.over_z(send, 1)

    def total_all(self, pair):
        if not self.square:
            groups = [
                [2 * column + core for column in range(self.replica_count // 2)]
                for core in range(2)
            ]
            return lax.psum(pair, "replica", axis_index_groups=groups)
        return pair + self.over_z(pair, 2)

    def total_halves(self, full):
        return (full, self.over_z(full, 1)) if self.square else (full,)

    def sides(self, sums):
        if self.square:
            parts = list(sums) + [self.over_core(half) for half in sums]
            return finish_sides(self.core_ref, (self.column % 2).astype(jnp.int32)[None], parts)
        own = sums[0]
        other = self.over_core(own)
        first = self.core == 0
        low, high = jnp.where(first, own, other), jnp.where(first, other, own)
        return jnp.concatenate([low[:, : FIRST_HEAD * HDIM], high[:, :OWN]], axis=1).astype(F32)

    def alike(self, array):
        if not self.square:
            groups = [
                [2 * column + core for column in range(even, self.replica_count // 2, 2)]
                for even in range(2)
                for core in range(2)
            ]
            return lax.psum(array, "replica", axis_index_groups=groups)
        return self.over_z(array, 2)

    def alike_sum(self, array, came):
        return array + came if self.square else came

    def total_small(self, array):
        if not self.square:
            return lax.psum(array, AXES)
        array = array + self.over_core(array)
        array = array + self.over_x(array)
        array = array + self.over_y(array)
        array = array + self.over_z(array, 1)
        return array + self.over_z(array, 2)

    def owners(self, step, seqs):
        return lambda s, z, c: (seqs * c + (s + step) % seqs, z, s // seqs)

    def to_chips(self, local):
        seqs, _, count = local.shape
        came = []
        for step in range(seqs):
            at = (self.shard + step) % seqs
            sent = lax.dynamic_index_in_dim(local, at, 0, keepdims=False)
            came.append(self.move(sent, self.owners(step, seqs)))
        return came

    def in_half(self, came):
        seqs = len(came)
        count = came[0].shape[1]
        at = self.shard % seqs
        if seqs == 2:
            first = at == 0
            return jnp.concatenate(
                [jnp.where(first, came[0], came[1]), jnp.where(first, came[1], came[0])], axis=1
            )
        ring = jnp.concatenate((came[::-1] * 2)[: 2 * seqs - 1], axis=1)
        return lax.dynamic_slice_in_dim(ring, (seqs - 1 - at) * count, seqs * count, 1)

    def from_chips(self, half, seqs):
        count = half.shape[1] // seqs
        at = self.shard % seqs
        outs = []
        for step in range(seqs):
            route = self.owners(step, seqs)
            back = {}
            for s in range(self.shard_count):
                for z in range(self.replica_count // 2):
                    for c in range(2):
                        back[route(s, z, c)] = (s, z, c)
            sent = lax.dynamic_slice_in_dim(half, ((at - step) % seqs) * count, count, 1)
            outs.append(self.move(sent, lambda s, z, c: back[(s, z, c)]))
        if seqs == 2:
            first = at == 0
            return jnp.stack(
                [jnp.where(first, outs[0], outs[1]), jnp.where(first, outs[1], outs[0])]
            )
        stacked = jnp.stack(outs)
        doubled = jnp.concatenate([stacked, stacked[: seqs - 1]], axis=0)
        return lax.dynamic_slice_in_dim(doubled, (seqs - at) % seqs, seqs, 0)

    def ordered(self, half, other):
        first = self.core == 0
        return jnp.concatenate(
            [jnp.where(first, half, other), jnp.where(first, other, half)], axis=1
        )


def shards(
    shard_count,
    replica_count,
    hidden_in,
    out_grad,
    segments,
    ln1_gain,
    ln1_bias,
    qkv_weight,
    q_bias,
    v_bias,
    output_projection_weight,
    out_bias,
    ln2_gain,
    ln2_bias,
    up_weight,
    up_bias,
    down_weight,
    down_bias,
):
    moves = Moves(shard_count, replica_count)
    core = moves.core
    quarter = 2 * (moves.column % 2) + core
    seqs = hidden_in.shape[1]
    width = hidden_in.shape[2]
    length = segments.shape[0]
    half_len = length // 2
    ff = up_bias.shape[0]
    strip = ff // shard_count // 4
    first_row = core * FIRST_HEAD * HDIM
    rows_of = functools.partial(lax.dynamic_slice_in_dim, slice_size=OWN, axis=0)
    half_of = functools.partial(lax.dynamic_slice_in_dim, slice_size=half_len, axis=1)
    mine, theirs = core * half_len, (1 - core) * half_len

    def column(vector):
        return vector[:, None]


    counts = (qkv_weight.shape[0], output_projection_weight.shape[0])
    taken = tuple(to_sixteen(count // 2) for count in counts)
    mine_of = [
        lax.dynamic_slice_in_dim(weight, core * (count - rows), rows, 0)
        for weight, count, rows in zip((qkv_weight, output_projection_weight), counts, taken)
    ]
    ff_piece = jnp.concatenate(
        [
            lax.dynamic_slice_in_dim(up_weight, quarter * strip, strip, 0),
            jnp.concatenate(
                [
                    lax.dynamic_slice_in_dim(down_weight, (4 * shard + quarter) * strip, strip, 1)
                    for shard in range(shard_count)
                ],
                axis=1,
            ),
        ],
        axis=0,
    )
    up_bias_own = lax.dynamic_index_in_dim(
        up_bias.reshape(shard_count, 4, strip), quarter, 1, keepdims=False
    ).reshape(-1)
    tokens_came = moves.to_chips(hidden_in.transpose(1, 2, 0))
    if moves.square:
        heads_piece = jnp.concatenate(mine_of, axis=0)
        heads_x, heads_y = moves.over_x(heads_piece), moves.over_y(heads_piece)
        other_own = moves.over_core(heads_piece)
        events = [heads_x, heads_y, other_own, *tokens_came, ff_piece]

        heads_x, heads_y, segments_sent, *tokens_came = late(
            [heads_x, heads_y, segments, *tokens_came], events
        )
        split = to_sixteen(heads_piece.shape[0] // 2)
        heads_low = moves.over_x(heads_y[:split])
        heads_high = moves.over_y(heads_x[split:])
        other_x, other_y = moves.over_core(heads_x), moves.over_core(heads_y)
        segments_other = moves.over_core(segments_sent)
        events = [heads_low, heads_high, other_x, other_y, segments_other]
    else:
        segments_other = moves.over_core(segments)
        events = []
    tokens = moves.in_half(tokens_came).astype(F32)
    unit_one, scale_one = norm_parts(tokens)
    normed_half = (unit_one * column(ln1_gain) + column(ln1_bias)).astype(BF16)
    events = [*events, normed_half]
    home = moves.shard // seqs
    seg = jnp.where(home == core, segments, segments_other)
    seg = lax.dynamic_index_in_dim(seg, moves.shard % seqs, 1, keepdims=False)

    out_grad, normed_half = late([out_grad, normed_half], events)
    if moves.square:
        heads_low, heads_high = late([heads_low, heads_high], events)
        other_low, other_high = moves.over_core(heads_low), moves.over_core(heads_high)
        events = [other_low, other_high]
    else:
        events = []
    normed_other = moves.over_core(normed_half)
    grad_came = moves.to_chips(out_grad.transpose(1, 2, 0))
    events = [*events, normed_other, *grad_came]

    ff_piece, normed_other, *grad_came = late([ff_piece, normed_other, *grad_came], events)
    if moves.square:
        ff_x, ff_y = moves.over_x(ff_piece), moves.over_y(ff_piece)
        w_qkv, w_out = lay_heads(
            moves.core_ref,
            moves.places,
            [heads_piece, heads_x, heads_y, heads_low, heads_high],
            [other_own, other_x, other_y, other_low, other_high],
            counts,
            taken,
            events,
        )
        events = [ff_x, ff_y]
    else:
        (qkv_half,) = moves.lay([mine_of[0]], ())
        qkv_other = moves.over_core(qkv_half)
        low = jnp.where(core == 0, qkv_half, qkv_other)
        high = jnp.where(core == 0, qkv_other, qkv_half)
        rows = taken[0]
        qkv_full = jnp.concatenate(
            [
                block[shard * rows + skip : (shard + 1) * rows]
                for shard in range(shard_count)
                for block, skip in ((low, 0), (high, 2 * rows - counts[0]))
            ],
            axis=0,
        )
        w_qkv = jnp.concatenate(
            [rows_of(qkv_full, part * width + first_row) for part in range(3)], axis=0
        )
        twice = (core == 1) & (jnp.arange(OWN) < HDIM)
        own = lax.dynamic_slice_in_dim(output_projection_weight, first_row, OWN, 1)
        (w_out,) = moves.lay([jnp.where(twice[None, :], 0, own).astype(BF16)], ())
        w_up, w_down = moves.lay([ff_piece], (), 2)
        events = []
    grad_half = moves.in_half(grad_came)
    grad_across = moves.over_z(grad_half, 1)
    normed = moves.ordered(normed_half, normed_other)
    zeros = jnp.zeros((OWN,), F32)
    joined_bias = jnp.concatenate([rows_of(q_bias, first_row), zeros, rows_of(v_bias, first_row)])
    row_scale = jnp.where(jnp.arange(3 * OWN) < OWN, 0.125, 1.0).astype(F32)
    joined = product(
        w_qkv,
        normed,
        "nn",
        416,
        lambda value, at, bias, scale: (
            (value + bias[...]).astype(BF16).astype(F32) * scale[...],
        ),
        (column(joined_bias), column(row_scale)),
        name="project_qkv",
    )
    mixed, lse = attention(seg, joined, [])
    branch = product(w_out, mixed, "nn", 400, name="project_out")
    events = [*events, branch, grad_across]

    branch, grad_half, grad_across = late([branch, grad_half, grad_across], events)
    grad_other, grad_far = moves.over_core(grad_half), moves.over_core(grad_across)
    branch_half = half_of(branch, mine).astype(F32)
    branch_half = branch_half + moves.over_core(half_of(branch, theirs)).astype(F32)
    middle = tokens + branch_half + column(out_bias)
    unit_two, scale_two = norm_parts(middle)
    norm_half = (unit_two * column(ln2_gain) + column(ln2_bias)).astype(BF16)
    events = [norm_half, grad_other, grad_far]
    grad_out = [grad_half, grad_across, grad_other, grad_far]

    (norm_half,) = late([norm_half], events)
    norm_across = moves.over_z(norm_half, 1)
    norm_other = moves.over_core(norm_half)
    if moves.square:
        ff_x, ff_y = late([ff_x, ff_y], events)
        split = ff_piece.shape[0] // 2
        ff_low, ff_high = moves.over_x(ff_y[:split]), moves.over_y(ff_x[split:])
        (norm_across,) = late([norm_across], [ff_low, ff_high])
        w_up, w_down = moves.lay((ff_piece, ff_x, ff_y), (ff_low, ff_high), 2)
    norm_far = moves.over_core(norm_across)
    normed_two = [norm_half, norm_across, norm_other, norm_far]

    activ, slope = product(
        w_up,
        normed_two,
        "nn",
        320,
        lambda value, at, bias: gelu_pair(value + bias[...]),
        (column(up_bias_own),),
        ((None, BF16), (None, BF16)),
        name="project_up",
        wait=grad_out,
    )

    def in_halves(value, at):
        half = value.shape[1] // 2
        return value[:, :half], value[:, half:]

    halves = ((length, BF16), (length, BF16))

    def through_gelu(value, at, slope_ref):
        size = value.shape[1]
        slope_here = slope_ref[:, at * size : (at + 1) * size].astype(F32)
        grad = (value * slope_here).astype(BF16)
        return grad, lane_sums(grad.astype(F32))

    grad_pre, grad_pre_sums = product(
        w_down,
        grad_out,
        "tn",
        256,
        through_gelu,
        (slope,),
        ((None, BF16), (512, F32)),
        name="back_down",
    )
    ff_cut = 896 if width == 1600 else width // 256 * 128
    norm_here, norm_there = product(
        w_up, grad_pre, "tn", 256, in_halves, (), halves, name="back_up"
    )

    norm_came = moves.over_core(norm_there)
    down_parts = moves.scatter_first([(grad_out, activ)], ff_cut, [norm_there])
    events = [norm_came, down_parts[0]]

    norm_came, norm_here = late([norm_came, norm_here], events)
    norm_last = moves.over_z(norm_here[:, half_len:] + norm_came[:, half_len:], 1)
    down_near = moves.scatter_near(down_parts, events)
    up_parts = moves.scatter_first([(grad_pre, normed_two)], ff_cut, events)
    down_here, down_there = product(
        w_down, activ, "nn", 320, in_halves, (), halves, name="project_down", wait=up_parts[:1]
    )
    events = [norm_last, *down_near[1], down_there]

    norm_last, down_there = late([norm_last, down_there], events)
    up_near = moves.scatter_near(up_parts, events)
    down_came = moves.over_core(down_there)
    grad_norm_two = norm_here[:, :half_len].astype(F32) + norm_came[:, :half_len].astype(F32)
    grad_norm_two = grad_norm_two + norm_last.astype(F32)
    grad_out_f = grad_half.astype(F32)
    grad_middle = grad_out_f + norm_back(grad_norm_two, unit_two, scale_two, column(ln2_gain))
    grad_branch_half = grad_middle.astype(BF16)
    grad_branch = moves.ordered(grad_branch_half, moves.over_core(grad_branch_half))
    grad_mixed = product(w_out, grad_branch, "tn", OWN, name="back_out")
    padded = to_tiles(OWN)
    out_parts = moves.scatter_first([(grad_branch, mixed)], 512, [grad_mixed])
    events = [*up_near[1], down_came, grad_mixed, out_parts[0]]

    down_here, down_came = late([down_here, down_came], events)
    down_last = moves.over_z(down_here[:, half_len:] + down_came[:, half_len:], 1)
    down_far = moves.scatter_far(down_near, events)
    out_near = moves.scatter_near(out_parts, events)
    grad_own = attention_back(seg, joined, mixed, grad_mixed, lse, events).reshape(3 * OWN, length)
    events = [down_last, *down_far[1], *out_near[1], grad_own]

    (grad_own,) = late([grad_own], events)
    grad_heads = moves.over_core(grad_own)
    down_part = moves.scatter_last(down_far, width)
    down_come = moves.alike(down_part)
    up_far = moves.scatter_far(up_near, events)
    norm_one = product(w_qkv, grad_own, "tn", 256, name="back_qkv", wait=[down_part])
    events = [grad_heads, *up_far[1], norm_one]

    (grad_heads,) = late([grad_heads], events)
    out_far = moves.scatter_far(out_near, events)
    if moves.square:
        grad_joined = join_heads(moves.core_ref, grad_own, grad_heads)
    else:
        low = jnp.where(core == 0, grad_own, grad_heads)
        high = jnp.where(core == 0, grad_heads, grad_own)
        grad_joined = jnp.concatenate(
            [
                piece
                for part in range(3)
                for piece in (
                    low[part * OWN : (part + 1) * OWN],
                    high[part * OWN + HDIM : (part + 1) * OWN],
                )
            ],
            axis=0,
        )
    qkv_parts = moves.scatter_first([(grad_joined, rows_of(normed, first_row))], 512, events)
    qkv_near = moves.scatter_near(qkv_parts)
    up_part = moves.scatter_last(up_far, width)
    down_come, up_part = late([down_come, up_part], [qkv_parts[0]])
    down_sum = moves.alike_sum(down_part, down_come)
    down_across = moves.over_z(down_sum, 1)
    up_come = moves.alike(late([up_part], [down_come])[0])
    out_part = moves.scatter_last(out_far, padded)
    events = qkv_near[1]

    qkv_far = moves.scatter_far(qkv_near, events)
    norm_one, out_part = late([norm_one, out_part], events)
    norm_one_came = moves.over_core(half_of(norm_one, theirs))
    out_pair = moves.total_pair(out_part)
    events = [*qkv_far[1], norm_one_came, down_across, out_pair]

    norm_one, norm_one_came, down_sum = late([norm_one, norm_one_came, down_sum], events)
    qkv_pair = moves.total_pair(moves.scatter_last(qkv_far, padded))
    grad_norm_one = half_of(norm_one, mine).astype(F32) + norm_one_came.astype(F32)
    input_half = grad_middle + norm_back(grad_norm_one, unit_one, scale_one, column(ln1_gain))
    input_came = moves.from_chips(input_half.astype(BF16), seqs)
    down_other = moves.over_core(down_sum)
    events = [qkv_pair, input_came, down_other, up_come]

    result_half = middle + down_here[:, :half_len].astype(F32)
    result_half = result_half + down_came[:, :half_len].astype(F32) + down_last.astype(F32)
    result_half = (result_half + column(down_bias)).astype(BF16)
    up_sum = moves.alike_sum(up_part, up_come)
    qkv_pair, up_sum, result_half, out_pair, down_across = late(
        [qkv_pair, up_sum, result_half, out_pair, down_across], events
    )
    qkv_full = moves.total_all(qkv_pair)
    up_across = moves.over_z(up_sum, 1)
    result = moves.from_chips(result_half, seqs)
    out_full = moves.total_all(out_pair)
    down_far_other = moves.over_core(down_across)
    events = [qkv_full, up_across, out_full, down_far_other]

    qkv_full, out_full, up_across, up_sum, down_far_other = late(
        [qkv_full, out_full, up_across, up_sum, down_far_other], [*events, result]
    )
    qkv_sum = moves.total_halves(qkv_full)
    out_sum = moves.total_halves(out_full)
    input_grad = input_came.astype(F32)

    up_bias_grad = jnp.sum(grad_pre_sums, axis=1).reshape(shard_count, 1, strip)
    up_bias_grad = up_bias_grad * (jnp.arange(4)[None, :, None] == quarter).astype(F32)
    head_sums = jnp.sum(grad_own.astype(F32), axis=1).reshape(3, OWN)
    bias_sums = lax.dynamic_update_slice(
        jnp.zeros((3, width), F32), head_sums, (jnp.int32(0), first_row)
    )
    small = moves.total_small(
        jnp.concatenate(
            [
                up_bias_grad.reshape(-1),
                jnp.sum(grad_norm_two * unit_two, axis=1),
                jnp.sum(grad_norm_two, axis=1),
                jnp.sum(grad_out_f, axis=1),
                jnp.sum(grad_branch_half.astype(F32), axis=1),
                jnp.sum(grad_norm_one * unit_one, axis=1),
                jnp.sum(grad_norm_one, axis=1),
                bias_sums[0],
                bias_sums[2],
            ]
        ).reshape(-1, 128)
    ).reshape(-1)
    up_bias_grad, rest = small[:ff], small[ff:]
    (
        ln2_gain_grad,
        ln2_bias_grad,
        down_bias_grad,
        out_bias_grad,
        ln1_gain_grad,
        ln1_bias_grad,
        q_bias_grad,
        v_bias_grad,
    ) = rest.reshape(8, width)

    quarter_ref = quarter.astype(jnp.int32)[None]
    down_total = finish_down(
        quarter_ref, [down_sum, down_other, down_across, down_far_other], shard_count
    )
    up_total = finish_up(
        quarter_ref, [up_sum, moves.over_core(up_sum), up_across, moves.over_core(up_across)]
    )

    return (
        result.transpose(2, 0, 1),
        input_grad.transpose(2, 0, 1),
        ln1_gain_grad,
        ln1_bias_grad,
        moves.sides(qkv_sum),
        q_bias_grad,
        v_bias_grad,
        moves.sides(out_sum),
        out_bias_grad,
        ln2_gain_grad,
        ln2_bias_grad,
        up_total,
        up_bias_grad,
        down_total,
        down_bias_grad,
    )


def solution(mesh):
    rows = P("shard", None)
    tokens = P("shard", "replica", None)
    in_specs = (
        tokens,
        tokens,
        P(None, "replica"),
        P(),
        P(),
        rows,
        P(),
        P(),
        rows,
        P(),
        P(),
        P(),
        rows,
        P(),
        rows,
        P(),
    )
    out_specs = (
        tokens,
        tokens,
        P(),
        P(),
        rows,
        P(),
        P(),
        rows,
        P(),
        P(),
        P(),
        rows,
        P(),
        rows,
        P(),
    )
    body = functools.partial(shards, mesh.shape["shard"], mesh.shape["replica"])
    return jax.shard_map(body, mesh=mesh, in_specs=in_specs, out_specs=out_specs, check_vma=False)
```

```python
import functools

import jax
import jax.numpy as jnp
from jax import lax
from jax.experimental import pallas as pl
from jax.experimental.pallas import tpu as pltpu
from jax.sharding import PartitionSpec as P

HEADS = 25
HDIM = 64
OWN_HEADS = HEADS // 2 + 1
FIRST_HEAD = HEADS // 2
OWN = OWN_HEADS * HDIM
BLOCK = 256
AXES = ("shard", "replica")
BF16 = jnp.bfloat16
F32 = jnp.float32


def dot(left, right, left_dim, right_dim):
    return lax.dot_general(
        left, right, (((left_dim,), (right_dim,)), ((), ())), preferred_element_type=F32
    )


COST_SCALE = 8


def cost(flops, bytes_accessed, share=1.0):
    return pl.CostEstimate(
        flops=int(flops * COST_SCALE * share),
        bytes_accessed=int(bytes_accessed * COST_SCALE * share),
        transcendentals=0,
    )


def gelu_pair(value):
    root = 0.7978845608028654
    cube = 0.044715
    square = value * value
    tanh = jnp.tanh(root * value * (1.0 + cube * square))
    half = 0.5 * (1.0 + tanh)
    slope = half + 0.5 * value * (1.0 - tanh * tanh) * root * (1.0 + 3.0 * cube * square)
    return value * half, slope


def fill_mask(seg_row, seg_col, mask, blocks):
    for q_at in range(blocks):
        for k_at in range(q_at + 1):
            keys = seg_col[pl.ds(k_at * BLOCK, BLOCK), :]
            queries = seg_row[:, pl.ds(q_at * BLOCK, BLOCK)]
            seen = keys == queries
            if k_at == q_at:
                k_place = lax.broadcasted_iota(jnp.int32, (BLOCK, BLOCK), 0)
                q_place = lax.broadcasted_iota(jnp.int32, (BLOCK, BLOCK), 1)
                seen = seen & (k_place <= q_place)
            mask[pl.ds(k_at * BLOCK, BLOCK), pl.ds(q_at * BLOCK, BLOCK)] = jnp.where(
                seen, 0.0, -1e30
            )


def forward_kernel(seg_row, seg_col, q_ref, k_ref, v_ref, *refs):
    o_ref, lse_ref, mask = refs[-3:]
    length = q_ref.shape[1]
    blocks = length // BLOCK

    @pl.when(pl.program_id(0) == 0)
    def _():
        fill_mask(seg_row, seg_col, mask, blocks)

    keys = k_ref[...].T
    for q_at in range(blocks):
        span = (q_at + 1) * BLOCK
        here = pl.ds(q_at * BLOCK, BLOCK)
        scores = dot(keys[:span], q_ref[:, here], 1, 0) + mask[:span, here]
        peak = jnp.max(scores, axis=0, keepdims=True)
        terms = jnp.exp(scores - peak)
        total = jnp.sum(terms, axis=0, keepdims=True)
        mixed = dot(v_ref[:, :span], terms.astype(BF16), 1, 0)
        o_ref[:, here] = (mixed / total).astype(BF16)
        lse_ref[0, :, here] = peak + jnp.log(total)


def backward_kernel(seg_row, seg_col, q_ref, k_ref, v_ref, o_ref, g_ref, lse_ref, *refs):
    grads, mask, acc = refs[-3:]
    length = q_ref.shape[1]
    blocks = length // BLOCK

    @pl.when(pl.program_id(0) == 0)
    def _():
        fill_mask(seg_row, seg_col, mask, blocks)

    keys = k_ref[...].T
    values = v_ref[...].T
    delta = jnp.sum(g_ref[...].astype(F32) * o_ref[...].astype(F32), axis=0, keepdims=True)
    lse = lse_ref[0]
    for k_at in range(blocks):
        low = k_at * BLOCK
        here = pl.ds(low, BLOCK)
        rest = pl.ds(low, length - low)
        scores = dot(keys[low : low + BLOCK], q_ref[:, rest], 1, 0) + mask[here, rest]
        soft = jnp.exp(scores - lse[:, low:])
        soft_grad = dot(values[low : low + BLOCK], g_ref[:, rest], 1, 0)
        score_grad = (soft * (soft_grad - delta[:, low:])).astype(BF16)
        grads[2, :, here] = dot(g_ref[:, rest], soft.astype(BF16), 1, 1).astype(BF16)
        grads[1, :, here] = dot(q_ref[:, rest], score_grad, 1, 1).astype(BF16)
        grad_q = dot(k_ref[:, here], score_grad, 1, 0)
        if k_at == 0:
            acc[...] = grad_q
        else:
            acc[:, rest] += grad_q
    grads[0] = (acc[...] * 0.125).astype(BF16)


def head_spec(first, length):
    return pl.BlockSpec((HDIM, length), lambda head: (first + head, 0))


def whole_spec(shape):
    return pl.BlockSpec(shape, lambda head: (0,) * len(shape))


def attention(seg, joined, wait):
    length = seg.shape[0]
    lse_spec = pl.BlockSpec((1, 1, length), lambda head: (head, 0, 0))
    pairs = OWN_HEADS * length * length
    return pl.pallas_call(
        forward_kernel,
        grid=(OWN_HEADS,),
        in_specs=[whole_spec((1, length)), whole_spec((length, 1))]
        + [head_spec(part * OWN_HEADS, length) for part in range(3)]
        + [pl.BlockSpec(memory_space=pl.ANY)] * len(wait),
        out_specs=[head_spec(0, length), lse_spec],
        out_shape=[
            jax.ShapeDtypeStruct((OWN, length), BF16),
            jax.ShapeDtypeStruct((OWN_HEADS, 1, length), F32),
        ],
        scratch_shapes=[pltpu.VMEM((length, length), F32)],
        compiler_params=pltpu.CompilerParams(vmem_limit_bytes=40 * 2**20),
        cost_estimate=cost(16 * pairs * HDIM, 8 * OWN * length),
        name="attention_forward",
    )(seg.reshape(1, length), seg.reshape(length, 1), joined, joined, joined, *wait)


def attention_back(seg, joined, mixed, grad, lse, wait):
    length = seg.shape[0]
    lse_spec = pl.BlockSpec((1, 1, length), lambda head: (head, 0, 0))
    pairs = OWN_HEADS * length * length
    return pl.pallas_call(
        backward_kernel,
        grid=(OWN_HEADS,),
        in_specs=[whole_spec((1, length)), whole_spec((length, 1))]
        + [head_spec(part * OWN_HEADS, length) for part in range(3)]
        + [head_spec(0, length), head_spec(0, length), lse_spec]
        + [pl.BlockSpec(memory_space=pl.ANY)] * len(wait),
        out_specs=pl.BlockSpec((3, HDIM, length), lambda head: (0, head, 0)),
        out_shape=jax.ShapeDtypeStruct((3, OWN, length), BF16),
        scratch_shapes=[pltpu.VMEM((length, length), F32), pltpu.VMEM((HDIM, length), F32)],
        compiler_params=pltpu.CompilerParams(vmem_limit_bytes=48 * 2**20),
        cost_estimate=cost(40 * pairs * HDIM, 16 * OWN * length),
        name="attention_backward",
    )(
        seg.reshape(1, length),
        seg.reshape(length, 1),
        joined,
        joined,
        joined,
        mixed,
        grad,
        lse,
        *wait,
    )


def product(left, rights, form, block, finish=None, extras=(), outs=((None, BF16),), name="product",
            wait=(), share=1.0):
    rights = rights if isinstance(rights, (list, tuple)) else [rights]
    many = len(rights)
    left_dim, right_dim = (0 if form == "tn" else 1), (1 if form == "nt" else 0)
    m, k = left.shape[1 - left_dim], left.shape[left_dim]
    size = rights[0].shape[1 - right_dim]
    n = size * many
    block = min(block, m)

    def body(left_ref, *refs):
        extra_refs = refs[many : many + len(extras)]
        out_refs = refs[many + len(extras) + len(wait) :]
        for at in range(many):
            value = dot(left_ref[...], refs[at][...], left_dim, right_dim)
            values = (value,)
            if finish is not None:
                values = finish(value, at, *extra_refs)
            for ref, part in zip(out_refs, values):
                if part is not None:
                    width = part.shape[1]
                    begin = at * width % ref.shape[1]
                    ref[:, begin : begin + width] = part.astype(ref.dtype)

    if form == "tn":
        left_spec = pl.BlockSpec((k, block), lambda i: (0, i))
    else:
        left_spec = pl.BlockSpec((block, k), lambda i: (i, 0))
    sizes = [(columns or n, kind) for columns, kind in outs]
    results = pl.pallas_call(
        body,
        grid=(pl.cdiv(m, block),),
        in_specs=[left_spec]
        + [
            pl.BlockSpec(right.shape, lambda i: (0, 0), pipeline_mode=pl.Buffered(1))
            for right in rights
        ]
        + [pl.BlockSpec((block, extra.shape[1]), lambda i: (i, 0)) for extra in extras]
        + [pl.BlockSpec(memory_space=pl.ANY)] * len(wait),
        out_specs=[pl.BlockSpec((block, columns), lambda i: (i, 0)) for columns, _ in sizes],
        out_shape=[jax.ShapeDtypeStruct((m, columns), kind) for columns, kind in sizes],
        compiler_params=pltpu.CompilerParams(vmem_limit_bytes=56 * 2**20),
        cost_estimate=cost(2 * m * n * k, 2 * (m * k + n * k + m * n), share),
        name=name,
    )(left, *rights, *extras, *wait)
    return results if len(outs) > 1 else results[0]


def lane_sums(value):
    return sum(value[:, at : at + 128] for at in range(0, value.shape[1], 128))


PARAMS = pltpu.CompilerParams(vmem_limit_bytes=56 * 2**20)


def norm_parts(rows):
    centre = rows - jnp.mean(rows, axis=0, keepdims=True)
    scale = lax.rsqrt(jnp.mean(centre * centre, axis=0, keepdims=True) + 1e-05)
    return centre * scale, scale


def norm_back(grad, unit, scale, gain):
    inner = grad * gain
    mean_inner = jnp.mean(inner, axis=0, keepdims=True)
    mean_cross = jnp.mean(inner * unit, axis=0, keepdims=True)
    return scale * (inner - mean_inner - unit * mean_cross)


def column_specs(shape, size, many):
    return [pl.BlockSpec((shape[0], size), lambda i, *_: (0, i))] * many


def fixed_specs(shape, many):
    return [pl.BlockSpec(shape, lambda i, *_: (0,) * len(shape))] * many


def norm_in(at, came, gain, bias):
    pieces = len(came)
    rows, count = came[0].shape

    def body(at_ref, *refs):
        gain_ref, bias_ref, tokens_ref, norm_ref = refs[pieces:]
        which = lax.rem(at_ref[0] - pl.program_id(0) + pieces, pieces)
        for piece in range(pieces):

            @pl.when(which == piece)
            def _(piece=piece):
                tokens_ref[...] = refs[piece][...]

        unit, _ = norm_parts(tokens_ref[...].astype(F32))
        norm_ref[...] = (unit * gain_ref[...] + bias_ref[...]).astype(BF16)

    return pl.pallas_call(
        body,
        grid_spec=pltpu.PrefetchScalarGridSpec(
            num_scalar_prefetch=1,
            grid=(pieces,),
            in_specs=fixed_specs((rows, count), pieces) + fixed_specs((rows, 1), 2),
            out_specs=column_specs((rows, pieces * count), count, 2),
        ),
        out_shape=[jax.ShapeDtypeStruct((rows, pieces * count), BF16)] * 2,
        compiler_params=PARAMS,
        cost_estimate=cost(0, 40 * rows * pieces * count),
        name="norm_in",
    )(at, *came, gain, bias)


def norm_mid(tokens, mine, came, shift, gain, bias):
    rows, columns = tokens.shape
    size = columns // 2

    def body(tokens_ref, mine_ref, came_ref, shift_ref, gain_ref, bias_ref, middle_ref, norm_ref):
        middle = mine_ref[...].astype(F32) + came_ref[...].astype(F32)
        middle = tokens_ref[...].astype(F32) + middle + shift_ref[...]
        middle_ref[...] = middle
        unit, _ = norm_parts(middle)
        norm_ref[...] = (unit * gain_ref[...] + bias_ref[...]).astype(BF16)

    return pl.pallas_call(
        body,
        grid=(2,),
        in_specs=column_specs((rows, columns), size, 3) + fixed_specs((rows, 1), 3),
        out_specs=column_specs((rows, columns), size, 2),
        out_shape=[
            jax.ShapeDtypeStruct((rows, columns), F32),
            jax.ShapeDtypeStruct((rows, columns), BF16),
        ],
        compiler_params=PARAMS,
        cost_estimate=cost(0, 40 * rows * columns),
        name="norm_mid",
    )(tokens, mine, came, shift, gain, bias)


def norm_mid_back(parts, middle, grad, gain, wait):
    rows, columns = middle.shape
    size = columns // 2
    many = len(parts)

    def body(*refs):
        middle_ref, grad_ref, gain_ref = refs[many : many + 3]
        out_ref, low_ref, sums_ref = refs[-3:]
        norm_grad = sum(ref[...].astype(F32) for ref in refs[:many])
        unit, scale = norm_parts(middle_ref[...])
        through = grad_ref[...].astype(F32)
        value = through + norm_back(norm_grad, unit, scale, gain_ref[...])
        out_ref[...] = value
        low_ref[...] = value.astype(BF16)
        sums = (norm_grad * unit, norm_grad, through, value.astype(BF16).astype(F32))
        for at, rows_of_sum in enumerate(sums):
            here = lane_sums(rows_of_sum)

            @pl.when(pl.program_id(0) == 0)
            def _(at=at, here=here):
                sums_ref[at] = here

            @pl.when(pl.program_id(0) > 0)
            def _(at=at, here=here):
                sums_ref[at] += here

    return pl.pallas_call(
        body,
        grid=(2,),
        in_specs=column_specs((rows, columns), size, many + 2)
        + fixed_specs((rows, 1), 1)
        + [pl.BlockSpec(memory_space=pl.ANY)] * len(wait),
        out_specs=column_specs((rows, columns), size, 2) + fixed_specs((4, rows, 128), 1),
        out_shape=[
            jax.ShapeDtypeStruct((rows, columns), F32),
            jax.ShapeDtypeStruct((rows, columns), BF16),
            jax.ShapeDtypeStruct((4, rows, 128), F32),
        ],
        compiler_params=PARAMS,
        cost_estimate=cost(0, 60 * rows * columns),
        name="norm_mid_back",
    )(*parts, middle, grad, gain, *wait)


def norm_in_back(parts, tokens, grad, gain):
    rows, columns = tokens.shape
    size = columns // 2
    many = len(parts)

    def body(*refs):
        tokens_ref, grad_ref, gain_ref, out_ref, sums_ref = refs[many:]
        norm_grad = sum(ref[...].astype(F32) for ref in refs[:many])
        unit, scale = norm_parts(tokens_ref[...].astype(F32))
        value = grad_ref[...] + norm_back(norm_grad, unit, scale, gain_ref[...])
        out_ref[...] = value.astype(BF16)
        for at, rows_of_sum in enumerate((norm_grad * unit, norm_grad)):
            here = lane_sums(rows_of_sum)

            @pl.when(pl.program_id(0) == 0)
            def _(at=at, here=here):
                sums_ref[at] = here

            @pl.when(pl.program_id(0) > 0)
            def _(at=at, here=here):
                sums_ref[at] += here

    return pl.pallas_call(
        body,
        grid=(2,),
        in_specs=column_specs((rows, columns), size, many + 2) + fixed_specs((rows, 1), 1),
        out_specs=column_specs((rows, columns), size, 1) + fixed_specs((2, rows, 128), 1),
        out_shape=[
            jax.ShapeDtypeStruct((rows, columns), BF16),
            jax.ShapeDtypeStruct((2, rows, 128), F32),
        ],
        compiler_params=PARAMS,
        cost_estimate=cost(0, 60 * rows * columns),
        name="norm_in_back",
    )(*parts, tokens, grad, gain)


def results(at, pieces, middle, parts, shift, input_half):
    rows, columns = middle.shape
    size = columns // pieces
    many = len(parts)

    def body(at_ref, middle_ref, *refs):
        shift_ref, input_ref = refs[many : many + 2]
        outs = refs[many + 2 :]
        value = middle_ref[...] + shift_ref[...]
        for ref in refs[:many]:
            value = value + ref[...].astype(F32)
        value = value.astype(BF16)
        which = lax.rem(at_ref[0] - pl.program_id(0) + pieces, pieces)
        for piece, out in enumerate(outs):

            @pl.when(which == piece)
            def _(out=out):
                out[:rows] = value
                out[rows:] = input_ref[...]

    block = column_specs((rows, columns), size, 1)
    return pl.pallas_call(
        body,
        grid_spec=pltpu.PrefetchScalarGridSpec(
            num_scalar_prefetch=1,
            grid=(pieces,),
            in_specs=block * (1 + many) + fixed_specs((rows, 1), 1) + block,
            out_specs=fixed_specs((2 * rows, size), pieces),
        ),
        out_shape=[jax.ShapeDtypeStruct((2 * rows, size), BF16)] * pieces,
        compiler_params=PARAMS,
        cost_estimate=cost(0, 40 * rows * columns),
        name="results",
    )(at, middle, *parts, shift, input_half)


def lay(places, near, far, parts):
    count, columns = near[0].shape
    size = count // parts
    kind = near[0].dtype

    def body(places_ref, *refs):
        step = pl.program_id(0)
        outs = refs[5:]
        for at in range(3):

            @pl.when(step == at)
            def _(at=at):
                for index, out in enumerate(outs):
                    out[...] = refs[at][index * size : (index + 1) * size]

        @pl.when(step == 3)
        def _():
            start = 0
            for ref in refs[3:5]:
                rows = ref.shape[0]
                for index, out in enumerate(outs):
                    low, high = max(start, index * size), min(start + rows, (index + 1) * size)
                    if low < high:
                        out[low - index * size : high - index * size] = ref[
                            low - start : high - start
                        ]
                start += rows

    pieces = list(near) + list(far)
    return pl.pallas_call(
        body,
        grid_spec=pltpu.PrefetchScalarGridSpec(
            num_scalar_prefetch=1,
            grid=(4,),
            in_specs=[
                pl.BlockSpec(piece.shape, lambda i, p: (0, 0), pipeline_mode=pl.Buffered(1))
                for piece in pieces
            ],
            out_specs=[pl.BlockSpec((size, columns), lambda i, p: (p[i], 0))] * parts,
        ),
        out_shape=[jax.ShapeDtypeStruct((4 * size, columns), kind)] * parts,
        compiler_params=pltpu.CompilerParams(vmem_limit_bytes=56 * 2**20),
        cost_estimate=cost(0, 16 * count * columns),
        name="lay",
    )(places, *pieces)


def lay_heads(core, places, mine, others, counts, taken, wait):
    width = mine[0].shape[1]
    split = mine[3].shape[0]
    cut = FIRST_HEAD * HDIM

    def body(core_ref, places_ref, *refs):
        heads_ref, out_ref, block, out_block = refs[-4:]
        step = pl.program_id(0)

        def copy(halves, at, begin, end, target, row):
            if at < 3:
                target[row : row + end - begin] = halves[at][begin:end]
                return
            if begin < split:
                middle = min(end, split)
                target[row : row + middle - begin] = halves[3][begin:middle]
            if end > split:
                middle = max(begin, split)
                target[row + middle - begin : row + end - begin] = halves[4][
                    middle - split : end - split
                ]

        for which in range(2):

            @pl.when(core_ref[0] == which)
            def _(which=which):
                low, high = (refs[:5], refs[5:10]) if which == 0 else (refs[5:10], refs[:5])
                for at in range(4):

                    @pl.when(step == at)
                    def _(at=at):
                        begin = 0
                        for target, rows, count in zip((block, out_block), taken, counts):
                            copy(low, at, begin, begin + rows, target, 0)
                            over = 2 * rows - count
                            copy(high, at, begin + over, begin + rows, target, rows)
                            begin += rows

                out_ref[...] = out_block[:, which * cut : which * cut + OWN]
                if which == 1:
                    out_ref[:, :HDIM] = jnp.zeros((counts[1], HDIM), BF16)
                for shard in range(4):

                    @pl.when(places_ref[step] == shard)
                    def _(shard=shard):
                        for part in range(3):
                            begin = part * width + which * cut
                            first = max(begin, shard * counts[0])
                            last = min(begin + OWN, (shard + 1) * counts[0])
                            if first < last:
                                heads_ref[
                                    part * OWN + first - begin : part * OWN + last - begin
                                ] = block[first - shard * counts[0] : last - shard * counts[0]]

    pieces = list(mine) + list(others)
    return pl.pallas_call(
        body,
        grid_spec=pltpu.PrefetchScalarGridSpec(
            num_scalar_prefetch=2,
            grid=(4,),
            in_specs=[
                pl.BlockSpec(piece.shape, lambda i, c, p: (0, 0), pipeline_mode=pl.Buffered(1))
                for piece in pieces
            ]
            + [pl.BlockSpec(memory_space=pl.ANY)] * len(wait),
            out_specs=[
                pl.BlockSpec(
                    (3 * OWN, width), lambda i, c, p: (0, 0), pipeline_mode=pl.Buffered(1)
                ),
                pl.BlockSpec((counts[1], OWN), lambda i, c, p: (p[i], 0)),
            ],
            scratch_shapes=[pltpu.VMEM((count, width), BF16) for count in counts],
        ),
        out_shape=[
            jax.ShapeDtypeStruct((3 * OWN, width), BF16),
            jax.ShapeDtypeStruct((4 * counts[1], OWN), BF16),
        ],
        compiler_params=pltpu.CompilerParams(vmem_limit_bytes=56 * 2**20),
        cost_estimate=cost(0, 16 * counts[0] * width),
        name="lay_heads",
    )(core, places, *pieces, *wait)


def join_heads(core, own, other, count, taken, wait):
    length = own.shape[1]
    rows = 2 * OWN - HDIM

    def body(core_ref, own_ref, other_ref, *refs):
        out = refs[-1]
        step = pl.program_id(0)
        for which in range(2):
            for shard in range(4):

                @pl.when((core_ref[0] == which) & (step == shard))
                def _(which=which, shard=shard):
                    low, high = (own_ref, other_ref) if which == 0 else (other_ref, own_ref)
                    begin = shard * count + which * (count - taken)
                    at = begin
                    while at < begin + taken:
                        part, row = at // rows, at % rows
                        source, skip, last = (
                            (low, 0, OWN) if row < OWN else (high, OWN - HDIM, rows)
                        )
                        end = min(begin + taken, part * rows + last)
                        first = part * OWN + row - skip
                        out[at - begin : end - begin] = source[first : first + end - at]
                        at = end

    whole = pl.BlockSpec(own.shape, lambda i, c: (0, 0), pipeline_mode=pl.Buffered(1))
    return pl.pallas_call(
        body,
        grid_spec=pltpu.PrefetchScalarGridSpec(
            num_scalar_prefetch=1,
            grid=(4,),
            in_specs=[whole, whole] + [pl.BlockSpec(memory_space=pl.ANY)] * len(wait),
            out_specs=pl.BlockSpec((taken, length), lambda i, c: (i, 0)),
        ),
        out_shape=jax.ShapeDtypeStruct((4 * taken, length), BF16),
        compiler_params=pltpu.CompilerParams(vmem_limit_bytes=56 * 2**20),
        cost_estimate=cost(0, 12 * rows * length),
        name="join_heads",
    )(core, own, other, *wait)


def product_parts(order, pairs, cut, wait):
    many = len(pairs)
    lefts = [side_of(left) for left, _ in pairs]
    rights = [side_of(right) for _, right in pairs]
    count = lefts[0][0].shape[0] // 4
    depth = sum(piece.shape[1] for piece in lefts[0])
    columns = rights[0][0].shape[0]
    rest = columns - cut
    filled = to_tiles(rest)
    starts = [0]
    for sides in lefts + rights:
        starts.append(starts[-1] + len(sides))

    def body(order_ref, *refs):
        send_x, send_y, keep_x, keep_y = refs[starts[-1] + len(wait) :]
        step = pl.program_id(0)
        targets = ((send_x, send_y), (send_x, keep_y), (keep_x, send_y), (keep_x, keep_y))
        for pair in range(many):

            @pl.when(step // 4 == pair)
            def _(pair=pair):
                left = refs[starts[pair] : starts[pair + 1]]
                right = refs[starts[many + pair] : starts[many + pair + 1]]
                value = side_product(left, right).astype(BF16)
                for at, (along_x, along_y) in enumerate(targets):

                    @pl.when(step % 4 == at)
                    def _(along_x=along_x, along_y=along_y):
                        along_x[...] = value[:, :cut]
                        along_y[:, :rest] = value[:, cut:]
                        if filled > rest:
                            along_y[:, rest:] = jnp.zeros((count, filled - rest), BF16)

    def left_spec(pair, piece):
        return pl.BlockSpec(
            (count, piece.shape[1]), lambda i, o: (o[jnp.clip(i - 4 * pair, 0, 3)], 0)
        )

    def out_spec(size, second):
        return pl.BlockSpec(
            (count, size), lambda i, o: (jnp.where(i % 4 >= second, many, 0) + i // 4, 0)
        )

    return pl.pallas_call(
        body,
        grid_spec=pltpu.PrefetchScalarGridSpec(
            num_scalar_prefetch=1,
            grid=(4 * many,),
            in_specs=[left_spec(pair, piece) for pair in range(many) for piece in lefts[pair]]
            + [
                pl.BlockSpec(piece.shape, lambda i, o: (0, 0), pipeline_mode=pl.Buffered(1))
                for right in rights
                for piece in right
            ]
            + [pl.BlockSpec(memory_space=pl.ANY)] * len(wait),
            out_specs=[
                out_spec(cut, 1),
                out_spec(filled, 2),
                out_spec(cut, 3),
                out_spec(filled, 3),
            ],
        ),
        out_shape=[
            jax.ShapeDtypeStruct((2 * many * count, size), BF16)
            for size in (cut, filled, cut, filled)
        ],
        compiler_params=pltpu.CompilerParams(vmem_limit_bytes=56 * 2**20),
        cost_estimate=cost(8 * many * count * depth * columns, 8 * many * count * (depth + columns)),
        name="product_parts",
    )(order, *[piece for sides in lefts + rights for piece in sides], *wait)


def side_of(side):
    return list(side) if isinstance(side, (list, tuple)) else [side]


def side_product(left, right):
    total = None
    size = min(piece.shape[1] for piece in (*left, *right))
    depth = sum(piece.shape[1] for piece in left)

    def chunk(pieces, begin):
        width = pieces[0].shape[1]
        return pieces[begin // width][:, begin % width : begin % width + size]

    for begin in range(0, depth, size):
        value = dot(chunk(left, begin), chunk(right, begin), 1, 1)
        total = value if total is None else total + value
    return total


def to_tiles(count):
    return -(-count // 128) * 128


def fold(keep_x, came_x, last_x, keep_y, came_y, last_y, columns):
    rows, cut = last_x.shape
    filled = last_y.shape[1]
    rest = columns - cut
    block = 400 if rows % 400 == 0 else rows // 2
    steps = rows // block

    def body(*refs):
        out = refs[6]
        for first, begin, size in ((0, 0, cut), (3, cut, rest)):
            value = refs[first][:, :size].astype(F32) + refs[first + 1][:, :size].astype(F32)
            value = value + refs[first + 2][:, :size].astype(F32)
            out[:, begin : begin + size] = value.astype(BF16)

    def specs(size):
        second = pl.BlockSpec((block, size), lambda i: (steps + i, 0))
        return [second, second, pl.BlockSpec((block, size), lambda i: (i, 0))]

    return pl.pallas_call(
        body,
        grid=(steps,),
        in_specs=specs(cut) + specs(filled),
        out_specs=pl.BlockSpec((block, columns), lambda i: (i, 0)),
        out_shape=jax.ShapeDtypeStruct((rows, columns), BF16),
        compiler_params=pltpu.CompilerParams(vmem_limit_bytes=56 * 2**20),
        cost_estimate=cost(0, 8 * rows * columns, 0.01),
        name="fold",
    )(keep_x, came_x, last_x, keep_y, came_y, last_y)


def finish_up(quarter, parts):
    rows, width = parts[0].shape

    def body(quarter_ref, *refs):
        for at in range(4):

            @pl.when(pl.program_id(0) == at)
            def _(at=at):
                refs[4][...] = refs[at][...].astype(F32)

    return pl.pallas_call(
        body,
        grid_spec=pltpu.PrefetchScalarGridSpec(
            num_scalar_prefetch=1,
            grid=(4,),
            in_specs=[
                pl.BlockSpec((rows, width), lambda i, q: (0, 0), pipeline_mode=pl.Buffered(1))
            ]
            * 4,
            out_specs=pl.BlockSpec((rows, width), lambda i, q: (q[0] ^ i, 0)),
        ),
        out_shape=jax.ShapeDtypeStruct((4 * rows, width), F32),
        compiler_params=pltpu.CompilerParams(vmem_limit_bytes=56 * 2**20),
        cost_estimate=cost(0, 24 * rows * width),
        name="finish_up",
    )(quarter, *parts)


def finish_down(quarter, parts, shard_count):
    rows, width = parts[0].shape
    strip = width // shard_count
    block = 80 if rows % 80 == 0 else 40
    steps = rows // block

    def body(quarter_ref, *refs):
        for which in range(4):

            @pl.when(quarter_ref[0] == which)
            def _(which=which):
                for shard in range(shard_count):
                    for at in range(4):
                        begin = (4 * shard + at) * strip
                        refs[4][:, begin : begin + strip] = refs[which ^ at][
                            :, shard * strip : (shard + 1) * strip
                        ].astype(F32)

    return pl.pallas_call(
        body,
        grid_spec=pltpu.PrefetchScalarGridSpec(
            num_scalar_prefetch=1,
            grid=(steps,),
            in_specs=[pl.BlockSpec((block, width), lambda i, q: (i, 0))] * 4,
            out_specs=pl.BlockSpec((block, 4 * width), lambda i, q: (i, 0)),
        ),
        out_shape=jax.ShapeDtypeStruct((rows, 4 * width), F32),
        compiler_params=pltpu.CompilerParams(vmem_limit_bytes=56 * 2**20),
        cost_estimate=cost(0, 24 * rows * width),
        name="finish_down",
    )(quarter, *parts)


def finish_sides(core, even, parts):
    rows, width = parts[0].shape
    cut = FIRST_HEAD * HDIM

    def body(core_ref, even_ref, *refs):
        for which in range(2):
            for at in range(2):

                @pl.when((core_ref[0] == which) & (pl.program_id(0) == at))
                def _(which=which, at=at):
                    own, other = refs[at], refs[2 + at]
                    low, high = (own, other) if which == 0 else (other, own)
                    refs[4][:, :cut] = low[:, :cut].astype(F32)
                    refs[4][:, cut:] = high[:, :OWN].astype(F32)

    return pl.pallas_call(
        body,
        grid_spec=pltpu.PrefetchScalarGridSpec(
            num_scalar_prefetch=2,
            grid=(2,),
            in_specs=[
                pl.BlockSpec((rows, width), lambda i, c, e: (0, 0), pipeline_mode=pl.Buffered(1))
            ]
            * 4,
            out_specs=pl.BlockSpec((rows, cut + OWN), lambda i, c, e: (e[0] ^ i, 0)),
        ),
        out_shape=jax.ShapeDtypeStruct((2 * rows, cut + OWN), F32),
        compiler_params=pltpu.CompilerParams(vmem_limit_bytes=56 * 2**20),
        cost_estimate=cost(0, 16 * rows * width),
        name="finish_sides",
    )(core, even, *parts)


def finish_rows(core, even, parts, count):
    rows, width = parts[0].shape
    over = 4 * rows - count

    def body(core_ref, even_ref, *refs):
        out = refs[4]
        for which in range(2):
            for parity in range(2):

                @pl.when((core_ref[0] == which) & (even_ref[0] == parity))
                def _(which=which, parity=parity):
                    mine = [refs[parity], refs[1 - parity]]
                    others = [refs[2 + parity], refs[3 - parity]]
                    low, high = (mine, others) if which == 0 else (others, mine)
                    for at in range(2):

                        @pl.when(pl.program_id(0) == at)
                        def _(at=at):
                            out[...] = low[at][...].astype(F32)

                    @pl.when(pl.program_id(0) == 2)
                    def _():
                        out[: rows - over] = high[0][over:].astype(F32)
                        out[rows - over :] = high[1][:over].astype(F32)

                    @pl.when(pl.program_id(0) == 3)
                    def _():
                        out[: rows - over] = high[1][over:].astype(F32)

    return pl.pallas_call(
        body,
        grid_spec=pltpu.PrefetchScalarGridSpec(
            num_scalar_prefetch=2,
            grid=(4,),
            in_specs=[
                pl.BlockSpec((rows, width), lambda i, c, e: (0, 0), pipeline_mode=pl.Buffered(1))
            ]
            * 4,
            out_specs=pl.BlockSpec((rows, width), lambda i, c, e: (i, 0)),
        ),
        out_shape=jax.ShapeDtypeStruct((count, width), F32),
        compiler_params=pltpu.CompilerParams(vmem_limit_bytes=56 * 2**20),
        cost_estimate=cost(0, 24 * rows * width),
        name="finish_rows",
    )(core, even, *parts)


def to_sixteen(count):
    return -(-count // 16) * 16


def late(arrays, events):
    arrays = list(arrays)
    events = [event for event in events if event is not None]
    if not events:
        return arrays
    return lax.optimization_barrier((*arrays, *events))[: len(arrays)]


class Moves:
    def __init__(self, shard_count, replica_count):
        self.shard_count = shard_count
        self.replica_count = replica_count
        self.shard = lax.axis_index("shard")
        replica = lax.axis_index("replica")
        self.core = replica % 2
        self.column = replica // 2
        self.square = shard_count == 4 and replica_count == 8
        self.core_ref = self.core.astype(jnp.int32)[None]
        me = self.shard
        self.places = jnp.stack([me, me ^ 1, me ^ 2, me ^ 3]).astype(jnp.int32)
        self.order = jnp.stack([me ^ 3, me ^ 1, me ^ 2, me]).astype(jnp.int32)

    def move(self, array, route):
        pairs, stays = [], []
        for shard in range(self.shard_count):
            for column in range(self.replica_count // 2):
                for core in range(2):
                    target = route(shard, column, core)
                    if target == (shard, column, core):
                        stays.append((shard, core))
                    elif target is not None:
                        to_shard, to_column, to_core = target
                        pairs.append(
                            (
                                shard * self.replica_count + 2 * column + core,
                                to_shard * self.replica_count + 2 * to_column + to_core,
                            )
                        )
        came = lax.ppermute(array, AXES, pairs)
        if not stays:
            return came
        table = [(s, c) in stays for s in range(self.shard_count) for c in range(2)]
        return jnp.where(jnp.asarray(table)[2 * self.shard + self.core], array, came)

    def over_x(self, array):
        return self.move(array, lambda s, z, c: (s ^ 1, z, c))

    def over_y(self, array):
        return self.move(array, lambda s, z, c: (s ^ 2, z, c))

    def over_z(self, array, step):
        return self.move(array, lambda s, z, c: (s, z ^ step, c))

    def over_core(self, array):
        return self.move(array, lambda s, z, c: (s, z, 1 - c))

    def lay(self, near, far, parts=1):
        if self.square:
            return lay(self.places, near, far, parts)
        size = near[0].shape[0] // parts
        return [
            lax.all_gather(near[0][at * size : (at + 1) * size], "shard", axis=0, tiled=True)
            for at in range(parts)
        ]

    def scatter_first(self, pairs, cut, wait=()):
        if not self.square:
            return [
                product(
                    jnp.concatenate(side_of(left), axis=1),
                    jnp.concatenate(side_of(right), axis=1),
                    "nt",
                    400,
                )
                for left, right in pairs
            ]
        return product_parts(self.order, pairs, cut, wait)

    def scatter_near(self, parts, wait=()):
        if not self.square:
            return parts, []
        send_x, send_y = late(parts[:2], wait)
        return parts, [self.over_x(send_x), self.over_y(send_y)]

    def scatter_far(self, near, wait=()):
        parts, came = near
        if not self.square:
            return near, []
        keep_x, keep_y = parts[2:]
        half = keep_x.shape[0] // 2
        came_x, came_y = late(came, wait)
        last_x = self.over_y(keep_x[:half] + came_x[:half])
        last_y = self.over_x(keep_y[:half] + came_y[:half])
        return near, [last_x, last_y]

    def scatter_last(self, far, columns):
        (parts, came), last = far
        if not self.square:
            sums = [
                lax.psum_scatter(part, "shard", scatter_dimension=0, tiled=True) for part in parts
            ]
            return jnp.concatenate(sums, axis=0)
        return fold(parts[2], came[0], last[0], parts[3], came[1], last[1], columns)

    def total_pair(self, array):
        if not self.square:
            return array
        rows = array.shape[0] // 2
        even = self.column % 2
        keep = lax.dynamic_slice_in_dim(array, even * rows, rows, 0)
        send = lax.dynamic_slice_in_dim(array, (1 - even) * rows, rows, 0)
        return keep + self.over_z(send, 1)

    def total_all(self, pair):
        if not self.square:
            groups = [
                [2 * column + core for column in range(self.replica_count // 2)]
                for core in range(2)
            ]
            return lax.psum(pair, "replica", axis_index_groups=groups)
        return pair + self.over_z(pair, 2)

    def total_halves(self, full):
        return (full, self.over_z(full, 1)) if self.square else (full,)

    def four(self, sums):
        return list(sums) + [self.over_core(half) for half in sums]

    def sides(self, parts):
        even = (self.column % 2).astype(jnp.int32)[None]
        if self.square:
            return finish_sides(self.core_ref, even, parts)
        first = self.core == 0
        low, high = jnp.where(first, *parts), jnp.where(first, *parts[::-1])
        return jnp.concatenate([low[:, : FIRST_HEAD * HDIM], high[:, :OWN]], axis=1).astype(F32)

    def rows(self, parts, count):
        if self.square:
            even = (self.column % 2).astype(jnp.int32)[None]
            return finish_rows(self.core_ref, even, parts, count)
        first = self.core == 0
        low, high = jnp.where(first, *parts), jnp.where(first, *parts[::-1])
        return jnp.concatenate([low, high[2 * low.shape[0] - count :]], axis=0).astype(F32)

    def alike(self, array):
        return self.over_z(array, 2) if self.square else self.total_alike(array)

    def alike_sum(self, array, came):
        came = jnp.concatenate(came, axis=0)
        return array + came if self.square else came

    def total_alike(self, array):
        groups = [
            [2 * column + core for column in range(even, self.replica_count // 2, 2)]
            for even in range(2)
            for core in range(2)
        ]
        return lax.psum(array, "replica", axis_index_groups=groups)

    def small_cores(self, array):
        return array + self.over_core(array) if self.square else lax.psum(array, AXES)

    def small_square(self, array):
        if not self.square:
            return array
        array = array + self.over_x(array)
        return array + self.over_y(array)

    def small_columns(self, array, step):
        return array + self.over_z(array, step) if self.square else array

    def owners(self, step, seqs):
        return lambda s, z, c: (seqs * c + (s + step) % seqs, z, s // seqs)

    def to_chips(self, local):
        seqs, _, count = local.shape
        came = []
        for step in range(seqs):
            at = (self.shard + step) % seqs
            sent = lax.dynamic_index_in_dim(local, at, 0, keepdims=False)
            came.append(self.move(sent, self.owners(step, seqs)))
        return came

    def in_half(self, came):
        seqs = len(came)
        count = came[0].shape[1]
        at = self.shard % seqs
        if seqs == 2:
            first = at == 0
            return jnp.concatenate(
                [jnp.where(first, came[0], came[1]), jnp.where(first, came[1], came[0])], axis=1
            )
        ring = jnp.concatenate((came[::-1] * 2)[: 2 * seqs - 1], axis=1)
        return lax.dynamic_slice_in_dim(ring, (seqs - 1 - at) * count, seqs * count, 1)

    def from_chips(self, pieces):
        seqs = len(pieces)
        at = self.shard % seqs
        outs = []
        for step in range(seqs):
            route = self.owners(step, seqs)
            back = {}
            for s in range(self.shard_count):
                for z in range(self.replica_count // 2):
                    for c in range(2):
                        back[route(s, z, c)] = (s, z, c)
            outs.append(self.move(pieces[step], lambda s, z, c: back[(s, z, c)]))
        if seqs == 2:
            first = at == 0
            return jnp.stack(
                [jnp.where(first, outs[0], outs[1]), jnp.where(first, outs[1], outs[0])]
            )
        stacked = jnp.stack(outs)
        doubled = jnp.concatenate([stacked, stacked[: seqs - 1]], axis=0)
        return lax.dynamic_slice_in_dim(doubled, (seqs - at) % seqs, seqs, 0)

    def ordered(self, half, other):
        first = self.core == 0
        return jnp.concatenate(
            [jnp.where(first, half, other), jnp.where(first, other, half)], axis=1
        )


def shards(
    shard_count,
    replica_count,
    hidden_in,
    out_grad,
    segments,
    ln1_gain,
    ln1_bias,
    qkv_weight,
    q_bias,
    v_bias,
    output_projection_weight,
    out_bias,
    ln2_gain,
    ln2_bias,
    up_weight,
    up_bias,
    down_weight,
    down_bias,
):
    moves = Moves(shard_count, replica_count)
    core = moves.core
    quarter = 2 * (moves.column % 2) + core
    seqs = hidden_in.shape[1]
    width = hidden_in.shape[2]
    length = segments.shape[0]
    half_len = length // 2
    ff = up_bias.shape[0]
    strip = ff // shard_count // 4
    first_row = core * FIRST_HEAD * HDIM
    rows_of = functools.partial(lax.dynamic_slice_in_dim, slice_size=OWN, axis=0)

    def column(vector):
        return vector[:, None]


    counts = (qkv_weight.shape[0], output_projection_weight.shape[0])
    taken = tuple(to_sixteen(count // 2) for count in counts)
    mine_of = [
        lax.dynamic_slice_in_dim(weight, core * (count - rows), rows, 0)
        for weight, count, rows in zip((qkv_weight, output_projection_weight), counts, taken)
    ]
    ff_piece = jnp.concatenate(
        [
            lax.dynamic_slice_in_dim(up_weight, quarter * strip, strip, 0),
            jnp.concatenate(
                [
                    lax.dynamic_slice_in_dim(down_weight, (4 * shard + quarter) * strip, strip, 1)
                    for shard in range(shard_count)
                ],
                axis=1,
            ),
        ],
        axis=0,
    )
    up_bias_own = lax.dynamic_index_in_dim(
        up_bias.reshape(shard_count, 4, strip), quarter, 1, keepdims=False
    ).reshape(-1)
    tokens_came = moves.to_chips(hidden_in.transpose(1, 2, 0))
    if moves.square:
        heads_piece = jnp.concatenate(mine_of, axis=0)
        heads_x, heads_y = moves.over_x(heads_piece), moves.over_y(heads_piece)
        other_own = moves.over_core(heads_piece)
        events = [heads_x, heads_y, other_own, *tokens_came, ff_piece]

        heads_x, heads_y, segments_sent, *tokens_came = late(
            [heads_x, heads_y, segments, *tokens_came], events
        )
        split = to_sixteen(heads_piece.shape[0] // 2)
        heads_low = moves.over_x(heads_y[:split])
        heads_high = moves.over_y(heads_x[split:])
        other_x, other_y = moves.over_core(heads_x), moves.over_core(heads_y)
        segments_other = moves.over_core(segments_sent)
        events = [heads_low, heads_high, other_x, other_y, segments_other]
    else:
        segments_other = moves.over_core(segments)
        events = []
    at = (moves.shard % seqs).astype(jnp.int32)[None]
    tokens, normed_half = norm_in(at, tokens_came, column(ln1_gain), column(ln1_bias))
    events = [*events, normed_half]
    home = moves.shard // seqs
    seg = jnp.where(home == core, segments, segments_other)
    seg = lax.dynamic_index_in_dim(seg, moves.shard % seqs, 1, keepdims=False)

    out_grad, normed_half = late([out_grad, normed_half], events)
    if moves.square:
        heads_low, heads_high = late([heads_low, heads_high], events)
        other_low, other_high = moves.over_core(heads_low), moves.over_core(heads_high)
        events = [other_low, other_high]
    else:
        events = []
    normed_other = moves.over_core(normed_half)
    grad_came = moves.to_chips(out_grad.transpose(1, 2, 0))
    normed = moves.ordered(normed_half, normed_other)
    events = [*events, normed, *grad_came]

    ff_piece, normed, *grad_came = late([ff_piece, normed, *grad_came], events)
    if moves.square:
        ff_x, ff_y = moves.over_x(ff_piece), moves.over_y(ff_piece)
        w_qkv, w_out = lay_heads(
            moves.core_ref,
            moves.places,
            [heads_piece, heads_x, heads_y, heads_low, heads_high],
            [other_own, other_x, other_y, other_low, other_high],
            counts,
            taken,
            events,
        )
        events = [ff_x, ff_y]
    else:
        (qkv_half,) = moves.lay([mine_of[0]], ())
        qkv_other = moves.over_core(qkv_half)
        low = jnp.where(core == 0, qkv_half, qkv_other)
        high = jnp.where(core == 0, qkv_other, qkv_half)
        rows = taken[0]
        qkv_full = jnp.concatenate(
            [
                block[shard * rows + skip : (shard + 1) * rows]
                for shard in range(shard_count)
                for block, skip in ((low, 0), (high, 2 * rows - counts[0]))
            ],
            axis=0,
        )
        w_qkv = jnp.concatenate(
            [rows_of(qkv_full, part * width + first_row) for part in range(3)], axis=0
        )
        twice = (core == 1) & (jnp.arange(OWN) < HDIM)
        own = lax.dynamic_slice_in_dim(output_projection_weight, first_row, OWN, 1)
        (w_out,) = moves.lay([jnp.where(twice[None, :], 0, own).astype(BF16)], ())
        w_up, w_down = moves.lay([ff_piece], (), 2)
        events = []
    grad_half = moves.in_half(late(grad_came, [w_qkv]))
    grad_across = moves.over_z(grad_half, 1)
    zeros = jnp.zeros((OWN,), F32)
    joined_bias = jnp.concatenate([rows_of(q_bias, first_row), zeros, rows_of(v_bias, first_row)])
    row_scale = jnp.where(jnp.arange(3 * OWN) < OWN, 0.125, 1.0).astype(F32)
    joined = product(
        w_qkv,
        normed,
        "nn",
        416,
        lambda value, at, bias, scale: (
            (value + bias[...]).astype(BF16).astype(F32) * scale[...],
        ),
        (column(joined_bias), column(row_scale)),
        name="project_qkv",
    )
    mixed, lse = attention(seg, joined, [])
    side = jnp.broadcast_to(core.astype(F32), (width, 1))
    halves = ((half_len, BF16), (half_len, BF16))

    def by_side(value, at, side_ref):
        first, second = value[:, :half_len], value[:, half_len:]
        mine = side_ref[...] == 0
        return jnp.where(mine, first, second), jnp.where(mine, second, first)

    branch, branch_sent = product(
        w_out, mixed, "nn", 400, by_side, (side,), halves, name="project_out"
    )
    events = [*events, branch_sent, grad_across]

    branch_sent, grad_half, grad_across = late([branch_sent, grad_half, grad_across], events)
    branch_came = moves.over_core(branch_sent)
    grad_other, grad_far = moves.over_core(grad_half), moves.over_core(grad_across)
    middle, norm_half = norm_mid(
        tokens, branch, branch_came, column(out_bias), column(ln2_gain), column(ln2_bias)
    )
    events = [norm_half, grad_other, grad_far]
    if moves.square:
        split = ff_piece.shape[0] // 2
        ff_x, ff_y = late([ff_x, ff_y], [branch_sent])
        low_sent, high_sent = ff_y[:split], ff_x[split:]
        events = [*events, low_sent, high_sent]
    grad_out = [grad_half, grad_across, grad_other, grad_far]

    (norm_half,) = late([norm_half], events)
    norm_across = moves.over_z(norm_half, 1)
    norm_other = moves.over_core(norm_half)
    if moves.square:
        low_sent, high_sent = late([low_sent, high_sent], events)
        ff_low, ff_high = moves.over_x(low_sent), moves.over_y(high_sent)
        (norm_across,) = late([norm_across], [ff_low, ff_high])
        w_up, w_down = moves.lay((ff_piece, ff_x, ff_y), (ff_low, ff_high), 2)
    norm_far = moves.over_core(norm_across)
    normed_two = [norm_half, norm_across, norm_other, norm_far]

    activ, slope = product(
        w_up,
        normed_two,
        "nn",
        320,
        lambda value, at, bias: gelu_pair(value + bias[...]),
        (column(up_bias_own),),
        ((None, BF16), (None, BF16)),
        name="project_up",
        wait=grad_out,
    )

    def in_halves(value, at):
        half = value.shape[1] // 2
        return value[:, :half], value[:, half:]

    pairs = ((length, BF16), (length, BF16))

    def through_gelu(value, at, slope_ref):
        size = value.shape[1]
        slope_here = slope_ref[:, at * size : (at + 1) * size].astype(F32)
        grad = (value * slope_here).astype(BF16)
        sums = lane_sums(grad.astype(F32))
        return (grad, None, sums) if at < 2 else (None, grad, sums)

    ff_cut = 896 if width == 1600 else width // 256 * 128
    down_parts = moves.scatter_first([(grad_out, activ)], ff_cut)
    down_near = moves.scatter_near(down_parts)
    pre_here, pre_there, grad_pre_sums = product(
        w_down,
        grad_out,
        "tn",
        256,
        through_gelu,
        (slope,),
        (*pairs, (512, F32)),
        name="back_down",
        wait=down_parts[:1],
    )
    norm_there = product(w_up, pre_there, "tn", 256, name="back_up")

    norm_came = moves.over_core(norm_there)
    norm_here = product(
        w_up, pre_here, "tn", 256, name="back_up", wait=[norm_there, *down_near[1]]
    )
    events = [norm_came, norm_here]

    norm_came, norm_here = late([norm_came, norm_here], events)
    norm_last = moves.over_z(norm_here[:, half_len:] + norm_came[:, half_len:], 1)
    down_far = moves.scatter_far(down_near, events)
    down_here, down_there = product(
        w_down, activ, "nn", 320, in_halves, (), pairs, name="project_down", wait=events
    )
    up_parts = moves.scatter_first([([pre_here, pre_there], normed_two)], ff_cut, [down_there])
    events = [norm_last, *down_far[1], up_parts[0]]

    (norm_last,) = late([norm_last], events)
    grad_middle, grad_branch_half, mid_sums = norm_mid_back(
        (norm_here, norm_came, norm_last), middle, grad_half, column(ln2_gain), events
    )
    (down_part,) = late([moves.scatter_last(down_far, width)], [grad_branch_half])
    grad_branch = moves.ordered(grad_branch_half, moves.over_core(grad_branch_half))
    grad_mixed = product(w_out, grad_branch, "tn", OWN, name="back_out", wait=[down_part], share=0.01)
    upper = to_sixteen(down_part.shape[0] // 2)
    down_low, down_high = down_part[:upper], down_part[upper:]
    events = [grad_mixed, down_low, down_high]

    up_near = moves.scatter_near(up_parts, events)
    down_there, down_low, down_high = late([down_there, down_low, down_high], events)
    down_came = moves.over_core(down_there)
    down_come = [moves.alike(down_low)]
    grad_own = attention_back(seg, joined, mixed, grad_mixed, lse, events).reshape(3 * OWN, length)
    events = [*up_near[1], down_came, down_come[0], grad_own]

    (grad_own,) = late([grad_own], events)
    grad_heads = moves.over_core(grad_own)
    up_far = moves.scatter_far(up_near, events)
    (down_high,) = late([down_high], events)
    down_come.append(moves.alike(down_high))
    down_sent = down_here[:, half_len:] + down_came[:, half_len:]
    padded = to_tiles(OWN)
    out_parts = moves.scatter_first([(grad_branch, mixed)], 512, events)
    norm_one, norm_one_sent = product(
        w_qkv, grad_own, "tn", 256, by_side, (side,), halves, name="back_qkv", wait=out_parts[:1]
    )
    events = [grad_heads, *up_far[1], down_come[1], norm_one_sent]

    grad_heads, norm_one_sent = late([grad_heads, norm_one_sent], events)
    down_sum = moves.alike_sum(down_part, late(down_come, events))
    down_across = moves.over_z(down_sum, 1)
    (up_part,) = late([moves.scatter_last(up_far, width)], events)
    norm_one_came = moves.over_core(norm_one_sent)
    out_near = moves.scatter_near(out_parts, events)
    if moves.square:
        grad_rows = join_heads(
            moves.core_ref, grad_own, grad_heads, counts[0], taken[0], [up_part]
        )
    else:
        low = jnp.where(core == 0, grad_own, grad_heads)
        high = jnp.where(core == 0, grad_heads, grad_own)
        grad_joined = jnp.concatenate(
            [
                piece
                for part in range(3)
                for piece in (
                    low[part * OWN : (part + 1) * OWN],
                    high[part * OWN + HDIM : (part + 1) * OWN],
                )
            ],
            axis=0,
        )
        grad_rows = jnp.concatenate(
            [
                lax.dynamic_slice_in_dim(
                    grad_joined, shard * counts[0] + core * (counts[0] - taken[0]), taken[0], 0
                )
                for shard in range(shard_count)
            ],
            axis=0,
        )
    qkv_parts = moves.scatter_first([(grad_rows, normed)], ff_cut, events)
    up_low, up_high = up_part[:upper], up_part[upper:]
    events = [qkv_parts[0], norm_one_came, down_across, *out_near[1], up_low, up_high, down_sent]

    qkv_near = moves.scatter_near(qkv_parts, events)
    down_sent, norm_one_came, up_low, up_high = late(
        [down_sent, norm_one_came, up_low, up_high], events
    )
    up_come = [moves.alike(up_low)]
    down_last = moves.over_z(down_sent, 1)
    input_half, in_sums = norm_in_back(
        (norm_one, norm_one_came), tokens, grad_middle, column(ln1_gain)
    )
    up_bias_grad = jnp.sum(grad_pre_sums, axis=1).reshape(shard_count, 1, strip)
    up_bias_grad = up_bias_grad * (jnp.arange(4)[None, :, None] == quarter).astype(F32)
    head_sums = jnp.sum(grad_own.astype(F32), axis=1).reshape(3, OWN)
    bias_sums = lax.dynamic_update_slice(
        jnp.zeros((3, width), F32), head_sums, (jnp.int32(0), first_row)
    )
    small = jnp.concatenate(
        [
            up_bias_grad.reshape(-1),
            jnp.sum(mid_sums, axis=2).reshape(-1),
            jnp.sum(in_sums, axis=2).reshape(-1),
            bias_sums[0],
            bias_sums[2],
        ]
    ).reshape(-1, 128)
    events = [*qkv_near[1], down_last, up_come[0], input_half, small]

    qkv_far = moves.scatter_far(qkv_near, events)
    out_far = moves.scatter_far(out_near, events)
    up_high, down_last, small = late([up_high, down_last, small], events)
    up_come.append(moves.alike(up_high))
    small = moves.small_cores(small)
    tokens_back = results(
        at, seqs, middle, (down_here, down_came, down_last), column(down_bias), input_half
    )
    events = [*qkv_far[1], *out_far[1], up_come[1], small, *tokens_back]

    down_sum, down_across, *tokens_back = late([down_sum, down_across, *tokens_back], events)
    tokens_came = moves.from_chips(tokens_back)
    qkv_pair = moves.total_pair(moves.scatter_last(qkv_far, width))
    out_pair = moves.total_pair(moves.scatter_last(out_far, padded))
    down_other = moves.over_core(down_sum)
    down_far_other = moves.over_core(down_across)
    events = [qkv_pair, out_pair, down_other, down_far_other, tokens_came]

    up_sum = moves.alike_sum(up_part, late(up_come, events))
    qkv_pair, up_sum, small, down_far_other = late(
        [qkv_pair, up_sum, small, down_far_other], events
    )
    qkv_full = moves.total_all(qkv_pair)
    up_across = moves.over_z(up_sum, 1)
    small = moves.small_columns(moves.small_square(small), 1)
    quarter_ref = quarter.astype(jnp.int32)[None]
    down_total = finish_down(
        quarter_ref, [down_sum, down_other, down_across, down_far_other], shard_count
    )
    events = [qkv_full, up_across, small, down_total]

    qkv_full, out_pair, up_across, up_sum, small = late(
        [qkv_full, out_pair, up_across, up_sum, small], events
    )
    qkv_sum = moves.total_halves(qkv_full)
    out_full = moves.total_all(out_pair)
    small = moves.small_columns(small, 2).reshape(-1)
    up_parts = [up_sum, moves.over_core(up_sum), up_across, moves.over_core(up_across)]
    events = [*qkv_sum, out_full, *up_parts]

    (out_full,) = late([out_full], events)
    out_sum = moves.total_halves(out_full)
    qkv_sum = moves.four(late(qkv_sum, events))
    up_total = finish_up(quarter_ref, late(up_parts, events))
    qkv_total = moves.rows(late(qkv_sum, [up_total]), counts[0])
    out_sum = moves.four(late(out_sum, [up_total]))
    out_total = moves.sides(late(out_sum, [qkv_total]))
    (tokens_came,) = late([tokens_came], [up_total])
    result, input_grad = tokens_came[:, :width], tokens_came[:, width:].astype(F32)

    up_bias_grad, rest = small[:ff], small[ff:]
    (
        ln2_gain_grad,
        ln2_bias_grad,
        down_bias_grad,
        out_bias_grad,
        ln1_gain_grad,
        ln1_bias_grad,
        q_bias_grad,
        v_bias_grad,
    ) = rest.reshape(8, width)

    return (
        result.transpose(2, 0, 1),
        input_grad.transpose(2, 0, 1),
        ln1_gain_grad,
        ln1_bias_grad,
        qkv_total,
        q_bias_grad,
        v_bias_grad,
        out_total,
        out_bias_grad,
        ln2_gain_grad,
        ln2_bias_grad,
        up_total,
        up_bias_grad,
        down_total,
        down_bias_grad,
    )


def solution(mesh):
    rows = P("shard", None)
    tokens = P("shard", "replica", None)
    in_specs = (
        tokens,
        tokens,
        P(None, "replica"),
        P(),
        P(),
        rows,
        P(),
        P(),
        rows,
        P(),
        P(),
        P(),
        rows,
        P(),
        rows,
        P(),
    )
    out_specs = (
        tokens,
        tokens,
        P(),
        P(),
        rows,
        P(),
        P(),
        rows,
        P(),
        P(),
        P(),
        rows,
        P(),
        rows,
        P(),
    )
    body = functools.partial(shards, mesh.shape["shard"], mesh.shape["replica"])
    return jax.shard_map(body, mesh=mesh, in_specs=in_specs, out_specs=out_specs, check_vma=False)
```

```python
import functools

import jax
import jax.numpy as jnp
from jax import lax
from jax.experimental import pallas as pl
from jax.experimental.pallas import tpu as pltpu
from jax.sharding import PartitionSpec as P

HEADS = 25
HDIM = 64
OWN_HEADS = HEADS // 2 + 1
FIRST_HEAD = HEADS // 2
OWN = OWN_HEADS * HDIM
BLOCK = 256
AXES = ("shard", "replica")
BF16 = jnp.bfloat16
F32 = jnp.float32


def dot(left, right, left_dim, right_dim):
    return lax.dot_general(
        left, right, (((left_dim,), (right_dim,)), ((), ())), preferred_element_type=F32
    )


COST_SCALE = 8


def cost(flops, bytes_accessed, share=1.0):
    return pl.CostEstimate(
        flops=int(flops * COST_SCALE * share),
        bytes_accessed=int(bytes_accessed * COST_SCALE * share),
        transcendentals=0,
    )


def gelu_pair(value):
    root = 0.7978845608028654
    cube = 0.044715
    square = value * value
    tanh = jnp.tanh(root * value * (1.0 + cube * square))
    half = 0.5 * (1.0 + tanh)
    slope = half + 0.5 * value * (1.0 - tanh * tanh) * root * (1.0 + 3.0 * cube * square)
    return value * half, slope


def fill_mask(seg_row, seg_col, mask, blocks):
    for q_at in range(blocks):
        for k_at in range(q_at + 1):
            keys = seg_col[pl.ds(k_at * BLOCK, BLOCK), :]
            queries = seg_row[:, pl.ds(q_at * BLOCK, BLOCK)]
            seen = keys == queries
            if k_at == q_at:
                k_place = lax.broadcasted_iota(jnp.int32, (BLOCK, BLOCK), 0)
                q_place = lax.broadcasted_iota(jnp.int32, (BLOCK, BLOCK), 1)
                seen = seen & (k_place <= q_place)
            mask[pl.ds(k_at * BLOCK, BLOCK), pl.ds(q_at * BLOCK, BLOCK)] = jnp.where(
                seen, 0.0, -1e30
            )


def forward_kernel(seg_row, seg_col, q_ref, k_ref, v_ref, *refs):
    o_ref, lse_ref, mask = refs[-3:]
    length = q_ref.shape[1]
    blocks = length // BLOCK

    @pl.when(pl.program_id(0) == 0)
    def _():
        fill_mask(seg_row, seg_col, mask, blocks)

    keys = k_ref[...].T
    for q_at in range(blocks):
        span = (q_at + 1) * BLOCK
        here = pl.ds(q_at * BLOCK, BLOCK)
        scores = dot(keys[:span], q_ref[:, here], 1, 0) + mask[:span, here]
        peak = jnp.max(scores, axis=0, keepdims=True)
        terms = jnp.exp(scores - peak)
        total = jnp.sum(terms, axis=0, keepdims=True)
        mixed = dot(v_ref[:, :span], terms.astype(BF16), 1, 0)
        o_ref[:, here] = (mixed / total).astype(BF16)
        lse_ref[0, :, here] = peak + jnp.log(total)


def backward_kernel(seg_row, seg_col, q_ref, k_ref, v_ref, o_ref, g_ref, lse_ref, *refs):
    grads, mask, acc = refs[-3:]
    length = q_ref.shape[1]
    blocks = length // BLOCK

    @pl.when(pl.program_id(0) == 0)
    def _():
        fill_mask(seg_row, seg_col, mask, blocks)

    keys = k_ref[...].T
    values = v_ref[...].T
    delta = jnp.sum(g_ref[...].astype(F32) * o_ref[...].astype(F32), axis=0, keepdims=True)
    lse = lse_ref[0]
    for k_at in range(blocks):
        low = k_at * BLOCK
        here = pl.ds(low, BLOCK)
        rest = pl.ds(low, length - low)
        scores = dot(keys[low : low + BLOCK], q_ref[:, rest], 1, 0) + mask[here, rest]
        soft = jnp.exp(scores - lse[:, low:])
        soft_grad = dot(values[low : low + BLOCK], g_ref[:, rest], 1, 0)
        score_grad = (soft * (soft_grad - delta[:, low:])).astype(BF16)
        grads[2, :, here] = dot(g_ref[:, rest], soft.astype(BF16), 1, 1).astype(BF16)
        grads[1, :, here] = dot(q_ref[:, rest], score_grad, 1, 1).astype(BF16)
        grad_q = dot(k_ref[:, here], score_grad, 1, 0)
        if k_at == 0:
            acc[...] = grad_q
        else:
            acc[:, rest] += grad_q
    grads[0] = (acc[...] * 0.125).astype(BF16)


def head_spec(first, length):
    return pl.BlockSpec((HDIM, length), lambda head: (first + head, 0))


def whole_spec(shape):
    return pl.BlockSpec(shape, lambda head: (0,) * len(shape))


def attention(seg, joined, wait):
    length = seg.shape[0]
    lse_spec = pl.BlockSpec((1, 1, length), lambda head: (head, 0, 0))
    pairs = OWN_HEADS * length * length
    return pl.pallas_call(
        forward_kernel,
        grid=(OWN_HEADS,),
        in_specs=[whole_spec((1, length)), whole_spec((length, 1))]
        + [head_spec(part * OWN_HEADS, length) for part in range(3)]
        + [pl.BlockSpec(memory_space=pl.ANY)] * len(wait),
        out_specs=[head_spec(0, length), lse_spec],
        out_shape=[
            jax.ShapeDtypeStruct((OWN, length), BF16),
            jax.ShapeDtypeStruct((OWN_HEADS, 1, length), F32),
        ],
        scratch_shapes=[pltpu.VMEM((length, length), F32)],
        compiler_params=pltpu.CompilerParams(vmem_limit_bytes=40 * 2**20),
        cost_estimate=cost(16 * pairs * HDIM, 8 * OWN * length),
        name="attention_forward",
    )(seg.reshape(1, length), seg.reshape(length, 1), joined, joined, joined, *wait)


def attention_back(seg, joined, mixed, grad, lse, wait):
    length = seg.shape[0]
    lse_spec = pl.BlockSpec((1, 1, length), lambda head: (head, 0, 0))
    pairs = OWN_HEADS * length * length
    return pl.pallas_call(
        backward_kernel,
        grid=(OWN_HEADS,),
        in_specs=[whole_spec((1, length)), whole_spec((length, 1))]
        + [head_spec(part * OWN_HEADS, length) for part in range(3)]
        + [head_spec(0, length), head_spec(0, length), lse_spec]
        + [pl.BlockSpec(memory_space=pl.ANY)] * len(wait),
        out_specs=pl.BlockSpec((3, HDIM, length), lambda head: (0, head, 0)),
        out_shape=jax.ShapeDtypeStruct((3, OWN, length), BF16),
        scratch_shapes=[pltpu.VMEM((length, length), F32), pltpu.VMEM((HDIM, length), F32)],
        compiler_params=pltpu.CompilerParams(vmem_limit_bytes=48 * 2**20),
        cost_estimate=cost(40 * pairs * HDIM, 16 * OWN * length),
        name="attention_backward",
    )(
        seg.reshape(1, length),
        seg.reshape(length, 1),
        joined,
        joined,
        joined,
        mixed,
        grad,
        lse,
        *wait,
    )


def product(left, rights, form, block, finish=None, extras=(), outs=((None, BF16),), name="product",
            wait=(), share=1.0):
    rights = rights if isinstance(rights, (list, tuple)) else [rights]
    many = len(rights)
    left_dim, right_dim = (0 if form == "tn" else 1), (1 if form == "nt" else 0)
    m, k = left.shape[1 - left_dim], left.shape[left_dim]
    size = rights[0].shape[1 - right_dim]
    n = size * many
    block = min(block, m)

    def body(left_ref, *refs):
        extra_refs = refs[many : many + len(extras)]
        out_refs = refs[many + len(extras) + len(wait) :]
        for at in range(many):
            value = dot(left_ref[...], refs[at][...], left_dim, right_dim)
            values = (value,)
            if finish is not None:
                values = finish(value, at, *extra_refs)
            for ref, part in zip(out_refs, values):
                if part is not None:
                    width = part.shape[1]
                    begin = at * width % ref.shape[1]
                    ref[:, begin : begin + width] = part.astype(ref.dtype)

    if form == "tn":
        left_spec = pl.BlockSpec((k, block), lambda i: (0, i))
    else:
        left_spec = pl.BlockSpec((block, k), lambda i: (i, 0))
    sizes = [(columns or n, kind) for columns, kind in outs]
    results = pl.pallas_call(
        body,
        grid=(pl.cdiv(m, block),),
        in_specs=[left_spec]
        + [
            pl.BlockSpec(right.shape, lambda i: (0, 0), pipeline_mode=pl.Buffered(1))
            for right in rights
        ]
        + [pl.BlockSpec((block, extra.shape[1]), lambda i: (i, 0)) for extra in extras]
        + [pl.BlockSpec(memory_space=pl.ANY)] * len(wait),
        out_specs=[pl.BlockSpec((block, columns), lambda i: (i, 0)) for columns, _ in sizes],
        out_shape=[jax.ShapeDtypeStruct((m, columns), kind) for columns, kind in sizes],
        compiler_params=pltpu.CompilerParams(vmem_limit_bytes=56 * 2**20),
        cost_estimate=cost(2 * m * n * k, 2 * (m * k + n * k + m * n), share),
        name=name,
    )(left, *rights, *extras, *wait)
    return results if len(outs) > 1 else results[0]


def lane_sums(value):
    return sum(value[:, at : at + 128] for at in range(0, value.shape[1], 128))


PARAMS = pltpu.CompilerParams(vmem_limit_bytes=56 * 2**20)


def norm_parts(rows):
    centre = rows - jnp.mean(rows, axis=0, keepdims=True)
    scale = lax.rsqrt(jnp.mean(centre * centre, axis=0, keepdims=True) + 1e-05)
    return centre * scale, scale


def norm_back(grad, unit, scale, gain):
    inner = grad * gain
    mean_inner = jnp.mean(inner, axis=0, keepdims=True)
    mean_cross = jnp.mean(inner * unit, axis=0, keepdims=True)
    return scale * (inner - mean_inner - unit * mean_cross)


def column_specs(shape, size, many):
    return [pl.BlockSpec((shape[0], size), lambda i, *_: (0, i))] * many


def fixed_specs(shape, many):
    return [pl.BlockSpec(shape, lambda i, *_: (0,) * len(shape))] * many


def norm_in(at, came, gain, bias):
    pieces = len(came)
    rows, count = came[0].shape

    def body(at_ref, *refs):
        gain_ref, bias_ref, tokens_ref, norm_ref = refs[pieces:]
        which = lax.rem(at_ref[0] - pl.program_id(0) + pieces, pieces)
        for piece in range(pieces):

            @pl.when(which == piece)
            def _(piece=piece):
                tokens_ref[...] = refs[piece][...]

        unit, _ = norm_parts(tokens_ref[...].astype(F32))
        norm_ref[...] = (unit * gain_ref[...] + bias_ref[...]).astype(BF16)

    return pl.pallas_call(
        body,
        grid_spec=pltpu.PrefetchScalarGridSpec(
            num_scalar_prefetch=1,
            grid=(pieces,),
            in_specs=fixed_specs((rows, count), pieces) + fixed_specs((rows, 1), 2),
            out_specs=column_specs((rows, pieces * count), count, 2),
        ),
        out_shape=[jax.ShapeDtypeStruct((rows, pieces * count), BF16)] * 2,
        compiler_params=PARAMS,
        cost_estimate=cost(0, 40 * rows * pieces * count),
        name="norm_in",
    )(at, *came, gain, bias)


def norm_mid(tokens, mine, came, shift, gain, bias):
    rows, columns = tokens.shape
    size = columns // 2

    def body(tokens_ref, mine_ref, came_ref, shift_ref, gain_ref, bias_ref, middle_ref, norm_ref):
        middle = mine_ref[...].astype(F32) + came_ref[...].astype(F32)
        middle = tokens_ref[...].astype(F32) + middle + shift_ref[...]
        middle_ref[...] = middle
        unit, _ = norm_parts(middle)
        norm_ref[...] = (unit * gain_ref[...] + bias_ref[...]).astype(BF16)

    return pl.pallas_call(
        body,
        grid=(2,),
        in_specs=column_specs((rows, columns), size, 3) + fixed_specs((rows, 1), 3),
        out_specs=column_specs((rows, columns), size, 2),
        out_shape=[
            jax.ShapeDtypeStruct((rows, columns), F32),
            jax.ShapeDtypeStruct((rows, columns), BF16),
        ],
        compiler_params=PARAMS,
        cost_estimate=cost(0, 40 * rows * columns),
        name="norm_mid",
    )(tokens, mine, came, shift, gain, bias)


def norm_mid_back(parts, middle, grad, gain, wait):
    rows, columns = middle.shape
    size = columns // 2
    many = len(parts)

    def body(*refs):
        middle_ref, grad_ref, gain_ref = refs[many : many + 3]
        out_ref, low_ref, sums_ref = refs[-3:]
        norm_grad = sum(ref[...].astype(F32) for ref in refs[:many])
        unit, scale = norm_parts(middle_ref[...])
        through = grad_ref[...].astype(F32)
        value = through + norm_back(norm_grad, unit, scale, gain_ref[...])
        out_ref[...] = value
        low_ref[...] = value.astype(BF16)
        sums = (norm_grad * unit, norm_grad, through, value.astype(BF16).astype(F32))
        for at, rows_of_sum in enumerate(sums):
            here = lane_sums(rows_of_sum)

            @pl.when(pl.program_id(0) == 0)
            def _(at=at, here=here):
                sums_ref[at] = here

            @pl.when(pl.program_id(0) > 0)
            def _(at=at, here=here):
                sums_ref[at] += here

    return pl.pallas_call(
        body,
        grid=(2,),
        in_specs=column_specs((rows, columns), size, many + 2)
        + fixed_specs((rows, 1), 1)
        + [pl.BlockSpec(memory_space=pl.ANY)] * len(wait),
        out_specs=column_specs((rows, columns), size, 2) + fixed_specs((4, rows, 128), 1),
        out_shape=[
            jax.ShapeDtypeStruct((rows, columns), F32),
            jax.ShapeDtypeStruct((rows, columns), BF16),
            jax.ShapeDtypeStruct((4, rows, 128), F32),
        ],
        compiler_params=PARAMS,
        cost_estimate=cost(0, 60 * rows * columns),
        name="norm_mid_back",
    )(*parts, middle, grad, gain, *wait)


def norm_in_back(parts, tokens, grad, gain):
    rows, columns = tokens.shape
    size = columns // 2
    many = len(parts)

    def body(*refs):
        tokens_ref, grad_ref, gain_ref, out_ref, sums_ref = refs[many:]
        norm_grad = sum(ref[...].astype(F32) for ref in refs[:many])
        unit, scale = norm_parts(tokens_ref[...].astype(F32))
        value = grad_ref[...] + norm_back(norm_grad, unit, scale, gain_ref[...])
        out_ref[...] = value.astype(BF16)
        for at, rows_of_sum in enumerate((norm_grad * unit, norm_grad)):
            here = lane_sums(rows_of_sum)

            @pl.when(pl.program_id(0) == 0)
            def _(at=at, here=here):
                sums_ref[at] = here

            @pl.when(pl.program_id(0) > 0)
            def _(at=at, here=here):
                sums_ref[at] += here

    return pl.pallas_call(
        body,
        grid=(2,),
        in_specs=column_specs((rows, columns), size, many + 2) + fixed_specs((rows, 1), 1),
        out_specs=column_specs((rows, columns), size, 1) + fixed_specs((2, rows, 128), 1),
        out_shape=[
            jax.ShapeDtypeStruct((rows, columns), BF16),
            jax.ShapeDtypeStruct((2, rows, 128), F32),
        ],
        compiler_params=PARAMS,
        cost_estimate=cost(0, 60 * rows * columns),
        name="norm_in_back",
    )(*parts, tokens, grad, gain)


def results(at, pieces, middle, parts, shift, input_half):
    rows, columns = middle.shape
    size = columns // pieces
    many = len(parts)

    def body(at_ref, middle_ref, *refs):
        shift_ref, input_ref = refs[many : many + 2]
        outs = refs[many + 2 :]
        value = middle_ref[...] + shift_ref[...]
        for ref in refs[:many]:
            value = value + ref[...].astype(F32)
        value = value.astype(BF16)
        which = lax.rem(at_ref[0] - pl.program_id(0) + pieces, pieces)
        for piece, out in enumerate(outs):

            @pl.when(which == piece)
            def _(out=out):
                out[:rows] = value
                out[rows:] = input_ref[...]

    block = column_specs((rows, columns), size, 1)
    return pl.pallas_call(
        body,
        grid_spec=pltpu.PrefetchScalarGridSpec(
            num_scalar_prefetch=1,
            grid=(pieces,),
            in_specs=block * (1 + many) + fixed_specs((rows, 1), 1) + block,
            out_specs=fixed_specs((2 * rows, size), pieces),
        ),
        out_shape=[jax.ShapeDtypeStruct((2 * rows, size), BF16)] * pieces,
        compiler_params=PARAMS,
        cost_estimate=cost(0, 40 * rows * columns),
        name="results",
    )(at, middle, *parts, shift, input_half)


def lay(places, near, far, parts):
    count, columns = near[0].shape
    size = count // parts
    kind = near[0].dtype

    def body(places_ref, *refs):
        step = pl.program_id(0)
        outs = refs[5:]
        for at in range(3):

            @pl.when(step == at)
            def _(at=at):
                for index, out in enumerate(outs):
                    out[...] = refs[at][index * size : (index + 1) * size]

        @pl.when(step == 3)
        def _():
            start = 0
            for ref in refs[3:5]:
                rows = ref.shape[0]
                for index, out in enumerate(outs):
                    low, high = max(start, index * size), min(start + rows, (index + 1) * size)
                    if low < high:
                        out[low - index * size : high - index * size] = ref[
                            low - start : high - start
                        ]
                start += rows

    pieces = list(near) + list(far)
    return pl.pallas_call(
        body,
        grid_spec=pltpu.PrefetchScalarGridSpec(
            num_scalar_prefetch=1,
            grid=(4,),
            in_specs=[
                pl.BlockSpec(piece.shape, lambda i, p: (0, 0), pipeline_mode=pl.Buffered(1))
                for piece in pieces
            ],
            out_specs=[pl.BlockSpec((size, columns), lambda i, p: (p[i], 0))] * parts,
        ),
        out_shape=[jax.ShapeDtypeStruct((4 * size, columns), kind)] * parts,
        compiler_params=pltpu.CompilerParams(vmem_limit_bytes=56 * 2**20),
        cost_estimate=cost(0, 16 * count * columns),
        name="lay",
    )(places, *pieces)


def lay_near(places, near, parts):
    count, columns = near[0].shape
    size = count // parts

    def body(places_ref, *refs):
        for at in range(3):

            @pl.when(pl.program_id(0) == at)
            def _(at=at):
                for index, out in enumerate(refs[3:]):
                    out[...] = refs[at][index * size : (index + 1) * size]

    return pl.pallas_call(
        body,
        grid_spec=pltpu.PrefetchScalarGridSpec(
            num_scalar_prefetch=1,
            grid=(3,),
            in_specs=[
                pl.BlockSpec(piece.shape, lambda i, p: (0, 0), pipeline_mode=pl.Buffered(1))
                for piece in near
            ],
            out_specs=[pl.BlockSpec((size, columns), lambda i, p: (p[i], 0))] * parts,
        ),
        out_shape=[jax.ShapeDtypeStruct((4 * size, columns), near[0].dtype)] * parts,
        compiler_params=PARAMS,
        cost_estimate=cost(0, 12 * count * columns),
        name="lay_near",
    )(places, *near)


def lay_far(places, far, laid):
    parts = len(far)
    size, columns = far[0].shape

    def body(places_ref, *refs):
        for ref, out in zip(refs[:parts], refs[2 * parts :]):
            out[...] = ref[...]

    return pl.pallas_call(
        body,
        grid_spec=pltpu.PrefetchScalarGridSpec(
            num_scalar_prefetch=1,
            grid=(1,),
            in_specs=[pl.BlockSpec(piece.shape, lambda i, p: (0, 0)) for piece in far]
            + [pl.BlockSpec(memory_space=pl.ANY)] * parts,
            out_specs=[pl.BlockSpec((size, columns), lambda i, p: (p[3], 0))] * parts,
        ),
        out_shape=[jax.ShapeDtypeStruct(array.shape, array.dtype) for array in laid],
        input_output_aliases={1 + parts + index: index for index in range(parts)},
        compiler_params=PARAMS,
        cost_estimate=cost(0, 4 * size * columns),
        name="lay_far",
    )(places, *far, *laid)


def lay_heads(core, places, mine, others, counts, taken, wait):
    width = mine[0].shape[1]
    split = mine[3].shape[0]
    cut = FIRST_HEAD * HDIM

    def body(core_ref, places_ref, *refs):
        heads_ref, out_ref, block, out_block = refs[-4:]
        step = pl.program_id(0)

        def copy(halves, at, begin, end, target, row):
            if at < 3:
                target[row : row + end - begin] = halves[at][begin:end]
                return
            if begin < split:
                middle = min(end, split)
                target[row : row + middle - begin] = halves[3][begin:middle]
            if end > split:
                middle = max(begin, split)
                target[row + middle - begin : row + end - begin] = halves[4][
                    middle - split : end - split
                ]

        for which in range(2):

            @pl.when(core_ref[0] == which)
            def _(which=which):
                low, high = (refs[:5], refs[5:10]) if which == 0 else (refs[5:10], refs[:5])
                for at in range(4):

                    @pl.when(step == at)
                    def _(at=at):
                        begin = 0
                        for target, rows, count in zip((block, out_block), taken, counts):
                            copy(low, at, begin, begin + rows, target, 0)
                            over = 2 * rows - count
                            copy(high, at, begin + over, begin + rows, target, rows)
                            begin += rows

                out_ref[...] = out_block[:, which * cut : which * cut + OWN]
                if which == 1:
                    out_ref[:, :HDIM] = jnp.zeros((counts[1], HDIM), BF16)
                for shard in range(4):

                    @pl.when(places_ref[step] == shard)
                    def _(shard=shard):
                        for part in range(3):
                            begin = part * width + which * cut
                            first = max(begin, shard * counts[0])
                            last = min(begin + OWN, (shard + 1) * counts[0])
                            if first < last:
                                heads_ref[
                                    part * OWN + first - begin : part * OWN + last - begin
                                ] = block[first - shard * counts[0] : last - shard * counts[0]]

    pieces = list(mine) + list(others)
    return pl.pallas_call(
        body,
        grid_spec=pltpu.PrefetchScalarGridSpec(
            num_scalar_prefetch=2,
            grid=(4,),
            in_specs=[
                pl.BlockSpec(piece.shape, lambda i, c, p: (0, 0), pipeline_mode=pl.Buffered(1))
                for piece in pieces
            ]
            + [pl.BlockSpec(memory_space=pl.ANY)] * len(wait),
            out_specs=[
                pl.BlockSpec(
                    (3 * OWN, width), lambda i, c, p: (0, 0), pipeline_mode=pl.Buffered(1)
                ),
                pl.BlockSpec((counts[1], OWN), lambda i, c, p: (p[i], 0)),
            ],
            scratch_shapes=[pltpu.VMEM((count, width), BF16) for count in counts],
        ),
        out_shape=[
            jax.ShapeDtypeStruct((3 * OWN, width), BF16),
            jax.ShapeDtypeStruct((4 * counts[1], OWN), BF16),
        ],
        compiler_params=pltpu.CompilerParams(vmem_limit_bytes=56 * 2**20),
        cost_estimate=cost(0, 16 * counts[0] * width),
        name="lay_heads",
    )(core, places, *pieces, *wait)


def join_heads(core, own, other, count, taken, wait):
    length = own.shape[1]
    rows = 2 * OWN - HDIM

    def body(core_ref, own_ref, other_ref, *refs):
        out = refs[-1]
        step = pl.program_id(0)
        for which in range(2):
            for shard in range(4):

                @pl.when((core_ref[0] == which) & (step == shard))
                def _(which=which, shard=shard):
                    low, high = (own_ref, other_ref) if which == 0 else (other_ref, own_ref)
                    begin = shard * count + which * (count - taken)
                    at = begin
                    while at < begin + taken:
                        part, row = at // rows, at % rows
                        source, skip, last = (
                            (low, 0, OWN) if row < OWN else (high, OWN - HDIM, rows)
                        )
                        end = min(begin + taken, part * rows + last)
                        first = part * OWN + row - skip
                        out[at - begin : end - begin] = source[first : first + end - at]
                        at = end

    whole = pl.BlockSpec(own.shape, lambda i, c: (0, 0), pipeline_mode=pl.Buffered(1))
    return pl.pallas_call(
        body,
        grid_spec=pltpu.PrefetchScalarGridSpec(
            num_scalar_prefetch=1,
            grid=(4,),
            in_specs=[whole, whole] + [pl.BlockSpec(memory_space=pl.ANY)] * len(wait),
            out_specs=pl.BlockSpec((taken, length), lambda i, c: (i, 0)),
        ),
        out_shape=jax.ShapeDtypeStruct((4 * taken, length), BF16),
        compiler_params=pltpu.CompilerParams(vmem_limit_bytes=56 * 2**20),
        cost_estimate=cost(0, 12 * rows * length),
        name="join_heads",
    )(core, own, other, *wait)


def product_parts(order, pairs, cut, wait):
    many = len(pairs)
    lefts = [side_of(left) for left, _ in pairs]
    rights = [side_of(right) for _, right in pairs]
    count = lefts[0][0].shape[0] // 4
    depth = sum(piece.shape[1] for piece in lefts[0])
    columns = rights[0][0].shape[0]
    rest = columns - cut
    filled = to_tiles(rest)
    starts = [0]
    for sides in lefts + rights:
        starts.append(starts[-1] + len(sides))

    def body(order_ref, *refs):
        send_x, send_y, keep_x, keep_y = refs[starts[-1] + len(wait) :]
        step = pl.program_id(0)
        targets = ((send_x, send_y), (send_x, keep_y), (keep_x, send_y), (keep_x, keep_y))
        for pair in range(many):

            @pl.when(step // 4 == pair)
            def _(pair=pair):
                left = refs[starts[pair] : starts[pair + 1]]
                right = refs[starts[many + pair] : starts[many + pair + 1]]
                value = side_product(left, right).astype(BF16)
                for at, (along_x, along_y) in enumerate(targets):

                    @pl.when(step % 4 == at)
                    def _(along_x=along_x, along_y=along_y):
                        along_x[...] = value[:, :cut]
                        along_y[:, :rest] = value[:, cut:]
                        if filled > rest:
                            along_y[:, rest:] = jnp.zeros((count, filled - rest), BF16)

    def left_spec(pair, piece):
        return pl.BlockSpec(
            (count, piece.shape[1]), lambda i, o: (o[jnp.clip(i - 4 * pair, 0, 3)], 0)
        )

    def out_spec(size, second):
        return pl.BlockSpec(
            (count, size), lambda i, o: (jnp.where(i % 4 >= second, many, 0) + i // 4, 0)
        )

    return pl.pallas_call(
        body,
        grid_spec=pltpu.PrefetchScalarGridSpec(
            num_scalar_prefetch=1,
            grid=(4 * many,),
            in_specs=[left_spec(pair, piece) for pair in range(many) for piece in lefts[pair]]
            + [
                pl.BlockSpec(piece.shape, lambda i, o: (0, 0), pipeline_mode=pl.Buffered(1))
                for right in rights
                for piece in right
            ]
            + [pl.BlockSpec(memory_space=pl.ANY)] * len(wait),
            out_specs=[
                out_spec(cut, 1),
                out_spec(filled, 2),
                out_spec(cut, 3),
                out_spec(filled, 3),
            ],
        ),
        out_shape=[
            jax.ShapeDtypeStruct((2 * many * count, size), BF16)
            for size in (cut, filled, cut, filled)
        ],
        compiler_params=pltpu.CompilerParams(vmem_limit_bytes=56 * 2**20),
        cost_estimate=cost(8 * many * count * depth * columns, 8 * many * count * (depth + columns)),
        name="product_parts",
    )(order, *[piece for sides in lefts + rights for piece in sides], *wait)


def side_of(side):
    return list(side) if isinstance(side, (list, tuple)) else [side]


def side_product(left, right):
    total = None
    size = min(piece.shape[1] for piece in (*left, *right))
    depth = sum(piece.shape[1] for piece in left)

    def chunk(pieces, begin):
        width = pieces[0].shape[1]
        return pieces[begin // width][:, begin % width : begin % width + size]

    for begin in range(0, depth, size):
        value = dot(chunk(left, begin), chunk(right, begin), 1, 1)
        total = value if total is None else total + value
    return total


def to_tiles(count):
    return -(-count // 128) * 128


def fold(keep_x, came_x, last_x, keep_y, came_y, last_y, columns, even=None):
    rows, cut = last_x.shape
    filled = last_y.shape[1]
    rest = columns - cut
    block = 400 if even is None else rows // 2
    steps = rows // block

    def fill(refs, out):
        for first, begin, size in ((0, 0, cut), (3, cut, rest)):
            value = refs[first][:, :size].astype(F32) + refs[first + 1][:, :size].astype(F32)
            value = value + refs[first + 2][:, :size].astype(F32)
            out[:, begin : begin + size] = value.astype(BF16)

    def body(*refs):
        if even is None:
            fill(refs[:6], refs[6])
            return
        mine = pl.program_id(0) == refs[0][0]

        @pl.when(mine)
        def _():
            fill(refs[1:7], refs[7])

        @pl.when(jnp.logical_not(mine))
        def _():
            fill(refs[1:7], refs[8])

    def specs(size):
        second = pl.BlockSpec((block, size), lambda i, *_: (steps + i, 0))
        return [second, second, pl.BlockSpec((block, size), lambda i, *_: (i, 0))]

    if even is not None:
        return pl.pallas_call(
            body,
            grid_spec=pltpu.PrefetchScalarGridSpec(
                num_scalar_prefetch=1,
                grid=(2,),
                in_specs=specs(cut) + specs(filled),
                out_specs=fixed_specs((block, columns), 2),
            ),
            out_shape=[jax.ShapeDtypeStruct((block, columns), BF16)] * 2,
            compiler_params=PARAMS,
            cost_estimate=cost(0, 8 * rows * columns, 0.01),
            name="fold_halves",
        )(even, keep_x, came_x, last_x, keep_y, came_y, last_y)
    return pl.pallas_call(
        body,
        grid=(steps,),
        in_specs=specs(cut) + specs(filled),
        out_specs=pl.BlockSpec((block, columns), lambda i: (i, 0)),
        out_shape=jax.ShapeDtypeStruct((rows, columns), BF16),
        compiler_params=pltpu.CompilerParams(vmem_limit_bytes=56 * 2**20),
        cost_estimate=cost(0, 8 * rows * columns, 0.01),
        name="fold",
    )(keep_x, came_x, last_x, keep_y, came_y, last_y)


def finish_up(quarter, parts):
    rows, width = parts[0].shape

    def body(quarter_ref, *refs):
        for at in range(4):

            @pl.when(pl.program_id(0) == at)
            def _(at=at):
                refs[4][...] = refs[at][...].astype(F32)

    return pl.pallas_call(
        body,
        grid_spec=pltpu.PrefetchScalarGridSpec(
            num_scalar_prefetch=1,
            grid=(4,),
            in_specs=[
                pl.BlockSpec((rows, width), lambda i, q: (0, 0), pipeline_mode=pl.Buffered(1))
            ]
            * 4,
            out_specs=pl.BlockSpec((rows, width), lambda i, q: (q[0] ^ i, 0)),
        ),
        out_shape=jax.ShapeDtypeStruct((4 * rows, width), F32),
        compiler_params=pltpu.CompilerParams(vmem_limit_bytes=56 * 2**20),
        cost_estimate=cost(0, 24 * rows * width),
        name="finish_up",
    )(quarter, *parts)


def finish_down(quarter, parts, shard_count):
    rows, width = parts[0].shape
    strip = width // shard_count
    block = 80 if rows % 80 == 0 else 40
    steps = rows // block

    def body(quarter_ref, *refs):
        for which in range(4):

            @pl.when(quarter_ref[0] == which)
            def _(which=which):
                for shard in range(shard_count):
                    for at in range(4):
                        begin = (4 * shard + at) * strip
                        refs[4][:, begin : begin + strip] = refs[which ^ at][
                            :, shard * strip : (shard + 1) * strip
                        ].astype(F32)

    return pl.pallas_call(
        body,
        grid_spec=pltpu.PrefetchScalarGridSpec(
            num_scalar_prefetch=1,
            grid=(steps,),
            in_specs=[pl.BlockSpec((block, width), lambda i, q: (i, 0))] * 4,
            out_specs=pl.BlockSpec((block, 4 * width), lambda i, q: (i, 0)),
        ),
        out_shape=jax.ShapeDtypeStruct((rows, 4 * width), F32),
        compiler_params=pltpu.CompilerParams(vmem_limit_bytes=56 * 2**20),
        cost_estimate=cost(0, 24 * rows * width),
        name="finish_down",
    )(quarter, *parts)


def finish_sides(core, even, parts):
    rows, width = parts[0].shape
    cut = FIRST_HEAD * HDIM

    def body(core_ref, even_ref, *refs):
        for which in range(2):
            for at in range(2):

                @pl.when((core_ref[0] == which) & (pl.program_id(0) == at))
                def _(which=which, at=at):
                    own, other = refs[at], refs[2 + at]
                    low, high = (own, other) if which == 0 else (other, own)
                    refs[4][:, :cut] = low[:, :cut].astype(F32)
                    refs[4][:, cut:] = high[:, :OWN].astype(F32)

    return pl.pallas_call(
        body,
        grid_spec=pltpu.PrefetchScalarGridSpec(
            num_scalar_prefetch=2,
            grid=(2,),
            in_specs=[
                pl.BlockSpec((rows, width), lambda i, c, e: (0, 0), pipeline_mode=pl.Buffered(1))
            ]
            * 4,
            out_specs=pl.BlockSpec((rows, cut + OWN), lambda i, c, e: (e[0] ^ i, 0)),
        ),
        out_shape=jax.ShapeDtypeStruct((2 * rows, cut + OWN), F32),
        compiler_params=pltpu.CompilerParams(vmem_limit_bytes=56 * 2**20),
        cost_estimate=cost(0, 16 * rows * width),
        name="finish_sides",
    )(core, even, *parts)


def finish_rows(core, even, parts, count):
    rows, width = parts[0].shape
    over = 4 * rows - count

    def body(core_ref, even_ref, *refs):
        out = refs[4]
        for which in range(2):
            for parity in range(2):

                @pl.when((core_ref[0] == which) & (even_ref[0] == parity))
                def _(which=which, parity=parity):
                    mine = [refs[parity], refs[1 - parity]]
                    others = [refs[2 + parity], refs[3 - parity]]
                    low, high = (mine, others) if which == 0 else (others, mine)
                    for at in range(2):

                        @pl.when(pl.program_id(0) == at)
                        def _(at=at):
                            out[...] = low[at][...].astype(F32)

                    @pl.when(pl.program_id(0) == 2)
                    def _():
                        out[: rows - over] = high[0][over:].astype(F32)
                        out[rows - over :] = high[1][:over].astype(F32)

                    @pl.when(pl.program_id(0) == 3)
                    def _():
                        out[: rows - over] = high[1][over:].astype(F32)

    return pl.pallas_call(
        body,
        grid_spec=pltpu.PrefetchScalarGridSpec(
            num_scalar_prefetch=2,
            grid=(4,),
            in_specs=[
                pl.BlockSpec((rows, width), lambda i, c, e: (0, 0), pipeline_mode=pl.Buffered(1))
            ]
            * 4,
            out_specs=pl.BlockSpec((rows, width), lambda i, c, e: (i, 0)),
        ),
        out_shape=jax.ShapeDtypeStruct((count, width), F32),
        compiler_params=pltpu.CompilerParams(vmem_limit_bytes=56 * 2**20),
        cost_estimate=cost(0, 24 * rows * width),
        name="finish_rows",
    )(core, even, *parts)


def to_sixteen(count):
    return -(-count // 16) * 16


def late(arrays, events):
    arrays = list(arrays)
    events = [event for event in events if event is not None]
    if not events:
        return arrays
    return lax.optimization_barrier((*arrays, *events))[: len(arrays)]


class Moves:
    def __init__(self, shard_count, replica_count):
        self.shard_count = shard_count
        self.replica_count = replica_count
        self.shard = lax.axis_index("shard")
        replica = lax.axis_index("replica")
        self.core = replica % 2
        self.column = replica // 2
        self.square = shard_count == 4 and replica_count == 8
        self.core_ref = self.core.astype(jnp.int32)[None]
        me = self.shard
        self.places = jnp.stack([me, me ^ 1, me ^ 2, me ^ 3]).astype(jnp.int32)
        self.order = jnp.stack([me ^ 3, me ^ 1, me ^ 2, me]).astype(jnp.int32)

    def move(self, array, route):
        pairs, stays = [], []
        for shard in range(self.shard_count):
            for column in range(self.replica_count // 2):
                for core in range(2):
                    target = route(shard, column, core)
                    if target == (shard, column, core):
                        stays.append((shard, core))
                    elif target is not None:
                        to_shard, to_column, to_core = target
                        pairs.append(
                            (
                                shard * self.replica_count + 2 * column + core,
                                to_shard * self.replica_count + 2 * to_column + to_core,
                            )
                        )
        came = lax.ppermute(array, AXES, pairs)
        if not stays:
            return came
        table = [(s, c) in stays for s in range(self.shard_count) for c in range(2)]
        return jnp.where(jnp.asarray(table)[2 * self.shard + self.core], array, came)

    def over_x(self, array):
        return self.move(array, lambda s, z, c: (s ^ 1, z, c))

    def over_y(self, array):
        return self.move(array, lambda s, z, c: (s ^ 2, z, c))

    def over_z(self, array, step):
        return self.move(array, lambda s, z, c: (s, z ^ step, c))

    def over_core(self, array):
        return self.move(array, lambda s, z, c: (s, z, 1 - c))

    def lay(self, near, far, parts=1):
        if self.square:
            return lay(self.places, near, far, parts)
        size = near[0].shape[0] // parts
        return [
            lax.all_gather(near[0][at * size : (at + 1) * size], "shard", axis=0, tiled=True)
            for at in range(parts)
        ]

    def scatter_first(self, pairs, cut, wait=()):
        if not self.square:
            return [
                product(
                    jnp.concatenate(side_of(left), axis=1),
                    jnp.concatenate(side_of(right), axis=1),
                    "nt",
                    400,
                )
                for left, right in pairs
            ]
        return product_parts(self.order, pairs, cut, wait)

    def scatter_near(self, parts, wait=()):
        if not self.square:
            return parts, []
        send_x, send_y = late(parts[:2], wait)
        return parts, [self.over_x(send_x), self.over_y(send_y)]

    def scatter_far(self, near, wait=()):
        parts, came = near
        if not self.square:
            return near, [], []
        keep_x, keep_y = parts[2:]
        half = keep_x.shape[0] // 2
        came_x, came_y = late(came, wait)
        sent_x, sent_y = keep_x[:half] + came_x[:half], keep_y[:half] + came_y[:half]
        return near, [self.over_y(sent_x), self.over_x(sent_y)], [sent_x, sent_y]

    def scatter_last(self, far, columns):
        (parts, came), last, _ = far
        if not self.square:
            sums = [
                lax.psum_scatter(part, "shard", scatter_dimension=0, tiled=True) for part in parts
            ]
            return jnp.concatenate(sums, axis=0)
        return fold(parts[2], came[0], last[0], parts[3], came[1], last[1], columns)

    def scatter_pair(self, far, columns):
        (parts, came), last, _ = far
        if not self.square:
            return self.scatter_last(far, columns)
        even = (self.column % 2).astype(jnp.int32)[None]
        keep, send = fold(parts[2], came[0], last[0], parts[3], came[1], last[1], columns, even)
        return keep + self.over_z(send, 1)

    def halves(self, array):
        rows = array.shape[0] // 2
        even = self.column % 2
        keep = lax.dynamic_slice_in_dim(array, even * rows, rows, 0)
        return keep, lax.dynamic_slice_in_dim(array, (1 - even) * rows, rows, 0)

    def total_all(self, pair):
        if not self.square:
            groups = [
                [2 * column + core for column in range(self.replica_count // 2)]
                for core in range(2)
            ]
            return lax.psum(pair, "replica", axis_index_groups=groups)
        return pair + self.over_z(pair, 2)

    def total_halves(self, full):
        return (full, self.over_z(full, 1)) if self.square else (full,)

    def four(self, sums):
        return list(sums) + [self.over_core(half) for half in sums]

    def sides(self, parts):
        even = (self.column % 2).astype(jnp.int32)[None]
        if self.square:
            return finish_sides(self.core_ref, even, parts)
        first = self.core == 0
        low, high = jnp.where(first, *parts), jnp.where(first, *parts[::-1])
        return jnp.concatenate([low[:, : FIRST_HEAD * HDIM], high[:, :OWN]], axis=1).astype(F32)

    def rows(self, parts, count):
        if self.square:
            even = (self.column % 2).astype(jnp.int32)[None]
            return finish_rows(self.core_ref, even, parts, count)
        first = self.core == 0
        low, high = jnp.where(first, *parts), jnp.where(first, *parts[::-1])
        return jnp.concatenate([low, high[2 * low.shape[0] - count :]], axis=0).astype(F32)

    def alike(self, array):
        return self.over_z(array, 2) if self.square else self.total_alike(array)

    def alike_sum(self, array, came):
        came = jnp.concatenate(came, axis=0)
        return array + came if self.square else came

    def total_alike(self, array):
        groups = [
            [2 * column + core for column in range(even, self.replica_count // 2, 2)]
            for even in range(2)
            for core in range(2)
        ]
        return lax.psum(array, "replica", axis_index_groups=groups)

    def small_cores(self, array):
        return array + self.over_core(array) if self.square else lax.psum(array, AXES)

    def small_square(self, array):
        if not self.square:
            return array
        array = array + self.over_x(array)
        return array + self.over_y(array)

    def small_columns(self, array, step):
        return array + self.over_z(array, step) if self.square else array

    def owners(self, step, seqs):
        return lambda s, z, c: (seqs * c + (s + step) % seqs, z, s // seqs)

    def to_chips(self, local):
        seqs, _, count = local.shape
        came = []
        for step in range(seqs):
            at = (self.shard + step) % seqs
            sent = lax.dynamic_index_in_dim(local, at, 0, keepdims=False)
            came.append(self.move(sent, self.owners(step, seqs)))
        return came

    def in_half(self, came):
        seqs = len(came)
        count = came[0].shape[1]
        at = self.shard % seqs
        if seqs == 2:
            first = at == 0
            return jnp.concatenate(
                [jnp.where(first, came[0], came[1]), jnp.where(first, came[1], came[0])], axis=1
            )
        ring = jnp.concatenate((came[::-1] * 2)[: 2 * seqs - 1], axis=1)
        return lax.dynamic_slice_in_dim(ring, (seqs - 1 - at) * count, seqs * count, 1)

    def from_chips(self, pieces):
        seqs = len(pieces)
        at = self.shard % seqs
        outs = []
        for step in range(seqs):
            route = self.owners(step, seqs)
            back = {}
            for s in range(self.shard_count):
                for z in range(self.replica_count // 2):
                    for c in range(2):
                        back[route(s, z, c)] = (s, z, c)
            outs.append(self.move(pieces[step], lambda s, z, c: back[(s, z, c)]))
        if seqs == 2:
            first = at == 0
            return jnp.stack(
                [jnp.where(first, outs[0], outs[1]), jnp.where(first, outs[1], outs[0])]
            )
        stacked = jnp.stack(outs)
        doubled = jnp.concatenate([stacked, stacked[: seqs - 1]], axis=0)
        return lax.dynamic_slice_in_dim(doubled, (seqs - at) % seqs, seqs, 0)

    def ordered(self, half, other):
        first = self.core == 0
        return jnp.concatenate(
            [jnp.where(first, half, other), jnp.where(first, other, half)], axis=1
        )


def shards(
    shard_count,
    replica_count,
    hidden_in,
    out_grad,
    segments,
    ln1_gain,
    ln1_bias,
    qkv_weight,
    q_bias,
    v_bias,
    output_projection_weight,
    out_bias,
    ln2_gain,
    ln2_bias,
    up_weight,
    up_bias,
    down_weight,
    down_bias,
):
    moves = Moves(shard_count, replica_count)
    core = moves.core
    quarter = 2 * (moves.column % 2) + core
    seqs = hidden_in.shape[1]
    width = hidden_in.shape[2]
    length = segments.shape[0]
    half_len = length // 2
    ff = up_bias.shape[0]
    strip = ff // shard_count // 4
    first_row = core * FIRST_HEAD * HDIM
    rows_of = functools.partial(lax.dynamic_slice_in_dim, slice_size=OWN, axis=0)

    def column(vector):
        return vector[:, None]


    counts = (qkv_weight.shape[0], output_projection_weight.shape[0])
    taken = tuple(to_sixteen(count // 2) for count in counts)
    mine_of = [
        lax.dynamic_slice_in_dim(weight, core * (count - rows), rows, 0)
        for weight, count, rows in zip((qkv_weight, output_projection_weight), counts, taken)
    ]
    ff_piece = jnp.concatenate(
        [
            lax.dynamic_slice_in_dim(up_weight, quarter * strip, strip, 0),
            jnp.concatenate(
                [
                    lax.dynamic_slice_in_dim(down_weight, (4 * shard + quarter) * strip, strip, 1)
                    for shard in range(shard_count)
                ],
                axis=1,
            ),
        ],
        axis=0,
    )
    up_bias_own = lax.dynamic_index_in_dim(
        up_bias.reshape(shard_count, 4, strip), quarter, 1, keepdims=False
    ).reshape(-1)
    tokens_came = moves.to_chips(hidden_in.transpose(1, 2, 0))
    if moves.square:
        heads_piece = jnp.concatenate(mine_of, axis=0)
        heads_x, heads_y = moves.over_x(heads_piece), moves.over_y(heads_piece)
        other_own = moves.over_core(heads_piece)
        events = [heads_x, heads_y, other_own, *tokens_came, ff_piece]

        heads_x, heads_y, segments_sent, *tokens_came = late(
            [heads_x, heads_y, segments, *tokens_came], events
        )
        split = to_sixteen(heads_piece.shape[0] // 2)
        heads_low = moves.over_x(heads_y[:split])
        heads_high = moves.over_y(heads_x[split:])
        other_x, other_y = moves.over_core(heads_x), moves.over_core(heads_y)
        segments_other = moves.over_core(segments_sent)
        events = [heads_low, heads_high, other_x, other_y, segments_other]
    else:
        segments_other = moves.over_core(segments)
        events = []
    at = (moves.shard % seqs).astype(jnp.int32)[None]
    tokens, normed_half = norm_in(at, tokens_came, column(ln1_gain), column(ln1_bias))
    events = [*events, normed_half]
    home = moves.shard // seqs
    seg = jnp.where(home == core, segments, segments_other)
    seg = lax.dynamic_index_in_dim(seg, moves.shard % seqs, 1, keepdims=False)

    out_grad, normed_half = late([out_grad, normed_half], events)
    if moves.square:
        heads_low, heads_high = late([heads_low, heads_high], events)
        other_low, other_high = moves.over_core(heads_low), moves.over_core(heads_high)
        events = [other_low, other_high]
    else:
        events = []
    normed_other = moves.over_core(normed_half)
    grad_came = moves.to_chips(out_grad.transpose(1, 2, 0))
    normed = moves.ordered(normed_half, normed_other)
    events = [*events, normed, *grad_came]

    ff_piece, normed, *grad_came = late([ff_piece, normed, *grad_came], events)
    if moves.square:
        ff_x, ff_y = moves.over_x(ff_piece), moves.over_y(ff_piece)
        w_qkv, w_out = lay_heads(
            moves.core_ref,
            moves.places,
            [heads_piece, heads_x, heads_y, heads_low, heads_high],
            [other_own, other_x, other_y, other_low, other_high],
            counts,
            taken,
            events,
        )
        events = [ff_x, ff_y]
    else:
        (qkv_half,) = moves.lay([mine_of[0]], ())
        qkv_other = moves.over_core(qkv_half)
        low = jnp.where(core == 0, qkv_half, qkv_other)
        high = jnp.where(core == 0, qkv_other, qkv_half)
        rows = taken[0]
        qkv_full = jnp.concatenate(
            [
                block[shard * rows + skip : (shard + 1) * rows]
                for shard in range(shard_count)
                for block, skip in ((low, 0), (high, 2 * rows - counts[0]))
            ],
            axis=0,
        )
        w_qkv = jnp.concatenate(
            [rows_of(qkv_full, part * width + first_row) for part in range(3)], axis=0
        )
        twice = (core == 1) & (jnp.arange(OWN) < HDIM)
        own = lax.dynamic_slice_in_dim(output_projection_weight, first_row, OWN, 1)
        (w_out,) = moves.lay([jnp.where(twice[None, :], 0, own).astype(BF16)], ())
        w_up, w_down = moves.lay([ff_piece], (), 2)
        events = []
    grad_half = moves.in_half(late(grad_came, [w_qkv]))
    grad_across = moves.over_z(grad_half, 1)
    zeros = jnp.zeros((OWN,), F32)
    joined_bias = jnp.concatenate([rows_of(q_bias, first_row), zeros, rows_of(v_bias, first_row)])
    row_scale = jnp.where(jnp.arange(3 * OWN) < OWN, 0.125, 1.0).astype(F32)
    joined = product(
        w_qkv,
        normed,
        "nn",
        416,
        lambda value, at, bias, scale: (
            (value + bias[...]).astype(BF16).astype(F32) * scale[...],
        ),
        (column(joined_bias), column(row_scale)),
        name="project_qkv",
    )
    mixed, lse = attention(seg, joined, [])
    side = jnp.broadcast_to(core.astype(F32), (width, 1))
    halves = ((half_len, BF16), (half_len, BF16))

    def by_side(value, at, side_ref):
        first, second = value[:, :half_len], value[:, half_len:]
        mine = side_ref[...] == 0
        return jnp.where(mine, first, second), jnp.where(mine, second, first)

    branch, branch_sent = product(
        w_out, mixed, "nn", 400, by_side, (side,), halves, name="project_out"
    )
    events = [*events, branch_sent, grad_across]

    branch_sent, grad_half, grad_across = late([branch_sent, grad_half, grad_across], events)
    branch_came = moves.over_core(branch_sent)
    grad_other, grad_far = moves.over_core(grad_half), moves.over_core(grad_across)
    middle, norm_half = norm_mid(
        tokens, branch, branch_came, column(out_bias), column(ln2_gain), column(ln2_bias)
    )
    events = [norm_half, grad_other, grad_far]
    if moves.square:
        split = ff_piece.shape[0] // 2
        ff_x, ff_y = late([ff_x, ff_y], [branch_sent])
        low_sent, high_sent = ff_y[:split], ff_x[split:]
        events = [*events, low_sent, high_sent]
    grad_out = [grad_half, grad_across, grad_other, grad_far]

    (norm_half,) = late([norm_half], events)
    norm_across = moves.over_z(norm_half, 1)
    norm_other = moves.over_core(norm_half)
    if moves.square:
        low_sent, high_sent = late([low_sent, high_sent], events)
        ff_low, ff_high = moves.over_x(low_sent), moves.over_y(high_sent)
        laid = lay_near(moves.places, late([ff_piece, ff_x, ff_y], events), 2)
        w_up, w_down = lay_far(moves.places, (ff_low, ff_high), laid)
        (norm_across,) = late([norm_across], [w_up])
    norm_far = moves.over_core(norm_across)
    normed_two = [norm_half, norm_across, norm_other, norm_far]

    activ, slope = product(
        w_up,
        normed_two,
        "nn",
        320,
        lambda value, at, bias: gelu_pair(value + bias[...]),
        (column(up_bias_own),),
        ((None, BF16), (None, BF16)),
        name="project_up",
        wait=grad_out,
    )

    def in_halves(value, at):
        half = value.shape[1] // 2
        return value[:, :half], value[:, half:]

    pairs = ((length, BF16), (length, BF16))

    def through_gelu(value, at, slope_ref):
        size = value.shape[1]
        slope_here = slope_ref[:, at * size : (at + 1) * size].astype(F32)
        grad = (value * slope_here).astype(BF16)
        sums = lane_sums(grad.astype(F32))
        return (grad, None, sums) if at < 2 else (None, grad, sums)

    ff_cut = 896 if width == 1600 else width // 256 * 128
    down_parts = moves.scatter_first([(grad_out, activ)], ff_cut)
    down_near = moves.scatter_near(down_parts)
    pre_here, pre_there, grad_pre_sums = product(
        w_down,
        grad_out,
        "tn",
        256,
        through_gelu,
        (slope,),
        (*pairs, (512, F32)),
        name="back_down",
        wait=down_parts[:1],
    )
    norm_there = product(w_up, pre_there, "tn", 256, name="back_up")

    norm_came = moves.over_core(norm_there)
    norm_here = product(
        w_up, pre_here, "tn", 256, name="back_up", wait=[norm_there, *down_near[1]]
    )
    events = [norm_came, norm_here]

    norm_came, norm_here = late([norm_came, norm_here], events)
    norm_last = moves.over_z(norm_here[:, half_len:] + norm_came[:, half_len:], 1)
    down_far = moves.scatter_far(down_near, events)
    down_here, down_there = product(
        w_down, activ, "nn", 320, in_halves, (), pairs, name="project_down", wait=events
    )
    up_parts = moves.scatter_first([([pre_here, pre_there], normed_two)], ff_cut, [down_there])
    events = [norm_last, *down_far[1], up_parts[0]]

    (norm_last,) = late([norm_last], events)
    grad_middle, grad_branch_half, mid_sums = norm_mid_back(
        (norm_here, norm_came, norm_last), middle, grad_half, column(ln2_gain), events
    )
    (down_part,) = late([moves.scatter_last(down_far, width)], [grad_branch_half])
    grad_branch = moves.ordered(grad_branch_half, moves.over_core(grad_branch_half))
    grad_mixed = product(w_out, grad_branch, "tn", OWN, name="back_out", wait=[down_part], share=0.01)
    upper = to_sixteen(down_part.shape[0] // 2)
    down_low, down_high = down_part[:upper], down_part[upper:]
    events = [grad_mixed, down_low, down_high]

    up_near = moves.scatter_near(up_parts, events)
    down_there, down_low, down_high = late([down_there, down_low, down_high], events)
    down_came = moves.over_core(down_there)
    down_come = [moves.alike(down_low)]
    grad_own = attention_back(seg, joined, mixed, grad_mixed, lse, events).reshape(3 * OWN, length)
    events = [*up_near[1], down_came, down_come[0], grad_own]

    (grad_own,) = late([grad_own], events)
    grad_heads = moves.over_core(grad_own)
    up_far = moves.scatter_far(up_near, events)
    (down_high,) = late([down_high], events)
    down_come.append(moves.alike(down_high))
    down_sent = down_here[:, half_len:] + down_came[:, half_len:]
    down_last = [moves.over_z(down_sent[:, : half_len // 2], 1)]
    padded = to_tiles(OWN)
    out_parts = moves.scatter_first([(grad_branch, mixed)], 512, events)
    norm_one, norm_one_sent = product(
        w_qkv, grad_own, "tn", 256, by_side, (side,), halves, name="back_qkv", wait=out_parts[:1]
    )
    events = [grad_heads, *up_far[1], down_come[1], norm_one_sent, down_last[0]]

    grad_heads, norm_one_sent = late([grad_heads, norm_one_sent], events)
    down_sum = moves.alike_sum(down_part, late(down_come, events))
    down_across = moves.over_z(down_sum, 1)
    down_sent = down_sent[:, half_len // 2 :]
    norm_one_came = moves.over_core(norm_one_sent)
    out_near = moves.scatter_near(out_parts, events)
    if moves.square:
        grad_rows = join_heads(
            moves.core_ref, grad_own, grad_heads, counts[0], taken[0], []
        )
    else:
        low = jnp.where(core == 0, grad_own, grad_heads)
        high = jnp.where(core == 0, grad_heads, grad_own)
        grad_joined = jnp.concatenate(
            [
                piece
                for part in range(3)
                for piece in (
                    low[part * OWN : (part + 1) * OWN],
                    high[part * OWN + HDIM : (part + 1) * OWN],
                )
            ],
            axis=0,
        )
        grad_rows = jnp.concatenate(
            [
                lax.dynamic_slice_in_dim(
                    grad_joined, shard * counts[0] + core * (counts[0] - taken[0]), taken[0], 0
                )
                for shard in range(shard_count)
            ],
            axis=0,
        )
    qkv_parts = moves.scatter_first([(grad_rows, normed)], ff_cut, events)
    events = [qkv_parts[0], norm_one_came, down_across, *out_near[1], down_sent]

    qkv_near = moves.scatter_near(qkv_parts, events)
    down_sent, norm_one_came = late([down_sent, norm_one_came], events)
    up_part = moves.scatter_last(up_far, width)
    (up_part,) = late([up_part], events)
    up_low, up_high = up_part[:upper], up_part[upper:]
    up_come = [moves.alike(up_low)]
    down_last.append(moves.over_z(down_sent, 1))
    input_half, in_sums = norm_in_back(
        (norm_one, norm_one_came), tokens, grad_middle, column(ln1_gain)
    )
    up_bias_grad = jnp.sum(grad_pre_sums, axis=1).reshape(shard_count, 1, strip)
    up_bias_grad = up_bias_grad * (jnp.arange(4)[None, :, None] == quarter).astype(F32)
    head_sums = jnp.sum(grad_own.astype(F32), axis=1).reshape(3, OWN)
    bias_sums = lax.dynamic_update_slice(
        jnp.zeros((3, width), F32), head_sums, (jnp.int32(0), first_row)
    )
    small = jnp.concatenate(
        [
            up_bias_grad.reshape(-1),
            jnp.sum(mid_sums, axis=2).reshape(-1),
            jnp.sum(in_sums, axis=2).reshape(-1),
            bias_sums[0],
            bias_sums[2],
        ]
    ).reshape(-1, 128)
    up_low_sum = moves.alike_sum(up_low, up_come)
    events = [*qkv_near[1], down_last[1], up_low_sum, input_half, small, up_high]

    qkv_far = moves.scatter_far(qkv_near, events)
    up_high, up_low_sum, small, *down_last = late(
        [up_high, up_low_sum, small, *down_last], events
    )
    down_last = jnp.concatenate(down_last, axis=1)
    up_come.append(moves.alike(up_high))
    up_across = [moves.over_z(up_low_sum, 1)]
    small = moves.small_cores(small)
    tokens_back = results(
        at, seqs, middle, (down_here, down_came, down_last), column(down_bias), input_half
    )
    events = [*qkv_far[1], up_come[1], up_across[0], small, *tokens_back]

    down_sum, down_across, small = late([down_sum, down_across, small], events)
    out_far = moves.scatter_far(out_near, events)
    small = moves.small_square(small)
    qkv_pair = moves.scatter_pair(qkv_far, width)
    out_part = moves.scatter_last(out_far, padded)
    down_other = moves.over_core(down_sum)
    down_far_other = moves.over_core(down_across)
    up_high_sum = moves.alike_sum(up_high, late(up_come[1:], events))
    out_halves = moves.halves(out_part) if moves.square else [out_part, out_part]
    events = [qkv_pair, *out_halves, down_other, down_far_other, up_high_sum, small]

    qkv_pair, up_high_sum, down_far_other, *out_halves = late(
        [qkv_pair, up_high_sum, down_far_other, *out_halves], events
    )
    tokens_back = late(tokens_back, events)
    qkv_full = moves.total_all(qkv_pair)
    up_across.append(moves.over_z(up_high_sum, 1))
    up_sum = jnp.concatenate([up_low_sum, up_high_sum], axis=0)
    out_pair = out_halves[0]
    if moves.square:
        out_pair = out_pair + moves.over_z(out_halves[1], 1)
    tokens_came = moves.from_chips(tokens_back)
    quarter_ref = quarter.astype(jnp.int32)[None]
    down_total = finish_down(
        quarter_ref, [down_sum, down_other, down_across, down_far_other], shard_count
    )
    events = [qkv_full, up_across[1], tokens_came, down_total, up_sum, out_pair]

    qkv_full, out_pair, up_sum, small, tokens_came, *up_across = late(
        [qkv_full, out_pair, up_sum, small, tokens_came, *up_across], events
    )
    qkv_sum = moves.total_halves(qkv_full)
    out_full = moves.total_all(out_pair)
    small = moves.small_columns(small, 1)
    up_across = jnp.concatenate(up_across, axis=0)
    up_parts = [up_sum, moves.over_core(up_sum), up_across, moves.over_core(up_across)]
    events = [*qkv_sum, out_full, *up_parts, small]

    (out_full,) = late([out_full], events)
    out_sum = moves.total_halves(out_full)
    small = moves.small_columns(late([small], events)[0], 2).reshape(-1)
    qkv_sum = moves.four(late(qkv_sum, events))
    up_total = finish_up(quarter_ref, late(up_parts, events))
    qkv_total = moves.rows(late(qkv_sum, [up_total]), counts[0])
    out_sum = moves.four(late(out_sum, [up_total]))
    out_total = moves.sides(late(out_sum, [qkv_total]))
    (tokens_came,) = late([tokens_came], [up_total])
    result, input_grad = tokens_came[:, :width], tokens_came[:, width:].astype(F32)

    up_bias_grad, rest = small[:ff], small[ff:]
    (
        ln2_gain_grad,
        ln2_bias_grad,
        down_bias_grad,
        out_bias_grad,
        ln1_gain_grad,
        ln1_bias_grad,
        q_bias_grad,
        v_bias_grad,
    ) = rest.reshape(8, width)

    return (
        result.transpose(2, 0, 1),
        input_grad.transpose(2, 0, 1),
        ln1_gain_grad,
        ln1_bias_grad,
        qkv_total,
        q_bias_grad,
        v_bias_grad,
        out_total,
        out_bias_grad,
        ln2_gain_grad,
        ln2_bias_grad,
        up_total,
        up_bias_grad,
        down_total,
        down_bias_grad,
    )


def solution(mesh):
    rows = P("shard", None)
    tokens = P("shard", "replica", None)
    in_specs = (
        tokens,
        tokens,
        P(None, "replica"),
        P(),
        P(),
        rows,
        P(),
        P(),
        rows,
        P(),
        P(),
        P(),
        rows,
        P(),
        rows,
        P(),
    )
    out_specs = (
        tokens,
        tokens,
        P(),
        P(),
        rows,
        P(),
        P(),
        rows,
        P(),
        P(),
        P(),
        rows,
        P(),
        rows,
        P(),
    )
    body = functools.partial(shards, mesh.shape["shard"], mesh.shape["replica"])
    return jax.shard_map(body, mesh=mesh, in_specs=in_specs, out_specs=out_specs, check_vma=False)
```

```python
import functools

import jax
import jax.numpy as jnp
from jax import lax
from jax.experimental import pallas as pl
from jax.experimental.pallas import tpu as pltpu
from jax.sharding import PartitionSpec as P

HEADS = 25
HDIM = 64
OWN_HEADS = HEADS // 2 + 1
FIRST_HEAD = HEADS // 2
OWN = OWN_HEADS * HDIM
BLOCK = 256
AXES = ("shard", "replica")
BF16 = jnp.bfloat16
F32 = jnp.float32


def dot(left, right, left_dim, right_dim):
    return lax.dot_general(
        left, right, (((left_dim,), (right_dim,)), ((), ())), preferred_element_type=F32
    )


COST_SCALE = 8


def cost(flops, bytes_accessed, share=1.0):
    return pl.CostEstimate(
        flops=int(flops * COST_SCALE * share),
        bytes_accessed=int(bytes_accessed * COST_SCALE * share),
        transcendentals=0,
    )


def gelu_pair(value):
    root = 0.7978845608028654
    cube = 0.044715
    square = value * value
    tanh = jnp.tanh(root * value * (1.0 + cube * square))
    half = 0.5 * (1.0 + tanh)
    slope = half + 0.5 * value * (1.0 - tanh * tanh) * root * (1.0 + 3.0 * cube * square)
    return value * half, slope


def fill_mask(seg_row, seg_col, mask, blocks):
    for q_at in range(blocks):
        for k_at in range(q_at + 1):
            keys = seg_col[pl.ds(k_at * BLOCK, BLOCK), :]
            queries = seg_row[:, pl.ds(q_at * BLOCK, BLOCK)]
            seen = keys == queries
            if k_at == q_at:
                k_place = lax.broadcasted_iota(jnp.int32, (BLOCK, BLOCK), 0)
                q_place = lax.broadcasted_iota(jnp.int32, (BLOCK, BLOCK), 1)
                seen = seen & (k_place <= q_place)
            mask[pl.ds(k_at * BLOCK, BLOCK), pl.ds(q_at * BLOCK, BLOCK)] = jnp.where(
                seen, 0.0, -1e30
            )


def forward_kernel(seg_row, seg_col, q_ref, k_ref, v_ref, *refs):
    o_ref, lse_ref, mask = refs[-3:]
    length = q_ref.shape[1]
    blocks = length // BLOCK

    @pl.when(pl.program_id(0) == 0)
    def _():
        fill_mask(seg_row, seg_col, mask, blocks)

    keys = k_ref[...].T
    for q_at in range(blocks):
        span = (q_at + 1) * BLOCK
        here = pl.ds(q_at * BLOCK, BLOCK)
        scores = dot(keys[:span], q_ref[:, here], 1, 0) + mask[:span, here]
        peak = jnp.max(scores, axis=0, keepdims=True)
        terms = jnp.exp(scores - peak)
        total = jnp.sum(terms, axis=0, keepdims=True)
        mixed = dot(v_ref[:, :span], terms.astype(BF16), 1, 0)
        o_ref[:, here] = (mixed / total).astype(BF16)
        lse_ref[0, :, here] = peak + jnp.log(total)


def backward_kernel(seg_row, seg_col, q_ref, k_ref, v_ref, o_ref, g_ref, lse_ref, *refs):
    grads, mask, acc = refs[-3:]
    length = q_ref.shape[1]
    blocks = length // BLOCK

    @pl.when(pl.program_id(0) == 0)
    def _():
        fill_mask(seg_row, seg_col, mask, blocks)

    keys = k_ref[...].T
    values = v_ref[...].T
    delta = jnp.sum(g_ref[...].astype(F32) * o_ref[...].astype(F32), axis=0, keepdims=True)
    lse = lse_ref[0]
    for k_at in range(blocks):
        low = k_at * BLOCK
        here = pl.ds(low, BLOCK)
        rest = pl.ds(low, length - low)
        scores = dot(keys[low : low + BLOCK], q_ref[:, rest], 1, 0) + mask[here, rest]
        soft = jnp.exp(scores - lse[:, low:])
        soft_grad = dot(values[low : low + BLOCK], g_ref[:, rest], 1, 0)
        score_grad = (soft * (soft_grad - delta[:, low:])).astype(BF16)
        grads[2, :, here] = dot(g_ref[:, rest], soft.astype(BF16), 1, 1).astype(BF16)
        grads[1, :, here] = dot(q_ref[:, rest], score_grad, 1, 1).astype(BF16)
        grad_q = dot(k_ref[:, here], score_grad, 1, 0)
        if k_at == 0:
            acc[...] = grad_q
        else:
            acc[:, rest] += grad_q
    grads[0] = (acc[...] * 0.125).astype(BF16)


def head_spec(first, length):
    return pl.BlockSpec((HDIM, length), lambda head: (first + head, 0))


def whole_spec(shape):
    return pl.BlockSpec(shape, lambda head: (0,) * len(shape))


def attention(seg, joined, wait):
    length = seg.shape[0]
    lse_spec = pl.BlockSpec((1, 1, length), lambda head: (head, 0, 0))
    pairs = OWN_HEADS * length * length
    return pl.pallas_call(
        forward_kernel,
        grid=(OWN_HEADS,),
        in_specs=[whole_spec((1, length)), whole_spec((length, 1))]
        + [head_spec(part * OWN_HEADS, length) for part in range(3)]
        + [pl.BlockSpec(memory_space=pl.ANY)] * len(wait),
        out_specs=[head_spec(0, length), lse_spec],
        out_shape=[
            jax.ShapeDtypeStruct((OWN, length), BF16),
            jax.ShapeDtypeStruct((OWN_HEADS, 1, length), F32),
        ],
        scratch_shapes=[pltpu.VMEM((length, length), F32)],
        compiler_params=pltpu.CompilerParams(vmem_limit_bytes=40 * 2**20),
        cost_estimate=cost(16 * pairs * HDIM, 8 * OWN * length),
        name="attention_forward",
    )(seg.reshape(1, length), seg.reshape(length, 1), joined, joined, joined, *wait)


def attention_back(seg, joined, mixed, grad, lse, wait):
    length = seg.shape[0]
    lse_spec = pl.BlockSpec((1, 1, length), lambda head: (head, 0, 0))
    pairs = OWN_HEADS * length * length
    return pl.pallas_call(
        backward_kernel,
        grid=(OWN_HEADS,),
        in_specs=[whole_spec((1, length)), whole_spec((length, 1))]
        + [head_spec(part * OWN_HEADS, length) for part in range(3)]
        + [head_spec(0, length), head_spec(0, length), lse_spec]
        + [pl.BlockSpec(memory_space=pl.ANY)] * len(wait),
        out_specs=pl.BlockSpec((3, HDIM, length), lambda head: (0, head, 0)),
        out_shape=jax.ShapeDtypeStruct((3, OWN, length), BF16),
        scratch_shapes=[pltpu.VMEM((length, length), F32), pltpu.VMEM((HDIM, length), F32)],
        compiler_params=pltpu.CompilerParams(vmem_limit_bytes=48 * 2**20),
        cost_estimate=cost(40 * pairs * HDIM, 16 * OWN * length),
        name="attention_backward",
    )(
        seg.reshape(1, length),
        seg.reshape(length, 1),
        joined,
        joined,
        joined,
        mixed,
        grad,
        lse,
        *wait,
    )


def product(left, rights, form, block, finish=None, extras=(), outs=((None, BF16),), name="product",
            wait=(), share=1.0):
    rights = rights if isinstance(rights, (list, tuple)) else [rights]
    many = len(rights)
    left_dim, right_dim = (0 if form == "tn" else 1), (1 if form == "nt" else 0)
    m, k = left.shape[1 - left_dim], left.shape[left_dim]
    size = rights[0].shape[1 - right_dim]
    n = size * many
    block = min(block, m)

    def body(left_ref, *refs):
        extra_refs = refs[many : many + len(extras)]
        out_refs = refs[many + len(extras) + len(wait) :]
        for at in range(many):
            value = dot(left_ref[...], refs[at][...], left_dim, right_dim)
            values = (value,)
            if finish is not None:
                values = finish(value, at, *extra_refs)
            for ref, part in zip(out_refs, values):
                if part is not None:
                    width = part.shape[1]
                    begin = at * width % ref.shape[1]
                    ref[:, begin : begin + width] = part.astype(ref.dtype)

    if form == "tn":
        left_spec = pl.BlockSpec((k, block), lambda i: (0, i))
    else:
        left_spec = pl.BlockSpec((block, k), lambda i: (i, 0))
    sizes = [(columns or n, kind) for columns, kind in outs]
    results = pl.pallas_call(
        body,
        grid=(pl.cdiv(m, block),),
        in_specs=[left_spec]
        + [
            pl.BlockSpec(right.shape, lambda i: (0, 0), pipeline_mode=pl.Buffered(1))
            for right in rights
        ]
        + [pl.BlockSpec((block, extra.shape[1]), lambda i: (i, 0)) for extra in extras]
        + [pl.BlockSpec(memory_space=pl.ANY)] * len(wait),
        out_specs=[pl.BlockSpec((block, columns), lambda i: (i, 0)) for columns, _ in sizes],
        out_shape=[jax.ShapeDtypeStruct((m, columns), kind) for columns, kind in sizes],
        compiler_params=pltpu.CompilerParams(vmem_limit_bytes=56 * 2**20),
        cost_estimate=cost(2 * m * n * k, 2 * (m * k + n * k + m * n), share),
        name=name,
    )(left, *rights, *extras, *wait)
    return results if len(outs) > 1 else results[0]


def lane_sums(value):
    return sum(value[:, at : at + 128] for at in range(0, value.shape[1], 128))


PARAMS = pltpu.CompilerParams(vmem_limit_bytes=56 * 2**20)


def norm_parts(rows):
    centre = rows - jnp.mean(rows, axis=0, keepdims=True)
    scale = lax.rsqrt(jnp.mean(centre * centre, axis=0, keepdims=True) + 1e-05)
    return centre * scale, scale


def norm_back(grad, unit, scale, gain):
    inner = grad * gain
    mean_inner = jnp.mean(inner, axis=0, keepdims=True)
    mean_cross = jnp.mean(inner * unit, axis=0, keepdims=True)
    return scale * (inner - mean_inner - unit * mean_cross)


def column_specs(shape, size, many):
    return [pl.BlockSpec((shape[0], size), lambda i, *_: (0, i))] * many


def fixed_specs(shape, many):
    return [pl.BlockSpec(shape, lambda i, *_: (0,) * len(shape))] * many


def norm_in(at, came, gain, bias):
    pieces = len(came)
    rows, count = came[0].shape

    def body(at_ref, *refs):
        gain_ref, bias_ref, tokens_ref, norm_ref = refs[pieces:]
        which = lax.rem(at_ref[0] - pl.program_id(0) + pieces, pieces)
        for piece in range(pieces):

            @pl.when(which == piece)
            def _(piece=piece):
                tokens_ref[...] = refs[piece][...]

        unit, _ = norm_parts(tokens_ref[...].astype(F32))
        norm_ref[...] = (unit * gain_ref[...] + bias_ref[...]).astype(BF16)

    return pl.pallas_call(
        body,
        grid_spec=pltpu.PrefetchScalarGridSpec(
            num_scalar_prefetch=1,
            grid=(pieces,),
            in_specs=fixed_specs((rows, count), pieces) + fixed_specs((rows, 1), 2),
            out_specs=column_specs((rows, pieces * count), count, 2),
        ),
        out_shape=[jax.ShapeDtypeStruct((rows, pieces * count), BF16)] * 2,
        compiler_params=PARAMS,
        cost_estimate=cost(0, 40 * rows * pieces * count),
        name="norm_in",
    )(at, *came, gain, bias)


def norm_mid(tokens, mine, came, shift, gain, bias):
    rows, columns = tokens.shape
    size = columns // 2

    def body(tokens_ref, mine_ref, came_ref, shift_ref, gain_ref, bias_ref, middle_ref, norm_ref):
        middle = mine_ref[...].astype(F32) + came_ref[...].astype(F32)
        middle = tokens_ref[...].astype(F32) + middle + shift_ref[...]
        middle_ref[...] = middle
        unit, _ = norm_parts(middle)
        norm_ref[...] = (unit * gain_ref[...] + bias_ref[...]).astype(BF16)

    return pl.pallas_call(
        body,
        grid=(2,),
        in_specs=column_specs((rows, columns), size, 3) + fixed_specs((rows, 1), 3),
        out_specs=column_specs((rows, columns), size, 2),
        out_shape=[
            jax.ShapeDtypeStruct((rows, columns), F32),
            jax.ShapeDtypeStruct((rows, columns), BF16),
        ],
        compiler_params=PARAMS,
        cost_estimate=cost(0, 40 * rows * columns),
        name="norm_mid",
    )(tokens, mine, came, shift, gain, bias)


def norm_mid_back(parts, middle, grad, gain, wait):
    rows, columns = middle.shape
    size = columns // 2
    many = len(parts)

    def body(*refs):
        middle_ref, grad_ref, gain_ref = refs[many : many + 3]
        out_ref, low_ref, sums_ref = refs[-3:]
        norm_grad = sum(ref[...].astype(F32) for ref in refs[:many])
        unit, scale = norm_parts(middle_ref[...])
        through = grad_ref[...].astype(F32)
        value = through + norm_back(norm_grad, unit, scale, gain_ref[...])
        out_ref[...] = value
        low_ref[...] = value.astype(BF16)
        sums = (norm_grad * unit, norm_grad, through, value.astype(BF16).astype(F32))
        for at, rows_of_sum in enumerate(sums):
            here = lane_sums(rows_of_sum)

            @pl.when(pl.program_id(0) == 0)
            def _(at=at, here=here):
                sums_ref[at] = here

            @pl.when(pl.program_id(0) > 0)
            def _(at=at, here=here):
                sums_ref[at] += here

    return pl.pallas_call(
        body,
        grid=(2,),
        in_specs=column_specs((rows, columns), size, many + 2)
        + fixed_specs((rows, 1), 1)
        + [pl.BlockSpec(memory_space=pl.ANY)] * len(wait),
        out_specs=column_specs((rows, columns), size, 2) + fixed_specs((4, rows, 128), 1),
        out_shape=[
            jax.ShapeDtypeStruct((rows, columns), F32),
            jax.ShapeDtypeStruct((rows, columns), BF16),
            jax.ShapeDtypeStruct((4, rows, 128), F32),
        ],
        compiler_params=PARAMS,
        cost_estimate=cost(0, 60 * rows * columns),
        name="norm_mid_back",
    )(*parts, middle, grad, gain, *wait)


def norm_in_back(parts, tokens, grad, gain):
    rows, columns = tokens.shape
    size = columns // 2
    many = len(parts)

    def body(*refs):
        tokens_ref, grad_ref, gain_ref, out_ref, sums_ref = refs[many:]
        norm_grad = sum(ref[...].astype(F32) for ref in refs[:many])
        unit, scale = norm_parts(tokens_ref[...].astype(F32))
        value = grad_ref[...] + norm_back(norm_grad, unit, scale, gain_ref[...])
        out_ref[...] = value.astype(BF16)
        for at, rows_of_sum in enumerate((norm_grad * unit, norm_grad)):
            here = lane_sums(rows_of_sum)

            @pl.when(pl.program_id(0) == 0)
            def _(at=at, here=here):
                sums_ref[at] = here

            @pl.when(pl.program_id(0) > 0)
            def _(at=at, here=here):
                sums_ref[at] += here

    return pl.pallas_call(
        body,
        grid=(2,),
        in_specs=column_specs((rows, columns), size, many + 2) + fixed_specs((rows, 1), 1),
        out_specs=column_specs((rows, columns), size, 1) + fixed_specs((2, rows, 128), 1),
        out_shape=[
            jax.ShapeDtypeStruct((rows, columns), BF16),
            jax.ShapeDtypeStruct((2, rows, 128), F32),
        ],
        compiler_params=PARAMS,
        cost_estimate=cost(0, 60 * rows * columns),
        name="norm_in_back",
    )(*parts, tokens, grad, gain)


def results(at, pieces, middle, parts, shift, input_half):
    rows, columns = middle.shape
    size = columns // pieces
    many = len(parts)

    def body(at_ref, middle_ref, *refs):
        shift_ref, input_ref = refs[many : many + 2]
        outs = refs[many + 2 :]
        value = middle_ref[...] + shift_ref[...]
        for ref in refs[:many]:
            value = value + ref[...].astype(F32)
        value = value.astype(BF16)
        which = lax.rem(at_ref[0] - pl.program_id(0) + pieces, pieces)
        for piece, out in enumerate(outs):

            @pl.when(which == piece)
            def _(out=out):
                out[:rows] = value
                out[rows:] = input_ref[...]

    block = column_specs((rows, columns), size, 1)
    return pl.pallas_call(
        body,
        grid_spec=pltpu.PrefetchScalarGridSpec(
            num_scalar_prefetch=1,
            grid=(pieces,),
            in_specs=block * (1 + many) + fixed_specs((rows, 1), 1) + block,
            out_specs=fixed_specs((2 * rows, size), pieces),
        ),
        out_shape=[jax.ShapeDtypeStruct((2 * rows, size), BF16)] * pieces,
        compiler_params=PARAMS,
        cost_estimate=cost(0, 40 * rows * columns),
        name="results",
    )(at, middle, *parts, shift, input_half)


def lay(places, near, far, parts):
    count, columns = near[0].shape
    size = count // parts
    kind = near[0].dtype

    def body(places_ref, *refs):
        step = pl.program_id(0)
        outs = refs[5:]
        for at in range(3):

            @pl.when(step == at)
            def _(at=at):
                for index, out in enumerate(outs):
                    out[...] = refs[at][index * size : (index + 1) * size]

        @pl.when(step == 3)
        def _():
            start = 0
            for ref in refs[3:5]:
                rows = ref.shape[0]
                for index, out in enumerate(outs):
                    low, high = max(start, index * size), min(start + rows, (index + 1) * size)
                    if low < high:
                        out[low - index * size : high - index * size] = ref[
                            low - start : high - start
                        ]
                start += rows

    pieces = list(near) + list(far)
    return pl.pallas_call(
        body,
        grid_spec=pltpu.PrefetchScalarGridSpec(
            num_scalar_prefetch=1,
            grid=(4,),
            in_specs=[
                pl.BlockSpec(piece.shape, lambda i, p: (0, 0), pipeline_mode=pl.Buffered(1))
                for piece in pieces
            ],
            out_specs=[pl.BlockSpec((size, columns), lambda i, p: (p[i], 0))] * parts,
        ),
        out_shape=[jax.ShapeDtypeStruct((4 * size, columns), kind)] * parts,
        compiler_params=pltpu.CompilerParams(vmem_limit_bytes=56 * 2**20),
        cost_estimate=cost(0, 16 * count * columns),
        name="lay",
    )(places, *pieces)


def lay_near(places, near, parts):
    count, columns = near[0].shape
    size = count // parts

    def body(places_ref, *refs):
        for at in range(3):

            @pl.when(pl.program_id(0) == at)
            def _(at=at):
                for index, out in enumerate(refs[3:]):
                    out[...] = refs[at][index * size : (index + 1) * size]

    return pl.pallas_call(
        body,
        grid_spec=pltpu.PrefetchScalarGridSpec(
            num_scalar_prefetch=1,
            grid=(3,),
            in_specs=[
                pl.BlockSpec(piece.shape, lambda i, p: (0, 0), pipeline_mode=pl.Buffered(1))
                for piece in near
            ],
            out_specs=[pl.BlockSpec((size, columns), lambda i, p: (p[i], 0))] * parts,
        ),
        out_shape=[jax.ShapeDtypeStruct((4 * size, columns), near[0].dtype)] * parts,
        compiler_params=PARAMS,
        cost_estimate=cost(0, 12 * count * columns),
        name="lay_near",
    )(places, *near)


def lay_far(places, far, laid):
    parts = len(far)
    size, columns = far[0].shape

    def body(places_ref, *refs):
        for ref, out in zip(refs[:parts], refs[2 * parts :]):
            out[...] = ref[...]

    return pl.pallas_call(
        body,
        grid_spec=pltpu.PrefetchScalarGridSpec(
            num_scalar_prefetch=1,
            grid=(1,),
            in_specs=[pl.BlockSpec(piece.shape, lambda i, p: (0, 0)) for piece in far]
            + [pl.BlockSpec(memory_space=pl.ANY)] * parts,
            out_specs=[pl.BlockSpec((size, columns), lambda i, p: (p[3], 0))] * parts,
        ),
        out_shape=[jax.ShapeDtypeStruct(array.shape, array.dtype) for array in laid],
        input_output_aliases={1 + parts + index: index for index in range(parts)},
        compiler_params=PARAMS,
        cost_estimate=cost(0, 4 * size * columns),
        name="lay_far",
    )(places, *far, *laid)


def lay_heads(core, places, mine, others, counts, taken, wait):
    width = mine[0].shape[1]
    split = mine[3].shape[0]
    cut = FIRST_HEAD * HDIM

    def body(core_ref, places_ref, *refs):
        heads_ref, out_ref, block, out_block = refs[-4:]
        step = pl.program_id(0)

        def copy(halves, at, begin, end, target, row):
            if at < 3:
                target[row : row + end - begin] = halves[at][begin:end]
                return
            if begin < split:
                middle = min(end, split)
                target[row : row + middle - begin] = halves[3][begin:middle]
            if end > split:
                middle = max(begin, split)
                target[row + middle - begin : row + end - begin] = halves[4][
                    middle - split : end - split
                ]

        for which in range(2):

            @pl.when(core_ref[0] == which)
            def _(which=which):
                low, high = (refs[:5], refs[5:10]) if which == 0 else (refs[5:10], refs[:5])
                for at in range(4):

                    @pl.when(step == at)
                    def _(at=at):
                        begin = 0
                        for target, rows, count in zip((block, out_block), taken, counts):
                            copy(low, at, begin, begin + rows, target, 0)
                            over = 2 * rows - count
                            copy(high, at, begin + over, begin + rows, target, rows)
                            begin += rows

                out_ref[...] = out_block[:, which * cut : which * cut + OWN]
                if which == 1:
                    out_ref[:, :HDIM] = jnp.zeros((counts[1], HDIM), BF16)
                for shard in range(4):

                    @pl.when(places_ref[step] == shard)
                    def _(shard=shard):
                        for part in range(3):
                            begin = part * width + which * cut
                            first = max(begin, shard * counts[0])
                            last = min(begin + OWN, (shard + 1) * counts[0])
                            if first < last:
                                heads_ref[
                                    part * OWN + first - begin : part * OWN + last - begin
                                ] = block[first - shard * counts[0] : last - shard * counts[0]]

    pieces = list(mine) + list(others)
    return pl.pallas_call(
        body,
        grid_spec=pltpu.PrefetchScalarGridSpec(
            num_scalar_prefetch=2,
            grid=(4,),
            in_specs=[
                pl.BlockSpec(piece.shape, lambda i, c, p: (0, 0), pipeline_mode=pl.Buffered(1))
                for piece in pieces
            ]
            + [pl.BlockSpec(memory_space=pl.ANY)] * len(wait),
            out_specs=[
                pl.BlockSpec(
                    (3 * OWN, width), lambda i, c, p: (0, 0), pipeline_mode=pl.Buffered(1)
                ),
                pl.BlockSpec((counts[1], OWN), lambda i, c, p: (p[i], 0)),
            ],
            scratch_shapes=[pltpu.VMEM((count, width), BF16) for count in counts],
        ),
        out_shape=[
            jax.ShapeDtypeStruct((3 * OWN, width), BF16),
            jax.ShapeDtypeStruct((4 * counts[1], OWN), BF16),
        ],
        compiler_params=pltpu.CompilerParams(vmem_limit_bytes=56 * 2**20),
        cost_estimate=cost(0, 16 * counts[0] * width),
        name="lay_heads",
    )(core, places, *pieces, *wait)


def join_heads(core, own, other, count, taken, wait):
    length = own.shape[1]
    rows = 2 * OWN - HDIM

    def body(core_ref, own_ref, other_ref, *refs):
        out = refs[-1]
        step = pl.program_id(0)
        for which in range(2):
            for shard in range(4):

                @pl.when((core_ref[0] == which) & (step == shard))
                def _(which=which, shard=shard):
                    low, high = (own_ref, other_ref) if which == 0 else (other_ref, own_ref)
                    begin = shard * count + which * (count - taken)
                    at = begin
                    while at < begin + taken:
                        part, row = at // rows, at % rows
                        source, skip, last = (
                            (low, 0, OWN) if row < OWN else (high, OWN - HDIM, rows)
                        )
                        end = min(begin + taken, part * rows + last)
                        first = part * OWN + row - skip
                        out[at - begin : end - begin] = source[first : first + end - at]
                        at = end

    whole = pl.BlockSpec(own.shape, lambda i, c: (0, 0), pipeline_mode=pl.Buffered(1))
    return pl.pallas_call(
        body,
        grid_spec=pltpu.PrefetchScalarGridSpec(
            num_scalar_prefetch=1,
            grid=(4,),
            in_specs=[whole, whole] + [pl.BlockSpec(memory_space=pl.ANY)] * len(wait),
            out_specs=pl.BlockSpec((taken, length), lambda i, c: (i, 0)),
        ),
        out_shape=jax.ShapeDtypeStruct((4 * taken, length), BF16),
        compiler_params=pltpu.CompilerParams(vmem_limit_bytes=56 * 2**20),
        cost_estimate=cost(0, 12 * rows * length),
        name="join_heads",
    )(core, own, other, *wait)


def product_parts(order, pairs, cut, wait):
    many = len(pairs)
    lefts = [side_of(left) for left, _ in pairs]
    rights = [side_of(right) for _, right in pairs]
    count = lefts[0][0].shape[0] // 4
    depth = sum(piece.shape[1] for piece in lefts[0])
    columns = rights[0][0].shape[0]
    rest = columns - cut
    filled = to_tiles(rest)
    starts = [0]
    for sides in lefts + rights:
        starts.append(starts[-1] + len(sides))

    def body(order_ref, *refs):
        send_x, send_y, keep_x, keep_y = refs[starts[-1] + len(wait) :]
        step = pl.program_id(0)
        targets = ((send_x, send_y), (send_x, keep_y), (keep_x, send_y), (keep_x, keep_y))
        for pair in range(many):

            @pl.when(step // 4 == pair)
            def _(pair=pair):
                left = refs[starts[pair] : starts[pair + 1]]
                right = refs[starts[many + pair] : starts[many + pair + 1]]
                value = side_product(left, right).astype(BF16)
                for at, (along_x, along_y) in enumerate(targets):

                    @pl.when(step % 4 == at)
                    def _(along_x=along_x, along_y=along_y):
                        along_x[...] = value[:, :cut]
                        along_y[:, :rest] = value[:, cut:]
                        if filled > rest:
                            along_y[:, rest:] = jnp.zeros((count, filled - rest), BF16)

    def left_spec(pair, piece):
        return pl.BlockSpec(
            (count, piece.shape[1]), lambda i, o: (o[jnp.clip(i - 4 * pair, 0, 3)], 0)
        )

    def out_spec(size, second):
        return pl.BlockSpec(
            (count, size), lambda i, o: (jnp.where(i % 4 >= second, many, 0) + i // 4, 0)
        )

    return pl.pallas_call(
        body,
        grid_spec=pltpu.PrefetchScalarGridSpec(
            num_scalar_prefetch=1,
            grid=(4 * many,),
            in_specs=[left_spec(pair, piece) for pair in range(many) for piece in lefts[pair]]
            + [
                pl.BlockSpec(piece.shape, lambda i, o: (0, 0), pipeline_mode=pl.Buffered(1))
                for right in rights
                for piece in right
            ]
            + [pl.BlockSpec(memory_space=pl.ANY)] * len(wait),
            out_specs=[
                out_spec(cut, 1),
                out_spec(filled, 2),
                out_spec(cut, 3),
                out_spec(filled, 3),
            ],
        ),
        out_shape=[
            jax.ShapeDtypeStruct((2 * many * count, size), BF16)
            for size in (cut, filled, cut, filled)
        ],
        compiler_params=pltpu.CompilerParams(vmem_limit_bytes=56 * 2**20),
        cost_estimate=cost(8 * many * count * depth * columns, 8 * many * count * (depth + columns)),
        name="product_parts",
    )(order, *[piece for sides in lefts + rights for piece in sides], *wait)


def side_of(side):
    return list(side) if isinstance(side, (list, tuple)) else [side]


def side_product(left, right):
    total = None
    size = min(piece.shape[1] for piece in (*left, *right))
    depth = sum(piece.shape[1] for piece in left)

    def chunk(pieces, begin):
        width = pieces[0].shape[1]
        return pieces[begin // width][:, begin % width : begin % width + size]

    for begin in range(0, depth, size):
        value = dot(chunk(left, begin), chunk(right, begin), 1, 1)
        total = value if total is None else total + value
    return total


def to_tiles(count):
    return -(-count // 128) * 128


def fold(keep_x, came_x, last_x, keep_y, came_y, last_y, columns, even=None):
    rows, cut = last_x.shape
    filled = last_y.shape[1]
    rest = columns - cut
    block = 400 if even is None else rows // 2
    steps = rows // block

    def fill(refs, out):
        for first, begin, size in ((0, 0, cut), (3, cut, rest)):
            value = refs[first][:, :size].astype(F32) + refs[first + 1][:, :size].astype(F32)
            value = value + refs[first + 2][:, :size].astype(F32)
            out[:, begin : begin + size] = value.astype(BF16)

    def body(*refs):
        if even is None:
            fill(refs[:6], refs[6])
            return
        mine = pl.program_id(0) == refs[0][0]

        @pl.when(mine)
        def _():
            fill(refs[1:7], refs[7])

        @pl.when(jnp.logical_not(mine))
        def _():
            fill(refs[1:7], refs[8])

    def specs(size):
        second = pl.BlockSpec((block, size), lambda i, *_: (steps + i, 0))
        return [second, second, pl.BlockSpec((block, size), lambda i, *_: (i, 0))]

    if even is not None:
        return pl.pallas_call(
            body,
            grid_spec=pltpu.PrefetchScalarGridSpec(
                num_scalar_prefetch=1,
                grid=(2,),
                in_specs=specs(cut) + specs(filled),
                out_specs=fixed_specs((block, columns), 2),
            ),
            out_shape=[jax.ShapeDtypeStruct((block, columns), BF16)] * 2,
            compiler_params=PARAMS,
            cost_estimate=cost(0, 8 * rows * columns, 0.01),
            name="fold_halves",
        )(even, keep_x, came_x, last_x, keep_y, came_y, last_y)
    return pl.pallas_call(
        body,
        grid=(steps,),
        in_specs=specs(cut) + specs(filled),
        out_specs=pl.BlockSpec((block, columns), lambda i: (i, 0)),
        out_shape=jax.ShapeDtypeStruct((rows, columns), BF16),
        compiler_params=pltpu.CompilerParams(vmem_limit_bytes=56 * 2**20),
        cost_estimate=cost(0, 8 * rows * columns, 0.01),
        name="fold",
    )(keep_x, came_x, last_x, keep_y, came_y, last_y)


def finish_up(quarter, parts):
    rows, width = parts[0].shape

    def body(quarter_ref, *refs):
        for at in range(4):

            @pl.when(pl.program_id(0) == at)
            def _(at=at):
                refs[4][...] = refs[at][...].astype(F32)

    return pl.pallas_call(
        body,
        grid_spec=pltpu.PrefetchScalarGridSpec(
            num_scalar_prefetch=1,
            grid=(4,),
            in_specs=[
                pl.BlockSpec((rows, width), lambda i, q: (0, 0), pipeline_mode=pl.Buffered(1))
            ]
            * 4,
            out_specs=pl.BlockSpec((rows, width), lambda i, q: (q[0] ^ i, 0)),
        ),
        out_shape=jax.ShapeDtypeStruct((4 * rows, width), F32),
        compiler_params=pltpu.CompilerParams(vmem_limit_bytes=56 * 2**20),
        cost_estimate=cost(0, 24 * rows * width),
        name="finish_up",
    )(quarter, *parts)


def finish_down(quarter, parts, shard_count):
    rows, width = parts[0].shape
    strip = width // shard_count
    block = 80 if rows % 80 == 0 else 40
    steps = rows // block

    def body(quarter_ref, *refs):
        for which in range(4):

            @pl.when(quarter_ref[0] == which)
            def _(which=which):
                for shard in range(shard_count):
                    for at in range(4):
                        begin = (4 * shard + at) * strip
                        refs[4][:, begin : begin + strip] = refs[which ^ at][
                            :, shard * strip : (shard + 1) * strip
                        ].astype(F32)

    return pl.pallas_call(
        body,
        grid_spec=pltpu.PrefetchScalarGridSpec(
            num_scalar_prefetch=1,
            grid=(steps,),
            in_specs=[pl.BlockSpec((block, width), lambda i, q: (i, 0))] * 4,
            out_specs=pl.BlockSpec((block, 4 * width), lambda i, q: (i, 0)),
        ),
        out_shape=jax.ShapeDtypeStruct((rows, 4 * width), F32),
        compiler_params=pltpu.CompilerParams(vmem_limit_bytes=56 * 2**20),
        cost_estimate=cost(0, 24 * rows * width),
        name="finish_down",
    )(quarter, *parts)


def finish_sides(core, even, parts):
    rows, width = parts[0].shape
    cut = FIRST_HEAD * HDIM

    def body(core_ref, even_ref, *refs):
        for which in range(2):
            for at in range(2):

                @pl.when((core_ref[0] == which) & (pl.program_id(0) == at))
                def _(which=which, at=at):
                    own, other = refs[at], refs[2 + at]
                    low, high = (own, other) if which == 0 else (other, own)
                    refs[4][:, :cut] = low[:, :cut].astype(F32)
                    refs[4][:, cut:] = high[:, :OWN].astype(F32)

    return pl.pallas_call(
        body,
        grid_spec=pltpu.PrefetchScalarGridSpec(
            num_scalar_prefetch=2,
            grid=(2,),
            in_specs=[
                pl.BlockSpec((rows, width), lambda i, c, e: (0, 0), pipeline_mode=pl.Buffered(1))
            ]
            * 4,
            out_specs=pl.BlockSpec((rows, cut + OWN), lambda i, c, e: (e[0] ^ i, 0)),
        ),
        out_shape=jax.ShapeDtypeStruct((2 * rows, cut + OWN), F32),
        compiler_params=pltpu.CompilerParams(vmem_limit_bytes=56 * 2**20),
        cost_estimate=cost(0, 16 * rows * width),
        name="finish_sides",
    )(core, even, *parts)


def finish_rows(core, even, parts, count):
    rows, width = parts[0].shape
    over = 4 * rows - count

    def body(core_ref, even_ref, *refs):
        out = refs[4]
        for which in range(2):
            for parity in range(2):

                @pl.when((core_ref[0] == which) & (even_ref[0] == parity))
                def _(which=which, parity=parity):
                    mine = [refs[parity], refs[1 - parity]]
                    others = [refs[2 + parity], refs[3 - parity]]
                    low, high = (mine, others) if which == 0 else (others, mine)
                    for at in range(2):

                        @pl.when(pl.program_id(0) == at)
                        def _(at=at):
                            out[...] = low[at][...].astype(F32)

                    @pl.when(pl.program_id(0) == 2)
                    def _():
                        out[: rows - over] = high[0][over:].astype(F32)
                        out[rows - over :] = high[1][:over].astype(F32)

                    @pl.when(pl.program_id(0) == 3)
                    def _():
                        out[: rows - over] = high[1][over:].astype(F32)

    return pl.pallas_call(
        body,
        grid_spec=pltpu.PrefetchScalarGridSpec(
            num_scalar_prefetch=2,
            grid=(4,),
            in_specs=[
                pl.BlockSpec((rows, width), lambda i, c, e: (0, 0), pipeline_mode=pl.Buffered(1))
            ]
            * 4,
            out_specs=pl.BlockSpec((rows, width), lambda i, c, e: (i, 0)),
        ),
        out_shape=jax.ShapeDtypeStruct((count, width), F32),
        compiler_params=pltpu.CompilerParams(vmem_limit_bytes=56 * 2**20),
        cost_estimate=cost(0, 24 * rows * width),
        name="finish_rows",
    )(core, even, *parts)


def to_sixteen(count):
    return -(-count // 16) * 16


def late(arrays, events):
    arrays = list(arrays)
    events = [event for event in events if event is not None]
    if not events:
        return arrays
    return lax.optimization_barrier((*arrays, *events))[: len(arrays)]


class Moves:
    def __init__(self, shard_count, replica_count):
        self.shard_count = shard_count
        self.replica_count = replica_count
        self.shard = lax.axis_index("shard")
        replica = lax.axis_index("replica")
        self.core = replica % 2
        self.column = replica // 2
        self.square = shard_count == 4 and replica_count == 8
        self.core_ref = self.core.astype(jnp.int32)[None]
        me = self.shard
        self.places = jnp.stack([me, me ^ 1, me ^ 2, me ^ 3]).astype(jnp.int32)
        self.order = jnp.stack([me ^ 3, me ^ 1, me ^ 2, me]).astype(jnp.int32)

    def move(self, array, route):
        pairs, stays = [], []
        for shard in range(self.shard_count):
            for column in range(self.replica_count // 2):
                for core in range(2):
                    target = route(shard, column, core)
                    if target == (shard, column, core):
                        stays.append((shard, core))
                    elif target is not None:
                        to_shard, to_column, to_core = target
                        pairs.append(
                            (
                                shard * self.replica_count + 2 * column + core,
                                to_shard * self.replica_count + 2 * to_column + to_core,
                            )
                        )
        came = lax.ppermute(array, AXES, pairs)
        if not stays:
            return came
        table = [(s, c) in stays for s in range(self.shard_count) for c in range(2)]
        return jnp.where(jnp.asarray(table)[2 * self.shard + self.core], array, came)

    def over_x(self, array):
        return self.move(array, lambda s, z, c: (s ^ 1, z, c))

    def over_y(self, array):
        return self.move(array, lambda s, z, c: (s ^ 2, z, c))

    def over_z(self, array, step):
        return self.move(array, lambda s, z, c: (s, z ^ step, c))

    def over_core(self, array):
        return self.move(array, lambda s, z, c: (s, z, 1 - c))

    def lay(self, near, far, parts=1):
        if self.square:
            return lay(self.places, near, far, parts)
        size = near[0].shape[0] // parts
        return [
            lax.all_gather(near[0][at * size : (at + 1) * size], "shard", axis=0, tiled=True)
            for at in range(parts)
        ]

    def scatter_first(self, pairs, cut, wait=()):
        if not self.square:
            return [
                product(
                    jnp.concatenate(side_of(left), axis=1),
                    jnp.concatenate(side_of(right), axis=1),
                    "nt",
                    400,
                )
                for left, right in pairs
            ]
        return product_parts(self.order, pairs, cut, wait)

    def scatter_near(self, parts, wait=()):
        if not self.square:
            return parts, []
        send_x, send_y = late(parts[:2], wait)
        return parts, [self.over_x(send_x), self.over_y(send_y)]

    def scatter_far(self, near, wait=()):
        parts, came = near
        if not self.square:
            return near, [], []
        keep_x, keep_y = parts[2:]
        half = keep_x.shape[0] // 2
        came_x, came_y = late(came, wait)
        sent_x, sent_y = keep_x[:half] + came_x[:half], keep_y[:half] + came_y[:half]
        return near, [self.over_y(sent_x), self.over_x(sent_y)], [sent_x, sent_y]

    def scatter_last(self, far, columns):
        (parts, came), last, _ = far
        if not self.square:
            sums = [
                lax.psum_scatter(part, "shard", scatter_dimension=0, tiled=True) for part in parts
            ]
            return jnp.concatenate(sums, axis=0)
        return fold(parts[2], came[0], last[0], parts[3], came[1], last[1], columns)

    def scatter_pair(self, far, columns):
        (parts, came), last, _ = far
        if not self.square:
            return self.scatter_last(far, columns)
        even = (self.column % 2).astype(jnp.int32)[None]
        keep, send = fold(parts[2], came[0], last[0], parts[3], came[1], last[1], columns, even)
        return keep + self.over_z(send, 1)

    def halves(self, array):
        rows = array.shape[0] // 2
        even = self.column % 2
        keep = lax.dynamic_slice_in_dim(array, even * rows, rows, 0)
        return keep, lax.dynamic_slice_in_dim(array, (1 - even) * rows, rows, 0)

    def total_all(self, pair):
        if not self.square:
            groups = [
                [2 * column + core for column in range(self.replica_count // 2)]
                for core in range(2)
            ]
            return lax.psum(pair, "replica", axis_index_groups=groups)
        return pair + self.over_z(pair, 2)

    def total_halves(self, full):
        return (full, self.over_z(full, 1)) if self.square else (full,)

    def four(self, sums):
        return list(sums) + [self.over_core(half) for half in sums]

    def sides(self, parts):
        even = (self.column % 2).astype(jnp.int32)[None]
        if self.square:
            return finish_sides(self.core_ref, even, parts)
        first = self.core == 0
        low, high = jnp.where(first, *parts), jnp.where(first, *parts[::-1])
        return jnp.concatenate([low[:, : FIRST_HEAD * HDIM], high[:, :OWN]], axis=1).astype(F32)

    def rows(self, parts, count):
        if self.square:
            even = (self.column % 2).astype(jnp.int32)[None]
            return finish_rows(self.core_ref, even, parts, count)
        first = self.core == 0
        low, high = jnp.where(first, *parts), jnp.where(first, *parts[::-1])
        return jnp.concatenate([low, high[2 * low.shape[0] - count :]], axis=0).astype(F32)

    def alike(self, array):
        return self.over_z(array, 2) if self.square else self.total_alike(array)

    def alike_sum(self, array, came):
        came = jnp.concatenate(came, axis=0)
        return array + came if self.square else came

    def total_alike(self, array):
        groups = [
            [2 * column + core for column in range(even, self.replica_count // 2, 2)]
            for even in range(2)
            for core in range(2)
        ]
        return lax.psum(array, "replica", axis_index_groups=groups)

    def small_cores(self, array):
        return array + self.over_core(array) if self.square else lax.psum(array, AXES)

    def small_square(self, array):
        if not self.square:
            return array
        array = array + self.over_x(array)
        return array + self.over_y(array)

    def small_columns(self, array, step):
        return array + self.over_z(array, step) if self.square else array

    def owners(self, step, seqs):
        return lambda s, z, c: (seqs * c + (s + step) % seqs, z, s // seqs)

    def pieces(self, local):
        seqs = local.shape[0]
        return [
            lax.dynamic_index_in_dim(local, (self.shard + step) % seqs, 0, keepdims=False)
            for step in range(seqs)
        ]

    def to_chips(self, pieces):
        seqs = len(pieces)
        return [
            self.move(piece, self.owners(step, seqs)) for step, piece in enumerate(pieces)
        ]

    def in_half(self, came):
        seqs = len(came)
        count = came[0].shape[1]
        at = self.shard % seqs
        if seqs == 2:
            first = at == 0
            return jnp.concatenate(
                [jnp.where(first, came[0], came[1]), jnp.where(first, came[1], came[0])], axis=1
            )
        ring = jnp.concatenate((came[::-1] * 2)[: 2 * seqs - 1], axis=1)
        return lax.dynamic_slice_in_dim(ring, (seqs - 1 - at) * count, seqs * count, 1)

    def from_chips(self, pieces):
        seqs = len(pieces)
        at = self.shard % seqs
        outs = []
        for step in range(seqs):
            route = self.owners(step, seqs)
            back = {}
            for s in range(self.shard_count):
                for z in range(self.replica_count // 2):
                    for c in range(2):
                        back[route(s, z, c)] = (s, z, c)
            outs.append(self.move(pieces[step], lambda s, z, c: back[(s, z, c)]))
        if seqs == 2:
            first = at == 0
            return jnp.stack(
                [jnp.where(first, outs[0], outs[1]), jnp.where(first, outs[1], outs[0])]
            )
        stacked = jnp.stack(outs)
        doubled = jnp.concatenate([stacked, stacked[: seqs - 1]], axis=0)
        return lax.dynamic_slice_in_dim(doubled, (seqs - at) % seqs, seqs, 0)

    def ordered(self, half, other):
        first = self.core == 0
        return jnp.concatenate(
            [jnp.where(first, half, other), jnp.where(first, other, half)], axis=1
        )


def shards(
    shard_count,
    replica_count,
    hidden_in,
    out_grad,
    segments,
    ln1_gain,
    ln1_bias,
    qkv_weight,
    q_bias,
    v_bias,
    output_projection_weight,
    out_bias,
    ln2_gain,
    ln2_bias,
    up_weight,
    up_bias,
    down_weight,
    down_bias,
):
    moves = Moves(shard_count, replica_count)
    core = moves.core
    quarter = 2 * (moves.column % 2) + core
    seqs = hidden_in.shape[1]
    width = hidden_in.shape[2]
    length = segments.shape[0]
    half_len = length // 2
    ff = up_bias.shape[0]
    strip = ff // shard_count // 4
    first_row = core * FIRST_HEAD * HDIM
    rows_of = functools.partial(lax.dynamic_slice_in_dim, slice_size=OWN, axis=0)

    def column(vector):
        return vector[:, None]


    counts = (qkv_weight.shape[0], output_projection_weight.shape[0])
    taken = tuple(to_sixteen(count // 2) for count in counts)
    mine_of = [
        lax.dynamic_slice_in_dim(weight, core * (count - rows), rows, 0)
        for weight, count, rows in zip((qkv_weight, output_projection_weight), counts, taken)
    ]
    ff_piece = [
        lax.dynamic_slice_in_dim(up_weight, quarter * strip, strip, 0),
        jnp.concatenate(
            [
                lax.dynamic_slice_in_dim(down_weight, (4 * shard + quarter) * strip, strip, 1)
                for shard in range(shard_count)
            ],
            axis=1,
        ),
    ]
    up_bias_own = lax.dynamic_index_in_dim(
        up_bias.reshape(shard_count, 4, strip), quarter, 1, keepdims=False
    ).reshape(-1)
    tokens_came = moves.to_chips(moves.pieces(hidden_in.transpose(1, 2, 0)))
    grad_pieces = moves.pieces(out_grad.transpose(1, 2, 0))
    if moves.square:
        heads_piece = jnp.concatenate(mine_of, axis=0)
        heads_x, heads_y = moves.over_x(heads_piece), moves.over_y(heads_piece)
        other_own = moves.over_core(heads_piece)
        events = [heads_x, heads_y, other_own, *tokens_came, *ff_piece, *grad_pieces]

        heads_x, heads_y, segments_sent, *tokens_came = late(
            [heads_x, heads_y, segments, *tokens_came], events
        )
        split = to_sixteen(heads_piece.shape[0] // 2)
        heads_low = moves.over_x(heads_y[:split])
        heads_high = moves.over_y(heads_x[split:])
        other_x, other_y = moves.over_core(heads_x), moves.over_core(heads_y)
        segments_other = moves.over_core(segments_sent)
        events = [heads_low, heads_high, other_x, other_y, segments_other]
    else:
        segments_other = moves.over_core(segments)
        events = []
    at = (moves.shard % seqs).astype(jnp.int32)[None]
    tokens, normed_half = norm_in(at, tokens_came, column(ln1_gain), column(ln1_bias))
    events = [*events, normed_half]
    home = moves.shard // seqs
    seg = jnp.where(home == core, segments, segments_other)
    seg = lax.dynamic_index_in_dim(seg, moves.shard % seqs, 1, keepdims=False)

    normed_half, *grad_pieces = late([normed_half, *grad_pieces], events)
    if moves.square:
        heads_low, heads_high = late([heads_low, heads_high], events)
        other_low, other_high = moves.over_core(heads_low), moves.over_core(heads_high)
        events = [other_low, other_high]
    else:
        events = []
    normed_other = moves.over_core(normed_half)
    grad_came = moves.to_chips(grad_pieces)
    normed = moves.ordered(normed_half, normed_other)
    events = [*events, normed, *grad_came]

    normed, *grad_came = late([normed, *grad_came], events)
    ff_piece = late(ff_piece, events)
    if moves.square:
        ff_x = [moves.over_x(piece) for piece in ff_piece]
        ff_y = [moves.over_y(piece) for piece in ff_piece]
        w_qkv, w_out = lay_heads(
            moves.core_ref,
            moves.places,
            [heads_piece, heads_x, heads_y, heads_low, heads_high],
            [other_own, other_x, other_y, other_low, other_high],
            counts,
            taken,
            events,
        )
        events = [*ff_x, *ff_y]
    else:
        (qkv_half,) = moves.lay([mine_of[0]], ())
        qkv_other = moves.over_core(qkv_half)
        low = jnp.where(core == 0, qkv_half, qkv_other)
        high = jnp.where(core == 0, qkv_other, qkv_half)
        rows = taken[0]
        qkv_full = jnp.concatenate(
            [
                block[shard * rows + skip : (shard + 1) * rows]
                for shard in range(shard_count)
                for block, skip in ((low, 0), (high, 2 * rows - counts[0]))
            ],
            axis=0,
        )
        w_qkv = jnp.concatenate(
            [rows_of(qkv_full, part * width + first_row) for part in range(3)], axis=0
        )
        twice = (core == 1) & (jnp.arange(OWN) < HDIM)
        own = lax.dynamic_slice_in_dim(output_projection_weight, first_row, OWN, 1)
        (w_out,) = moves.lay([jnp.where(twice[None, :], 0, own).astype(BF16)], ())
        (w_up,), (w_down,) = moves.lay(ff_piece[:1], ()), moves.lay(ff_piece[1:], ())
        events = []
    grad_half = moves.in_half(late(grad_came, [w_qkv]))
    grad_across = moves.over_z(grad_half, 1)
    zeros = jnp.zeros((OWN,), F32)
    joined_bias = jnp.concatenate([rows_of(q_bias, first_row), zeros, rows_of(v_bias, first_row)])
    row_scale = jnp.where(jnp.arange(3 * OWN) < OWN, 0.125, 1.0).astype(F32)
    joined = product(
        w_qkv,
        normed,
        "nn",
        416,
        lambda value, at, bias, scale: (
            (value + bias[...]).astype(BF16).astype(F32) * scale[...],
        ),
        (column(joined_bias), column(row_scale)),
        name="project_qkv",
    )
    mixed, lse = attention(seg, joined, [])
    side = jnp.broadcast_to(core.astype(F32), (width, 1))
    halves = ((half_len, BF16), (half_len, BF16))

    def by_side(value, at, side_ref):
        first, second = value[:, :half_len], value[:, half_len:]
        mine = side_ref[...] == 0
        return jnp.where(mine, first, second), jnp.where(mine, second, first)

    branch, branch_sent = product(
        w_out, mixed, "nn", 400, by_side, (side,), halves, name="project_out"
    )
    events = [*events, branch_sent, grad_across]

    branch_sent, grad_half, grad_across = late([branch_sent, grad_half, grad_across], events)
    branch_came = moves.over_core(branch_sent)
    grad_other, grad_far = moves.over_core(grad_half), moves.over_core(grad_across)
    middle, norm_half = norm_mid(
        tokens, branch, branch_came, column(out_bias), column(ln2_gain), column(ln2_bias)
    )
    events = [norm_half, grad_other, grad_far]
    grad_out = [grad_half, grad_across, grad_other, grad_far]

    (norm_half,) = late([norm_half], events)
    norm_across = moves.over_z(norm_half, 1)
    norm_other = moves.over_core(norm_half)
    if moves.square:
        ff_x, ff_y = late(ff_x, events), late(ff_y, events)
        ff_low, ff_high = moves.over_x(ff_y[0]), moves.over_y(ff_x[1])
        laid = [
            lay_near(moves.places, near, 1) for near in zip(late(ff_piece, events), ff_x, ff_y)
        ]
        (w_up,) = lay_far(moves.places, (ff_low,), laid[0])
        (w_down,) = lay_far(moves.places, (ff_high,), laid[1])
        (norm_across,) = late([norm_across], [w_up, w_down])
    norm_far = moves.over_core(norm_across)
    normed_two = [norm_half, norm_across, norm_other, norm_far]

    activ, slope = product(
        w_up,
        normed_two,
        "nn",
        320,
        lambda value, at, bias: gelu_pair(value + bias[...]),
        (column(up_bias_own),),
        ((None, BF16), (None, BF16)),
        name="project_up",
        wait=grad_out,
    )

    def in_halves(value, at):
        half = value.shape[1] // 2
        return value[:, :half], value[:, half:]

    pairs = ((length, BF16), (length, BF16))

    def through_gelu(value, at, slope_ref):
        size = value.shape[1]
        slope_here = slope_ref[:, at * size : (at + 1) * size].astype(F32)
        grad = (value * slope_here).astype(BF16)
        sums = lane_sums(grad.astype(F32))
        return (grad, None, sums) if at < 2 else (None, grad, sums)

    ff_cut = 896 if width == 1600 else width // 256 * 128
    down_parts = moves.scatter_first([(grad_out, activ)], ff_cut)
    down_near = moves.scatter_near(down_parts)
    pre_here, pre_there, grad_pre_sums = product(
        w_down,
        grad_out,
        "tn",
        256,
        through_gelu,
        (slope,),
        (*pairs, (512, F32)),
        name="back_down",
        wait=down_parts[:1],
    )
    norm_there = product(w_up, pre_there, "tn", 256, name="back_up")

    norm_came = moves.over_core(norm_there)
    norm_here = product(
        w_up, pre_here, "tn", 256, name="back_up", wait=[norm_there, *down_near[1]]
    )
    events = [norm_came, norm_here]

    norm_came, norm_here = late([norm_came, norm_here], events)
    norm_last = moves.over_z(norm_here[:, half_len:] + norm_came[:, half_len:], 1)
    down_far = moves.scatter_far(down_near, events)
    down_here, down_there = product(
        w_down, activ, "nn", 320, in_halves, (), pairs, name="project_down", wait=events
    )
    up_parts = moves.scatter_first([([pre_here, pre_there], normed_two)], ff_cut, [down_there])
    events = [norm_last, *down_far[1], up_parts[0]]

    (norm_last,) = late([norm_last], events)
    grad_middle, grad_branch_half, mid_sums = norm_mid_back(
        (norm_here, norm_came, norm_last), middle, grad_half, column(ln2_gain), events
    )
    (down_part,) = late([moves.scatter_last(down_far, width)], [grad_branch_half])
    grad_branch = moves.ordered(grad_branch_half, moves.over_core(grad_branch_half))
    grad_mixed = product(w_out, grad_branch, "tn", OWN, name="back_out", wait=[down_part], share=0.01)
    upper = to_sixteen(down_part.shape[0] // 2)
    down_low, down_high = down_part[:upper], down_part[upper:]
    events = [grad_mixed, down_low, down_high]

    up_near = moves.scatter_near(up_parts, events)
    down_there, down_low, down_high = late([down_there, down_low, down_high], events)
    down_came = moves.over_core(down_there)
    down_come = [moves.alike(down_low)]
    grad_own = attention_back(seg, joined, mixed, grad_mixed, lse, events).reshape(3 * OWN, length)
    events = [*up_near[1], down_came, down_come[0], grad_own]

    (grad_own,) = late([grad_own], events)
    grad_heads = moves.over_core(grad_own)
    up_far = moves.scatter_far(up_near, events)
    (down_high,) = late([down_high], events)
    down_come.append(moves.alike(down_high))
    down_sent = down_here[:, half_len:] + down_came[:, half_len:]
    down_last = [moves.over_z(down_sent[:, : half_len // 2], 1)]
    padded = to_tiles(OWN)
    out_parts = moves.scatter_first([(grad_branch, mixed)], 512, events)
    norm_one, norm_one_sent = product(
        w_qkv, grad_own, "tn", 256, by_side, (side,), halves, name="back_qkv", wait=out_parts[:1]
    )
    events = [grad_heads, *up_far[1], down_come[1], norm_one_sent, down_last[0]]

    grad_heads, norm_one_sent = late([grad_heads, norm_one_sent], events)
    down_sum = moves.alike_sum(down_part, late(down_come, events))
    down_across = moves.over_z(down_sum, 1)
    down_sent = down_sent[:, half_len // 2 :]
    norm_one_came = moves.over_core(norm_one_sent)
    out_near = moves.scatter_near(out_parts, events)
    if moves.square:
        grad_rows = join_heads(
            moves.core_ref, grad_own, grad_heads, counts[0], taken[0], []
        )
    else:
        low = jnp.where(core == 0, grad_own, grad_heads)
        high = jnp.where(core == 0, grad_heads, grad_own)
        grad_joined = jnp.concatenate(
            [
                piece
                for part in range(3)
                for piece in (
                    low[part * OWN : (part + 1) * OWN],
                    high[part * OWN + HDIM : (part + 1) * OWN],
                )
            ],
            axis=0,
        )
        grad_rows = jnp.concatenate(
            [
                lax.dynamic_slice_in_dim(
                    grad_joined, shard * counts[0] + core * (counts[0] - taken[0]), taken[0], 0
                )
                for shard in range(shard_count)
            ],
            axis=0,
        )
    qkv_parts = moves.scatter_first([(grad_rows, normed)], ff_cut, events)
    events = [qkv_parts[0], norm_one_came, down_across, *out_near[1], down_sent]

    qkv_near = moves.scatter_near(qkv_parts, events)
    down_sent, norm_one_came = late([down_sent, norm_one_came], events)
    up_part = moves.scatter_last(up_far, width)
    (up_part,) = late([up_part], events)
    up_low, up_high = up_part[:upper], up_part[upper:]
    up_come = [moves.alike(up_low)]
    down_last.append(moves.over_z(down_sent, 1))
    input_half, in_sums = norm_in_back(
        (norm_one, norm_one_came), tokens, grad_middle, column(ln1_gain)
    )
    up_bias_grad = jnp.sum(grad_pre_sums, axis=1).reshape(shard_count, 1, strip)
    up_bias_grad = up_bias_grad * (jnp.arange(4)[None, :, None] == quarter).astype(F32)
    head_sums = jnp.sum(grad_own.astype(F32), axis=1).reshape(3, OWN)
    bias_sums = lax.dynamic_update_slice(
        jnp.zeros((3, width), F32), head_sums, (jnp.int32(0), first_row)
    )
    small = jnp.concatenate(
        [
            up_bias_grad.reshape(-1),
            jnp.sum(mid_sums, axis=2).reshape(-1),
            jnp.sum(in_sums, axis=2).reshape(-1),
            bias_sums[0],
            bias_sums[2],
        ]
    ).reshape(-1, 128)
    up_low_sum = moves.alike_sum(up_low, up_come)
    events = [*qkv_near[1], down_last[1], up_low_sum, input_half, small, up_high]

    qkv_far = moves.scatter_far(qkv_near, events)
    up_high, up_low_sum, small, *down_last = late(
        [up_high, up_low_sum, small, *down_last], events
    )
    down_last = jnp.concatenate(down_last, axis=1)
    up_come.append(moves.alike(up_high))
    up_across = [moves.over_z(up_low_sum, 1)]
    small = moves.small_cores(small)
    tokens_back = results(
        at, seqs, middle, (down_here, down_came, down_last), column(down_bias), input_half
    )
    events = [*qkv_far[1], up_come[1], up_across[0], small, *tokens_back]

    down_sum, down_across, small = late([down_sum, down_across, small], events)
    out_far = moves.scatter_far(out_near, events)
    small = moves.small_square(small)
    qkv_pair = moves.scatter_pair(qkv_far, width)
    out_part = moves.scatter_last(out_far, padded)
    down_other = moves.over_core(down_sum)
    down_far_other = moves.over_core(down_across)
    up_high_sum = moves.alike_sum(up_high, late(up_come[1:], events))
    out_halves = moves.halves(out_part) if moves.square else [out_part, out_part]
    events = [qkv_pair, *out_halves, down_other, down_far_other, up_high_sum, small]

    qkv_pair, up_high_sum, down_far_other, *out_halves = late(
        [qkv_pair, up_high_sum, down_far_other, *out_halves], events
    )
    tokens_back = late(tokens_back, events)
    qkv_full = moves.total_all(qkv_pair)
    up_across.append(moves.over_z(up_high_sum, 1))
    up_sum = jnp.concatenate([up_low_sum, up_high_sum], axis=0)
    out_pair = out_halves[0]
    if moves.square:
        out_pair = out_pair + moves.over_z(out_halves[1], 1)
    tokens_came = moves.from_chips(tokens_back)
    quarter_ref = quarter.astype(jnp.int32)[None]
    down_total = finish_down(
        quarter_ref, [down_sum, down_other, down_across, down_far_other], shard_count
    )
    events = [qkv_full, up_across[1], tokens_came, down_total, up_sum, out_pair]

    qkv_full, out_pair, up_sum, small, tokens_came, *up_across = late(
        [qkv_full, out_pair, up_sum, small, tokens_came, *up_across], events
    )
    qkv_sum = moves.total_halves(qkv_full)
    out_full = moves.total_all(out_pair)
    up_across = jnp.concatenate(up_across, axis=0)
    up_total = finish_up(
        quarter_ref, [up_sum, moves.over_core(up_sum), up_across, moves.over_core(up_across)]
    )
    result, input_grad = tokens_came[:, :width], tokens_came[:, width:].astype(F32)
    small = moves.small_columns(late([small], [up_total, input_grad])[0], 1)
    events = [*qkv_sum, out_full, small]

    (out_full,) = late([out_full], events)
    out_sum = moves.total_halves(out_full)
    small = moves.small_columns(late([small], events)[0], 2).reshape(-1)
    qkv_sum = moves.four(late(qkv_sum, events))
    qkv_total = moves.rows(qkv_sum, counts[0])
    out_sum = [*out_sum[:1], *late(out_sum[1:], [qkv_total])]
    out_total = moves.sides(moves.four(out_sum))

    up_bias_grad, rest = small[:ff], small[ff:]
    (
        ln2_gain_grad,
        ln2_bias_grad,
        down_bias_grad,
        out_bias_grad,
        ln1_gain_grad,
        ln1_bias_grad,
        q_bias_grad,
        v_bias_grad,
    ) = rest.reshape(8, width)

    return (
        result.transpose(2, 0, 1),
        input_grad.transpose(2, 0, 1),
        ln1_gain_grad,
        ln1_bias_grad,
        qkv_total,
        q_bias_grad,
        v_bias_grad,
        out_total,
        out_bias_grad,
        ln2_gain_grad,
        ln2_bias_grad,
        up_total,
        up_bias_grad,
        down_total,
        down_bias_grad,
    )


def solution(mesh):
    rows = P("shard", None)
    tokens = P("shard", "replica", None)
    in_specs = (
        tokens,
        tokens,
        P(None, "replica"),
        P(),
        P(),
        rows,
        P(),
        P(),
        rows,
        P(),
        P(),
        P(),
        rows,
        P(),
        rows,
        P(),
    )
    out_specs = (
        tokens,
        tokens,
        P(),
        P(),
        rows,
        P(),
        P(),
        rows,
        P(),
        P(),
        P(),
        rows,
        P(),
        rows,
        P(),
    )
    body = functools.partial(shards, mesh.shape["shard"], mesh.shape["replica"])
    return jax.shard_map(body, mesh=mesh, in_specs=in_specs, out_specs=out_specs, check_vma=False)
```

```python
import functools

import jax
import jax.numpy as jnp
from jax import lax
from jax.experimental import pallas as pl
from jax.experimental.pallas import tpu as pltpu
from jax.sharding import PartitionSpec as P

HEADS = 25
HDIM = 64
OWN_HEADS = HEADS // 2 + 1
FIRST_HEAD = HEADS // 2
OWN = OWN_HEADS * HDIM
BLOCK = 256
AXES = ("shard", "replica")
BF16 = jnp.bfloat16
F32 = jnp.float32


def dot(left, right, left_dim, right_dim):
    return lax.dot_general(
        left, right, (((left_dim,), (right_dim,)), ((), ())), preferred_element_type=F32
    )


COST_SCALE = 12


def cost(flops, bytes_accessed, share=1.0):
    return pl.CostEstimate(
        flops=int(flops * COST_SCALE * share),
        bytes_accessed=int(bytes_accessed * COST_SCALE * share),
        transcendentals=0,
    )


def gelu_pair(value):
    root = 0.7978845608028654
    cube = 0.044715
    square = value * value
    tanh = jnp.tanh(root * value * (1.0 + cube * square))
    half = 0.5 * (1.0 + tanh)
    slope = half + 0.5 * value * (1.0 - tanh * tanh) * root * (1.0 + 3.0 * cube * square)
    return value * half, slope


def fill_mask(seg_row, seg_col, mask, blocks):
    for q_at in range(blocks):
        for k_at in range(q_at + 1):
            keys = seg_col[pl.ds(k_at * BLOCK, BLOCK), :]
            queries = seg_row[:, pl.ds(q_at * BLOCK, BLOCK)]
            seen = keys == queries
            if k_at == q_at:
                k_place = lax.broadcasted_iota(jnp.int32, (BLOCK, BLOCK), 0)
                q_place = lax.broadcasted_iota(jnp.int32, (BLOCK, BLOCK), 1)
                seen = seen & (k_place <= q_place)
            mask[pl.ds(k_at * BLOCK, BLOCK), pl.ds(q_at * BLOCK, BLOCK)] = jnp.where(
                seen, 0.0, -1e30
            )


def forward_kernel(seg_row, seg_col, q_ref, k_ref, v_ref, *refs):
    o_ref, lse_ref, mask = refs[-3:]
    length = q_ref.shape[1]
    blocks = length // BLOCK

    @pl.when(pl.program_id(0) == 0)
    def _():
        fill_mask(seg_row, seg_col, mask, blocks)

    keys = k_ref[...].T
    for q_at in range(blocks):
        span = (q_at + 1) * BLOCK
        here = pl.ds(q_at * BLOCK, BLOCK)
        scores = dot(keys[:span], q_ref[:, here], 1, 0) + mask[:span, here]
        peak = jnp.max(scores, axis=0, keepdims=True)
        terms = jnp.exp(scores - peak)
        total = jnp.sum(terms, axis=0, keepdims=True)
        mixed = dot(v_ref[:, :span], terms.astype(BF16), 1, 0)
        o_ref[:, here] = (mixed / total).astype(BF16)
        lse_ref[0, :, here] = peak + jnp.log(total)


def backward_kernel(seg_row, seg_col, q_ref, k_ref, v_ref, o_ref, g_ref, lse_ref, *refs):
    grads, mask, acc = refs[-3:]
    length = q_ref.shape[1]
    blocks = length // BLOCK

    @pl.when(pl.program_id(0) == 0)
    def _():
        fill_mask(seg_row, seg_col, mask, blocks)

    keys = k_ref[...].T
    values = v_ref[...].T
    delta = jnp.sum(g_ref[...].astype(F32) * o_ref[...].astype(F32), axis=0, keepdims=True)
    lse = lse_ref[0]
    for k_at in range(blocks):
        low = k_at * BLOCK
        here = pl.ds(low, BLOCK)
        rest = pl.ds(low, length - low)
        scores = dot(keys[low : low + BLOCK], q_ref[:, rest], 1, 0) + mask[here, rest]
        soft = jnp.exp(scores - lse[:, low:])
        soft_grad = dot(values[low : low + BLOCK], g_ref[:, rest], 1, 0)
        score_grad = (soft * (soft_grad - delta[:, low:])).astype(BF16)
        grads[2, :, here] = dot(g_ref[:, rest], soft.astype(BF16), 1, 1).astype(BF16)
        grads[1, :, here] = dot(q_ref[:, rest], score_grad, 1, 1).astype(BF16)
        grad_q = dot(k_ref[:, here], score_grad, 1, 0)
        if k_at == 0:
            acc[...] = grad_q
        else:
            acc[:, rest] += grad_q
    grads[0] = (acc[...] * 0.125).astype(BF16)


def head_spec(first, length):
    return pl.BlockSpec((HDIM, length), lambda head: (first + head, 0))


def whole_spec(shape):
    return pl.BlockSpec(shape, lambda head: (0,) * len(shape))


def attention(seg, joined, wait):
    length = seg.shape[0]
    lse_spec = pl.BlockSpec((1, 1, length), lambda head: (head, 0, 0))
    pairs = OWN_HEADS * length * length
    return pl.pallas_call(
        forward_kernel,
        grid=(OWN_HEADS,),
        in_specs=[whole_spec((1, length)), whole_spec((length, 1))]
        + [head_spec(part * OWN_HEADS, length) for part in range(3)]
        + [pl.BlockSpec(memory_space=pl.ANY)] * len(wait),
        out_specs=[head_spec(0, length), lse_spec],
        out_shape=[
            jax.ShapeDtypeStruct((OWN, length), BF16),
            jax.ShapeDtypeStruct((OWN_HEADS, 1, length), F32),
        ],
        scratch_shapes=[pltpu.VMEM((length, length), F32)],
        compiler_params=pltpu.CompilerParams(vmem_limit_bytes=40 * 2**20),
        cost_estimate=cost(16 * pairs * HDIM, 8 * OWN * length),
        name="attention_forward",
    )(seg.reshape(1, length), seg.reshape(length, 1), joined, joined, joined, *wait)


def attention_back(seg, joined, mixed, grad, lse, wait):
    length = seg.shape[0]
    lse_spec = pl.BlockSpec((1, 1, length), lambda head: (head, 0, 0))
    pairs = OWN_HEADS * length * length
    return pl.pallas_call(
        backward_kernel,
        grid=(OWN_HEADS,),
        in_specs=[whole_spec((1, length)), whole_spec((length, 1))]
        + [head_spec(part * OWN_HEADS, length) for part in range(3)]
        + [head_spec(0, length), head_spec(0, length), lse_spec]
        + [pl.BlockSpec(memory_space=pl.ANY)] * len(wait),
        out_specs=pl.BlockSpec((3, HDIM, length), lambda head: (0, head, 0)),
        out_shape=jax.ShapeDtypeStruct((3, OWN, length), BF16),
        scratch_shapes=[pltpu.VMEM((length, length), F32), pltpu.VMEM((HDIM, length), F32)],
        compiler_params=pltpu.CompilerParams(vmem_limit_bytes=48 * 2**20),
        cost_estimate=cost(40 * pairs * HDIM, 16 * OWN * length),
        name="attention_backward",
    )(
        seg.reshape(1, length),
        seg.reshape(length, 1),
        joined,
        joined,
        joined,
        mixed,
        grad,
        lse,
        *wait,
    )


def product(left, rights, form, block, finish=None, extras=(), outs=((None, BF16),), name="product",
            wait=(), share=1.0):
    rights = rights if isinstance(rights, (list, tuple)) else [rights]
    many = len(rights)
    left_dim, right_dim = (0 if form == "tn" else 1), (1 if form == "nt" else 0)
    m, k = left.shape[1 - left_dim], left.shape[left_dim]
    size = rights[0].shape[1 - right_dim]
    n = size * many
    block = min(block, m)

    def body(left_ref, *refs):
        extra_refs = refs[many : many + len(extras)]
        out_refs = refs[many + len(extras) + len(wait) :]
        for at in range(many):
            value = dot(left_ref[...], refs[at][...], left_dim, right_dim)
            values = (value,)
            if finish is not None:
                values = finish(value, at, *extra_refs)
            for ref, part in zip(out_refs, values):
                if part is not None:
                    width = part.shape[1]
                    begin = at * width % ref.shape[1]
                    ref[:, begin : begin + width] = part.astype(ref.dtype)

    if form == "tn":
        left_spec = pl.BlockSpec((k, block), lambda i: (0, i))
    else:
        left_spec = pl.BlockSpec((block, k), lambda i: (i, 0))
    sizes = [(columns or n, kind) for columns, kind in outs]
    results = pl.pallas_call(
        body,
        grid=(pl.cdiv(m, block),),
        in_specs=[left_spec]
        + [
            pl.BlockSpec(right.shape, lambda i: (0, 0), pipeline_mode=pl.Buffered(1))
            for right in rights
        ]
        + [pl.BlockSpec((block, extra.shape[1]), lambda i: (i, 0)) for extra in extras]
        + [pl.BlockSpec(memory_space=pl.ANY)] * len(wait),
        out_specs=[pl.BlockSpec((block, columns), lambda i: (i, 0)) for columns, _ in sizes],
        out_shape=[jax.ShapeDtypeStruct((m, columns), kind) for columns, kind in sizes],
        compiler_params=pltpu.CompilerParams(vmem_limit_bytes=56 * 2**20),
        cost_estimate=cost(2 * m * n * k, 2 * (m * k + n * k + m * n), share),
        name=name,
    )(left, *rights, *extras, *wait)
    return results if len(outs) > 1 else results[0]


def lane_sums(value):
    return sum(value[:, at : at + 128] for at in range(0, value.shape[1], 128))


PARAMS = pltpu.CompilerParams(vmem_limit_bytes=56 * 2**20)


def norm_parts(rows):
    centre = rows - jnp.mean(rows, axis=0, keepdims=True)
    scale = lax.rsqrt(jnp.mean(centre * centre, axis=0, keepdims=True) + 1e-05)
    return centre * scale, scale


def norm_back(grad, unit, scale, gain):
    inner = grad * gain
    mean_inner = jnp.mean(inner, axis=0, keepdims=True)
    mean_cross = jnp.mean(inner * unit, axis=0, keepdims=True)
    return scale * (inner - mean_inner - unit * mean_cross)


def column_specs(shape, size, many):
    return [pl.BlockSpec((shape[0], size), lambda i, *_: (0, i))] * many


def fixed_specs(shape, many):
    return [pl.BlockSpec(shape, lambda i, *_: (0,) * len(shape))] * many


def norm_in(at, came, gain, bias):
    pieces = len(came)
    rows, count = came[0].shape

    def body(at_ref, *refs):
        gain_ref, bias_ref, tokens_ref, norm_ref = refs[pieces:]
        which = lax.rem(at_ref[0] - pl.program_id(0) + pieces, pieces)
        for piece in range(pieces):

            @pl.when(which == piece)
            def _(piece=piece):
                tokens_ref[...] = refs[piece][...]

        unit, _ = norm_parts(tokens_ref[...].astype(F32))
        norm_ref[...] = (unit * gain_ref[...] + bias_ref[...]).astype(BF16)

    return pl.pallas_call(
        body,
        grid_spec=pltpu.PrefetchScalarGridSpec(
            num_scalar_prefetch=1,
            grid=(pieces,),
            in_specs=fixed_specs((rows, count), pieces) + fixed_specs((rows, 1), 2),
            out_specs=column_specs((rows, pieces * count), count, 2),
        ),
        out_shape=[jax.ShapeDtypeStruct((rows, pieces * count), BF16)] * 2,
        compiler_params=PARAMS,
        cost_estimate=cost(0, 40 * rows * pieces * count),
        name="norm_in",
    )(at, *came, gain, bias)


def norm_mid(tokens, mine, came, shift, gain, bias):
    rows, columns = tokens.shape
    size = columns // 2

    def body(tokens_ref, mine_ref, came_ref, shift_ref, gain_ref, bias_ref, middle_ref, norm_ref):
        middle = mine_ref[...].astype(F32) + came_ref[...].astype(F32)
        middle = tokens_ref[...].astype(F32) + middle + shift_ref[...]
        middle_ref[...] = middle
        unit, _ = norm_parts(middle)
        norm_ref[...] = (unit * gain_ref[...] + bias_ref[...]).astype(BF16)

    return pl.pallas_call(
        body,
        grid=(2,),
        in_specs=column_specs((rows, columns), size, 3) + fixed_specs((rows, 1), 3),
        out_specs=column_specs((rows, columns), size, 2),
        out_shape=[
            jax.ShapeDtypeStruct((rows, columns), F32),
            jax.ShapeDtypeStruct((rows, columns), BF16),
        ],
        compiler_params=PARAMS,
        cost_estimate=cost(0, 40 * rows * columns),
        name="norm_mid",
    )(tokens, mine, came, shift, gain, bias)


def norm_mid_back(parts, middle, grad, gain, wait):
    rows, columns = middle.shape
    size = columns // 2
    many = len(parts)

    def body(*refs):
        middle_ref, grad_ref, gain_ref = refs[many : many + 3]
        out_ref, low_ref, sums_ref = refs[-3:]
        norm_grad = sum(ref[...].astype(F32) for ref in refs[:many])
        unit, scale = norm_parts(middle_ref[...])
        through = grad_ref[...].astype(F32)
        value = through + norm_back(norm_grad, unit, scale, gain_ref[...])
        out_ref[...] = value
        low_ref[...] = value.astype(BF16)
        sums = (norm_grad * unit, norm_grad, through, value.astype(BF16).astype(F32))
        for at, rows_of_sum in enumerate(sums):
            here = lane_sums(rows_of_sum)

            @pl.when(pl.program_id(0) == 0)
            def _(at=at, here=here):
                sums_ref[at] = here

            @pl.when(pl.program_id(0) > 0)
            def _(at=at, here=here):
                sums_ref[at] += here

    return pl.pallas_call(
        body,
        grid=(2,),
        in_specs=column_specs((rows, columns), size, many + 2)
        + fixed_specs((rows, 1), 1)
        + [pl.BlockSpec(memory_space=pl.ANY)] * len(wait),
        out_specs=column_specs((rows, columns), size, 2) + fixed_specs((4, rows, 128), 1),
        out_shape=[
            jax.ShapeDtypeStruct((rows, columns), F32),
            jax.ShapeDtypeStruct((rows, columns), BF16),
            jax.ShapeDtypeStruct((4, rows, 128), F32),
        ],
        compiler_params=PARAMS,
        cost_estimate=cost(0, 60 * rows * columns),
        name="norm_mid_back",
    )(*parts, middle, grad, gain, *wait)


def norm_in_back(parts, tokens, grad, gain):
    rows, columns = tokens.shape
    size = columns // 2
    many = len(parts)

    def body(*refs):
        tokens_ref, grad_ref, gain_ref, out_ref, sums_ref = refs[many:]
        norm_grad = sum(ref[...].astype(F32) for ref in refs[:many])
        unit, scale = norm_parts(tokens_ref[...].astype(F32))
        value = grad_ref[...] + norm_back(norm_grad, unit, scale, gain_ref[...])
        out_ref[...] = value.astype(BF16)
        for at, rows_of_sum in enumerate((norm_grad * unit, norm_grad)):
            here = lane_sums(rows_of_sum)

            @pl.when(pl.program_id(0) == 0)
            def _(at=at, here=here):
                sums_ref[at] = here

            @pl.when(pl.program_id(0) > 0)
            def _(at=at, here=here):
                sums_ref[at] += here

    return pl.pallas_call(
        body,
        grid=(2,),
        in_specs=column_specs((rows, columns), size, many + 2) + fixed_specs((rows, 1), 1),
        out_specs=column_specs((rows, columns), size, 1) + fixed_specs((2, rows, 128), 1),
        out_shape=[
            jax.ShapeDtypeStruct((rows, columns), BF16),
            jax.ShapeDtypeStruct((2, rows, 128), F32),
        ],
        compiler_params=PARAMS,
        cost_estimate=cost(0, 60 * rows * columns),
        name="norm_in_back",
    )(*parts, tokens, grad, gain)


def results(at, pieces, middle, parts, shift, input_half):
    rows, columns = middle.shape
    size = columns // pieces
    many = len(parts)

    def body(at_ref, middle_ref, *refs):
        shift_ref, input_ref = refs[many : many + 2]
        outs = refs[many + 2 :]
        value = middle_ref[...] + shift_ref[...]
        for ref in refs[:many]:
            value = value + ref[...].astype(F32)
        value = value.astype(BF16)
        which = lax.rem(at_ref[0] - pl.program_id(0) + pieces, pieces)
        for piece, out in enumerate(outs):

            @pl.when(which == piece)
            def _(out=out):
                out[:rows] = value
                out[rows:] = input_ref[...]

    block = column_specs((rows, columns), size, 1)
    return pl.pallas_call(
        body,
        grid_spec=pltpu.PrefetchScalarGridSpec(
            num_scalar_prefetch=1,
            grid=(pieces,),
            in_specs=block * (1 + many) + fixed_specs((rows, 1), 1) + block,
            out_specs=fixed_specs((2 * rows, size), pieces),
        ),
        out_shape=[jax.ShapeDtypeStruct((2 * rows, size), BF16)] * pieces,
        compiler_params=PARAMS,
        cost_estimate=cost(0, 40 * rows * columns),
        name="results",
    )(at, middle, *parts, shift, input_half)


def lay(places, near, far, parts):
    count, columns = near[0].shape
    size = count // parts
    kind = near[0].dtype

    def body(places_ref, *refs):
        step = pl.program_id(0)
        outs = refs[5:]
        for at in range(3):

            @pl.when(step == at)
            def _(at=at):
                for index, out in enumerate(outs):
                    out[...] = refs[at][index * size : (index + 1) * size]

        @pl.when(step == 3)
        def _():
            start = 0
            for ref in refs[3:5]:
                rows = ref.shape[0]
                for index, out in enumerate(outs):
                    low, high = max(start, index * size), min(start + rows, (index + 1) * size)
                    if low < high:
                        out[low - index * size : high - index * size] = ref[
                            low - start : high - start
                        ]
                start += rows

    pieces = list(near) + list(far)
    return pl.pallas_call(
        body,
        grid_spec=pltpu.PrefetchScalarGridSpec(
            num_scalar_prefetch=1,
            grid=(4,),
            in_specs=[
                pl.BlockSpec(piece.shape, lambda i, p: (0, 0), pipeline_mode=pl.Buffered(1))
                for piece in pieces
            ],
            out_specs=[pl.BlockSpec((size, columns), lambda i, p: (p[i], 0))] * parts,
        ),
        out_shape=[jax.ShapeDtypeStruct((4 * size, columns), kind)] * parts,
        compiler_params=pltpu.CompilerParams(vmem_limit_bytes=56 * 2**20),
        cost_estimate=cost(0, 16 * count * columns),
        name="lay",
    )(places, *pieces)


def lay_near(places, near, parts):
    count, columns = near[0].shape
    size = count // parts

    def body(places_ref, *refs):
        for at in range(3):

            @pl.when(pl.program_id(0) == at)
            def _(at=at):
                for index, out in enumerate(refs[3:]):
                    out[...] = refs[at][index * size : (index + 1) * size]

    return pl.pallas_call(
        body,
        grid_spec=pltpu.PrefetchScalarGridSpec(
            num_scalar_prefetch=1,
            grid=(3,),
            in_specs=[
                pl.BlockSpec(piece.shape, lambda i, p: (0, 0), pipeline_mode=pl.Buffered(1))
                for piece in near
            ],
            out_specs=[pl.BlockSpec((size, columns), lambda i, p: (p[i], 0))] * parts,
        ),
        out_shape=[jax.ShapeDtypeStruct((4 * size, columns), near[0].dtype)] * parts,
        compiler_params=PARAMS,
        cost_estimate=cost(0, 12 * count * columns),
        name="lay_near",
    )(places, *near)


def lay_far(places, far, laid):
    parts = len(far)
    size, columns = far[0].shape

    def body(places_ref, *refs):
        for ref, out in zip(refs[:parts], refs[2 * parts :]):
            out[...] = ref[...]

    return pl.pallas_call(
        body,
        grid_spec=pltpu.PrefetchScalarGridSpec(
            num_scalar_prefetch=1,
            grid=(1,),
            in_specs=[pl.BlockSpec(piece.shape, lambda i, p: (0, 0)) for piece in far]
            + [pl.BlockSpec(memory_space=pl.ANY)] * parts,
            out_specs=[pl.BlockSpec((size, columns), lambda i, p: (p[3], 0))] * parts,
        ),
        out_shape=[jax.ShapeDtypeStruct(array.shape, array.dtype) for array in laid],
        input_output_aliases={1 + parts + index: index for index in range(parts)},
        compiler_params=PARAMS,
        cost_estimate=cost(0, 4 * size * columns),
        name="lay_far",
    )(places, *far, *laid)


def lay_heads(core, places, mine, others, counts, taken, wait):
    width = mine[0].shape[1]
    split = mine[3].shape[0]
    cut = FIRST_HEAD * HDIM

    def body(core_ref, places_ref, *refs):
        heads_ref, out_ref, block, out_block = refs[-4:]
        step = pl.program_id(0)

        def copy(halves, at, begin, end, target, row):
            if at < 3:
                target[row : row + end - begin] = halves[at][begin:end]
                return
            if begin < split:
                middle = min(end, split)
                target[row : row + middle - begin] = halves[3][begin:middle]
            if end > split:
                middle = max(begin, split)
                target[row + middle - begin : row + end - begin] = halves[4][
                    middle - split : end - split
                ]

        for which in range(2):

            @pl.when(core_ref[0] == which)
            def _(which=which):
                low, high = (refs[:5], refs[5:10]) if which == 0 else (refs[5:10], refs[:5])
                for at in range(4):

                    @pl.when(step == at)
                    def _(at=at):
                        begin = 0
                        for target, rows, count in zip((block, out_block), taken, counts):
                            copy(low, at, begin, begin + rows, target, 0)
                            over = 2 * rows - count
                            copy(high, at, begin + over, begin + rows, target, rows)
                            begin += rows

                out_ref[...] = out_block[:, which * cut : which * cut + OWN]
                if which == 1:
                    out_ref[:, :HDIM] = jnp.zeros((counts[1], HDIM), BF16)
                for shard in range(4):

                    @pl.when(places_ref[step] == shard)
                    def _(shard=shard):
                        for part in range(3):
                            begin = part * width + which * cut
                            first = max(begin, shard * counts[0])
                            last = min(begin + OWN, (shard + 1) * counts[0])
                            if first < last:
                                heads_ref[
                                    part * OWN + first - begin : part * OWN + last - begin
                                ] = block[first - shard * counts[0] : last - shard * counts[0]]

    pieces = list(mine) + list(others)
    return pl.pallas_call(
        body,
        grid_spec=pltpu.PrefetchScalarGridSpec(
            num_scalar_prefetch=2,
            grid=(4,),
            in_specs=[
                pl.BlockSpec(piece.shape, lambda i, c, p: (0, 0), pipeline_mode=pl.Buffered(1))
                for piece in pieces
            ]
            + [pl.BlockSpec(memory_space=pl.ANY)] * len(wait),
            out_specs=[
                pl.BlockSpec(
                    (3 * OWN, width), lambda i, c, p: (0, 0), pipeline_mode=pl.Buffered(1)
                ),
                pl.BlockSpec((counts[1], OWN), lambda i, c, p: (p[i], 0)),
            ],
            scratch_shapes=[pltpu.VMEM((count, width), BF16) for count in counts],
        ),
        out_shape=[
            jax.ShapeDtypeStruct((3 * OWN, width), BF16),
            jax.ShapeDtypeStruct((4 * counts[1], OWN), BF16),
        ],
        compiler_params=pltpu.CompilerParams(vmem_limit_bytes=56 * 2**20),
        cost_estimate=cost(0, 16 * counts[0] * width),
        name="lay_heads",
    )(core, places, *pieces, *wait)


def join_heads(core, own, other, count, taken, wait):
    length = own.shape[1]
    rows = 2 * OWN - HDIM

    def body(core_ref, own_ref, other_ref, *refs):
        out = refs[-1]
        step = pl.program_id(0)
        for which in range(2):
            for shard in range(4):

                @pl.when((core_ref[0] == which) & (step == shard))
                def _(which=which, shard=shard):
                    low, high = (own_ref, other_ref) if which == 0 else (other_ref, own_ref)
                    begin = shard * count + which * (count - taken)
                    at = begin
                    while at < begin + taken:
                        part, row = at // rows, at % rows
                        source, skip, last = (
                            (low, 0, OWN) if row < OWN else (high, OWN - HDIM, rows)
                        )
                        end = min(begin + taken, part * rows + last)
                        first = part * OWN + row - skip
                        out[at - begin : end - begin] = source[first : first + end - at]
                        at = end

    whole = pl.BlockSpec(own.shape, lambda i, c: (0, 0), pipeline_mode=pl.Buffered(1))
    return pl.pallas_call(
        body,
        grid_spec=pltpu.PrefetchScalarGridSpec(
            num_scalar_prefetch=1,
            grid=(4,),
            in_specs=[whole, whole] + [pl.BlockSpec(memory_space=pl.ANY)] * len(wait),
            out_specs=pl.BlockSpec((taken, length), lambda i, c: (i, 0)),
        ),
        out_shape=jax.ShapeDtypeStruct((4 * taken, length), BF16),
        compiler_params=pltpu.CompilerParams(vmem_limit_bytes=56 * 2**20),
        cost_estimate=cost(0, 12 * rows * length),
        name="join_heads",
    )(core, own, other, *wait)


def product_parts(order, pairs, cut, wait):
    many = len(pairs)
    lefts = [side_of(left) for left, _ in pairs]
    rights = [side_of(right) for _, right in pairs]
    count = lefts[0][0].shape[0] // 4
    depth = sum(piece.shape[1] for piece in lefts[0])
    columns = rights[0][0].shape[0]
    rest = columns - cut
    filled = to_tiles(rest)
    starts = [0]
    for sides in lefts + rights:
        starts.append(starts[-1] + len(sides))

    def body(order_ref, *refs):
        send_x, send_y, keep_x, keep_y = refs[starts[-1] + len(wait) :]
        step = pl.program_id(0)
        targets = ((send_x, send_y), (send_x, keep_y), (keep_x, send_y), (keep_x, keep_y))
        for pair in range(many):

            @pl.when(step // 4 == pair)
            def _(pair=pair):
                left = refs[starts[pair] : starts[pair + 1]]
                right = refs[starts[many + pair] : starts[many + pair + 1]]
                value = side_product(left, right).astype(BF16)
                for at, (along_x, along_y) in enumerate(targets):

                    @pl.when(step % 4 == at)
                    def _(along_x=along_x, along_y=along_y):
                        along_x[...] = value[:, :cut]
                        along_y[:, :rest] = value[:, cut:]
                        if filled > rest:
                            along_y[:, rest:] = jnp.zeros((count, filled - rest), BF16)

    def left_spec(pair, piece):
        return pl.BlockSpec(
            (count, piece.shape[1]), lambda i, o: (o[jnp.clip(i - 4 * pair, 0, 3)], 0)
        )

    def out_spec(size, second):
        return pl.BlockSpec(
            (count, size), lambda i, o: (jnp.where(i % 4 >= second, many, 0) + i // 4, 0)
        )

    return pl.pallas_call(
        body,
        grid_spec=pltpu.PrefetchScalarGridSpec(
            num_scalar_prefetch=1,
            grid=(4 * many,),
            in_specs=[left_spec(pair, piece) for pair in range(many) for piece in lefts[pair]]
            + [
                pl.BlockSpec(piece.shape, lambda i, o: (0, 0), pipeline_mode=pl.Buffered(1))
                for right in rights
                for piece in right
            ]
            + [pl.BlockSpec(memory_space=pl.ANY)] * len(wait),
            out_specs=[
                out_spec(cut, 1),
                out_spec(filled, 2),
                out_spec(cut, 3),
                out_spec(filled, 3),
            ],
        ),
        out_shape=[
            jax.ShapeDtypeStruct((2 * many * count, size), BF16)
            for size in (cut, filled, cut, filled)
        ],
        compiler_params=pltpu.CompilerParams(vmem_limit_bytes=56 * 2**20),
        cost_estimate=cost(8 * many * count * depth * columns, 8 * many * count * (depth + columns)),
        name="product_parts",
    )(order, *[piece for sides in lefts + rights for piece in sides], *wait)


def side_of(side):
    return list(side) if isinstance(side, (list, tuple)) else [side]


def side_product(left, right):
    total = None
    size = min(piece.shape[1] for piece in (*left, *right))
    depth = sum(piece.shape[1] for piece in left)

    def chunk(pieces, begin):
        width = pieces[0].shape[1]
        return pieces[begin // width][:, begin % width : begin % width + size]

    for begin in range(0, depth, size):
        value = dot(chunk(left, begin), chunk(right, begin), 1, 1)
        total = value if total is None else total + value
    return total


def to_tiles(count):
    return -(-count // 128) * 128


def fold(keep_x, came_x, last_x, keep_y, came_y, last_y, columns, even=None):
    rows, cut = last_x.shape
    filled = last_y.shape[1]
    rest = columns - cut
    block = 400 if even is None else rows // 2
    steps = rows // block

    def fill(refs, out):
        for first, begin, size in ((0, 0, cut), (3, cut, rest)):
            value = refs[first][:, :size].astype(F32) + refs[first + 1][:, :size].astype(F32)
            value = value + refs[first + 2][:, :size].astype(F32)
            out[:, begin : begin + size] = value.astype(BF16)

    def body(*refs):
        if even is None:
            fill(refs[:6], refs[6])
            return
        mine = pl.program_id(0) == refs[0][0]

        @pl.when(mine)
        def _():
            fill(refs[1:7], refs[7])

        @pl.when(jnp.logical_not(mine))
        def _():
            fill(refs[1:7], refs[8])

    def specs(size):
        second = pl.BlockSpec((block, size), lambda i, *_: (steps + i, 0))
        return [second, second, pl.BlockSpec((block, size), lambda i, *_: (i, 0))]

    if even is not None:
        return pl.pallas_call(
            body,
            grid_spec=pltpu.PrefetchScalarGridSpec(
                num_scalar_prefetch=1,
                grid=(2,),
                in_specs=specs(cut) + specs(filled),
                out_specs=fixed_specs((block, columns), 2),
            ),
            out_shape=[jax.ShapeDtypeStruct((block, columns), BF16)] * 2,
            compiler_params=PARAMS,
            cost_estimate=cost(0, 8 * rows * columns, 0.01),
            name="fold_halves",
        )(even, keep_x, came_x, last_x, keep_y, came_y, last_y)
    return pl.pallas_call(
        body,
        grid=(steps,),
        in_specs=specs(cut) + specs(filled),
        out_specs=pl.BlockSpec((block, columns), lambda i: (i, 0)),
        out_shape=jax.ShapeDtypeStruct((rows, columns), BF16),
        compiler_params=pltpu.CompilerParams(vmem_limit_bytes=56 * 2**20),
        cost_estimate=cost(0, 8 * rows * columns, 0.01),
        name="fold",
    )(keep_x, came_x, last_x, keep_y, came_y, last_y)


def finish_up(quarter, parts):
    rows, width = parts[0].shape

    def body(quarter_ref, *refs):
        for at in range(4):

            @pl.when(pl.program_id(0) == at)
            def _(at=at):
                refs[4][...] = refs[at][...].astype(F32)

    return pl.pallas_call(
        body,
        grid_spec=pltpu.PrefetchScalarGridSpec(
            num_scalar_prefetch=1,
            grid=(4,),
            in_specs=[
                pl.BlockSpec((rows, width), lambda i, q: (0, 0), pipeline_mode=pl.Buffered(1))
            ]
            * 4,
            out_specs=pl.BlockSpec((rows, width), lambda i, q: (q[0] ^ i, 0)),
        ),
        out_shape=jax.ShapeDtypeStruct((4 * rows, width), F32),
        compiler_params=pltpu.CompilerParams(vmem_limit_bytes=56 * 2**20),
        cost_estimate=cost(0, 24 * rows * width),
        name="finish_up",
    )(quarter, *parts)


def finish_down(quarter, parts, shard_count):
    rows, width = parts[0].shape
    strip = width // shard_count
    block = 80 if rows % 80 == 0 else 40
    steps = rows // block

    def body(quarter_ref, *refs):
        for which in range(4):

            @pl.when(quarter_ref[0] == which)
            def _(which=which):
                for shard in range(shard_count):
                    for at in range(4):
                        begin = (4 * shard + at) * strip
                        refs[4][:, begin : begin + strip] = refs[which ^ at][
                            :, shard * strip : (shard + 1) * strip
                        ].astype(F32)

    return pl.pallas_call(
        body,
        grid_spec=pltpu.PrefetchScalarGridSpec(
            num_scalar_prefetch=1,
            grid=(steps,),
            in_specs=[pl.BlockSpec((block, width), lambda i, q: (i, 0))] * 4,
            out_specs=pl.BlockSpec((block, 4 * width), lambda i, q: (i, 0)),
        ),
        out_shape=jax.ShapeDtypeStruct((rows, 4 * width), F32),
        compiler_params=pltpu.CompilerParams(vmem_limit_bytes=56 * 2**20),
        cost_estimate=cost(0, 24 * rows * width),
        name="finish_down",
    )(quarter, *parts)


def finish_sides(core, even, parts):
    rows, width = parts[0].shape
    cut = FIRST_HEAD * HDIM

    def body(core_ref, even_ref, *refs):
        for which in range(2):
            for at in range(2):

                @pl.when((core_ref[0] == which) & (pl.program_id(0) == at))
                def _(which=which, at=at):
                    own, other = refs[at], refs[2 + at]
                    low, high = (own, other) if which == 0 else (other, own)
                    refs[4][:, :cut] = low[:, :cut].astype(F32)
                    refs[4][:, cut:] = high[:, :OWN].astype(F32)

    return pl.pallas_call(
        body,
        grid_spec=pltpu.PrefetchScalarGridSpec(
            num_scalar_prefetch=2,
            grid=(2,),
            in_specs=[
                pl.BlockSpec((rows, width), lambda i, c, e: (0, 0), pipeline_mode=pl.Buffered(1))
            ]
            * 4,
            out_specs=pl.BlockSpec((rows, cut + OWN), lambda i, c, e: (e[0] ^ i, 0)),
        ),
        out_shape=jax.ShapeDtypeStruct((2 * rows, cut + OWN), F32),
        compiler_params=pltpu.CompilerParams(vmem_limit_bytes=56 * 2**20),
        cost_estimate=cost(0, 16 * rows * width),
        name="finish_sides",
    )(core, even, *parts)


def finish_rows(core, even, parts, count):
    rows, width = parts[0].shape
    over = 4 * rows - count

    def body(core_ref, even_ref, *refs):
        out = refs[4]
        for which in range(2):
            for parity in range(2):

                @pl.when((core_ref[0] == which) & (even_ref[0] == parity))
                def _(which=which, parity=parity):
                    mine = [refs[parity], refs[1 - parity]]
                    others = [refs[2 + parity], refs[3 - parity]]
                    low, high = (mine, others) if which == 0 else (others, mine)
                    for at in range(2):

                        @pl.when(pl.program_id(0) == at)
                        def _(at=at):
                            out[...] = low[at][...].astype(F32)

                    @pl.when(pl.program_id(0) == 2)
                    def _():
                        out[: rows - over] = high[0][over:].astype(F32)
                        out[rows - over :] = high[1][:over].astype(F32)

                    @pl.when(pl.program_id(0) == 3)
                    def _():
                        out[: rows - over] = high[1][over:].astype(F32)

    return pl.pallas_call(
        body,
        grid_spec=pltpu.PrefetchScalarGridSpec(
            num_scalar_prefetch=2,
            grid=(4,),
            in_specs=[
                pl.BlockSpec((rows, width), lambda i, c, e: (0, 0), pipeline_mode=pl.Buffered(1))
            ]
            * 4,
            out_specs=pl.BlockSpec((rows, width), lambda i, c, e: (i, 0)),
        ),
        out_shape=jax.ShapeDtypeStruct((count, width), F32),
        compiler_params=pltpu.CompilerParams(vmem_limit_bytes=56 * 2**20),
        cost_estimate=cost(0, 24 * rows * width),
        name="finish_rows",
    )(core, even, *parts)


def to_sixteen(count):
    return -(-count // 16) * 16


def late(arrays, events):
    arrays = list(arrays)
    events = [event for event in events if event is not None]
    if not events:
        return arrays
    return lax.optimization_barrier((*arrays, *events))[: len(arrays)]


class Moves:
    def __init__(self, shard_count, replica_count):
        self.shard_count = shard_count
        self.replica_count = replica_count
        self.shard = lax.axis_index("shard")
        replica = lax.axis_index("replica")
        self.core = replica % 2
        self.column = replica // 2
        self.square = shard_count == 4 and replica_count == 8
        self.core_ref = self.core.astype(jnp.int32)[None]
        me = self.shard
        self.places = jnp.stack([me, me ^ 1, me ^ 2, me ^ 3]).astype(jnp.int32)
        self.order = jnp.stack([me ^ 3, me ^ 1, me ^ 2, me]).astype(jnp.int32)

    def move(self, array, route):
        pairs, stays = [], []
        for shard in range(self.shard_count):
            for column in range(self.replica_count // 2):
                for core in range(2):
                    target = route(shard, column, core)
                    if target == (shard, column, core):
                        stays.append((shard, core))
                    elif target is not None:
                        to_shard, to_column, to_core = target
                        pairs.append(
                            (
                                shard * self.replica_count + 2 * column + core,
                                to_shard * self.replica_count + 2 * to_column + to_core,
                            )
                        )
        came = lax.ppermute(array, AXES, pairs)
        if not stays:
            return came
        table = [(s, c) in stays for s in range(self.shard_count) for c in range(2)]
        return jnp.where(jnp.asarray(table)[2 * self.shard + self.core], array, came)

    def over_x(self, array):
        return self.move(array, lambda s, z, c: (s ^ 1, z, c))

    def over_y(self, array):
        return self.move(array, lambda s, z, c: (s ^ 2, z, c))

    def over_z(self, array, step):
        return self.move(array, lambda s, z, c: (s, z ^ step, c))

    def over_core(self, array):
        return self.move(array, lambda s, z, c: (s, z, 1 - c))

    def lay(self, near, far, parts=1):
        if self.square:
            return lay(self.places, near, far, parts)
        size = near[0].shape[0] // parts
        return [
            lax.all_gather(near[0][at * size : (at + 1) * size], "shard", axis=0, tiled=True)
            for at in range(parts)
        ]

    def scatter_first(self, pairs, cut, wait=()):
        if not self.square:
            return [
                product(
                    jnp.concatenate(side_of(left), axis=1),
                    jnp.concatenate(side_of(right), axis=1),
                    "nt",
                    400,
                )
                for left, right in pairs
            ]
        return product_parts(self.order, pairs, cut, wait)

    def scatter_near(self, parts, wait=()):
        if not self.square:
            return parts, []
        send_x, send_y = late(parts[:2], wait)
        return parts, [self.over_x(send_x), self.over_y(send_y)]

    def scatter_far(self, near, wait=()):
        parts, came = near
        if not self.square:
            return near, [], []
        keep_x, keep_y = parts[2:]
        half = keep_x.shape[0] // 2
        came_x, came_y = late(came, wait)
        sent_x, sent_y = keep_x[:half] + came_x[:half], keep_y[:half] + came_y[:half]
        return near, [self.over_y(sent_x), self.over_x(sent_y)], [sent_x, sent_y]

    def scatter_last(self, far, columns):
        (parts, came), last, _ = far
        if not self.square:
            sums = [
                lax.psum_scatter(part, "shard", scatter_dimension=0, tiled=True) for part in parts
            ]
            return jnp.concatenate(sums, axis=0)
        return fold(parts[2], came[0], last[0], parts[3], came[1], last[1], columns)

    def scatter_pair(self, far, columns):
        (parts, came), last, _ = far
        if not self.square:
            return self.scatter_last(far, columns)
        even = (self.column % 2).astype(jnp.int32)[None]
        keep, send = fold(parts[2], came[0], last[0], parts[3], came[1], last[1], columns, even)
        return keep + self.over_z(send, 1)

    def halves(self, array):
        rows = array.shape[0] // 2
        even = self.column % 2
        keep = lax.dynamic_slice_in_dim(array, even * rows, rows, 0)
        return keep, lax.dynamic_slice_in_dim(array, (1 - even) * rows, rows, 0)

    def total_all(self, pair):
        if not self.square:
            groups = [
                [2 * column + core for column in range(self.replica_count // 2)]
                for core in range(2)
            ]
            return lax.psum(pair, "replica", axis_index_groups=groups)
        return pair + self.over_z(pair, 2)

    def total_halves(self, full):
        return (full, self.over_z(full, 1)) if self.square else (full,)

    def four(self, sums):
        return list(sums) + [self.over_core(half) for half in sums]

    def sides(self, parts):
        even = (self.column % 2).astype(jnp.int32)[None]
        if self.square:
            return finish_sides(self.core_ref, even, parts)
        first = self.core == 0
        low, high = jnp.where(first, *parts), jnp.where(first, *parts[::-1])
        return jnp.concatenate([low[:, : FIRST_HEAD * HDIM], high[:, :OWN]], axis=1).astype(F32)

    def rows(self, parts, count):
        if self.square:
            even = (self.column % 2).astype(jnp.int32)[None]
            return finish_rows(self.core_ref, even, parts, count)
        first = self.core == 0
        low, high = jnp.where(first, *parts), jnp.where(first, *parts[::-1])
        return jnp.concatenate([low, high[2 * low.shape[0] - count :]], axis=0).astype(F32)

    def alike(self, array):
        return self.over_z(array, 2) if self.square else self.total_alike(array)

    def alike_sum(self, array, came):
        came = jnp.concatenate(came, axis=0)
        return array + came if self.square else came

    def total_alike(self, array):
        groups = [
            [2 * column + core for column in range(even, self.replica_count // 2, 2)]
            for even in range(2)
            for core in range(2)
        ]
        return lax.psum(array, "replica", axis_index_groups=groups)

    def small_cores(self, array):
        return array + self.over_core(array) if self.square else lax.psum(array, AXES)

    def small_square(self, array):
        if not self.square:
            return array
        array = array + self.over_x(array)
        return array + self.over_y(array)

    def small_columns(self, array, step):
        return array + self.over_z(array, step) if self.square else array

    def owners(self, step, seqs):
        return lambda s, z, c: (seqs * c + (s + step) % seqs, z, s // seqs)

    def pieces(self, local):
        seqs = local.shape[0]
        return [
            lax.dynamic_index_in_dim(local, (self.shard + step) % seqs, 0, keepdims=False)
            for step in range(seqs)
        ]

    def to_chips(self, pieces):
        seqs = len(pieces)
        return [
            self.move(piece, self.owners(step, seqs)) for step, piece in enumerate(pieces)
        ]

    def in_half(self, came):
        seqs = len(came)
        count = came[0].shape[1]
        at = self.shard % seqs
        if seqs == 2:
            first = at == 0
            return jnp.concatenate(
                [jnp.where(first, came[0], came[1]), jnp.where(first, came[1], came[0])], axis=1
            )
        ring = jnp.concatenate((came[::-1] * 2)[: 2 * seqs - 1], axis=1)
        return lax.dynamic_slice_in_dim(ring, (seqs - 1 - at) * count, seqs * count, 1)

    def from_chips(self, pieces):
        seqs = len(pieces)
        at = self.shard % seqs
        outs = []
        for step in range(seqs):
            route = self.owners(step, seqs)
            back = {}
            for s in range(self.shard_count):
                for z in range(self.replica_count // 2):
                    for c in range(2):
                        back[route(s, z, c)] = (s, z, c)
            outs.append(self.move(pieces[step], lambda s, z, c: back[(s, z, c)]))
        if seqs == 2:
            first = at == 0
            return jnp.stack(
                [jnp.where(first, outs[0], outs[1]), jnp.where(first, outs[1], outs[0])]
            )
        stacked = jnp.stack(outs)
        doubled = jnp.concatenate([stacked, stacked[: seqs - 1]], axis=0)
        return lax.dynamic_slice_in_dim(doubled, (seqs - at) % seqs, seqs, 0)

    def ordered(self, half, other):
        first = self.core == 0
        return jnp.concatenate(
            [jnp.where(first, half, other), jnp.where(first, other, half)], axis=1
        )


def shards(
    shard_count,
    replica_count,
    hidden_in,
    out_grad,
    segments,
    ln1_gain,
    ln1_bias,
    qkv_weight,
    q_bias,
    v_bias,
    output_projection_weight,
    out_bias,
    ln2_gain,
    ln2_bias,
    up_weight,
    up_bias,
    down_weight,
    down_bias,
):
    moves = Moves(shard_count, replica_count)
    core = moves.core
    quarter = 2 * (moves.column % 2) + core
    seqs = hidden_in.shape[1]
    width = hidden_in.shape[2]
    length = segments.shape[0]
    half_len = length // 2
    ff = up_bias.shape[0]
    strip = ff // shard_count // 4
    first_row = core * FIRST_HEAD * HDIM
    rows_of = functools.partial(lax.dynamic_slice_in_dim, slice_size=OWN, axis=0)

    def column(vector):
        return vector[:, None]


    counts = (qkv_weight.shape[0], output_projection_weight.shape[0])
    taken = tuple(to_sixteen(count // 2) for count in counts)
    mine_of = [
        lax.dynamic_slice_in_dim(weight, core * (count - rows), rows, 0)
        for weight, count, rows in zip((qkv_weight, output_projection_weight), counts, taken)
    ]
    ff_piece = [
        lax.dynamic_slice_in_dim(up_weight, quarter * strip, strip, 0),
        jnp.concatenate(
            [
                lax.dynamic_slice_in_dim(down_weight, (4 * shard + quarter) * strip, strip, 1)
                for shard in range(shard_count)
            ],
            axis=1,
        ),
    ]
    up_bias_own = lax.dynamic_index_in_dim(
        up_bias.reshape(shard_count, 4, strip), quarter, 1, keepdims=False
    ).reshape(-1)
    tokens_came = moves.to_chips(moves.pieces(hidden_in.transpose(1, 2, 0)))
    grad_pieces = moves.pieces(out_grad.transpose(1, 2, 0))
    if moves.square:
        heads_piece = jnp.concatenate(mine_of, axis=0)
        heads_x, heads_y = moves.over_x(heads_piece), moves.over_y(heads_piece)
        other_own = moves.over_core(heads_piece)
        events = [heads_x, heads_y, other_own, *tokens_came, *ff_piece, *grad_pieces]

        heads_x, heads_y, segments_sent, *tokens_came = late(
            [heads_x, heads_y, segments, *tokens_came], events
        )
        split = to_sixteen(heads_piece.shape[0] // 2)
        heads_low = moves.over_x(heads_y[:split])
        heads_high = moves.over_y(heads_x[split:])
        other_x, other_y = moves.over_core(heads_x), moves.over_core(heads_y)
        segments_other = moves.over_core(segments_sent)
        events = [heads_low, heads_high, other_x, other_y, segments_other]
    else:
        segments_other = moves.over_core(segments)
        events = []
    at = (moves.shard % seqs).astype(jnp.int32)[None]
    tokens, normed_half = norm_in(at, tokens_came, column(ln1_gain), column(ln1_bias))
    events = [*events, normed_half]
    home = moves.shard // seqs
    seg = jnp.where(home == core, segments, segments_other)
    seg = lax.dynamic_index_in_dim(seg, moves.shard % seqs, 1, keepdims=False)

    normed_half, *grad_pieces = late([normed_half, *grad_pieces], events)
    if moves.square:
        heads_low, heads_high = late([heads_low, heads_high], events)
        other_low, other_high = moves.over_core(heads_low), moves.over_core(heads_high)
        events = [other_low, other_high]
    else:
        events = []
    normed_other = moves.over_core(normed_half)
    grad_came = moves.to_chips(grad_pieces)
    normed = moves.ordered(normed_half, normed_other)
    events = [*events, normed, *grad_came]

    normed, *grad_came = late([normed, *grad_came], events)
    ff_piece = late(ff_piece, events)
    if moves.square:
        ff_x = [moves.over_x(piece) for piece in ff_piece]
        ff_y = [moves.over_y(piece) for piece in ff_piece]
        w_qkv, w_out = lay_heads(
            moves.core_ref,
            moves.places,
            [heads_piece, heads_x, heads_y, heads_low, heads_high],
            [other_own, other_x, other_y, other_low, other_high],
            counts,
            taken,
            events,
        )
        events = [*ff_x, *ff_y]
    else:
        (qkv_half,) = moves.lay([mine_of[0]], ())
        qkv_other = moves.over_core(qkv_half)
        low = jnp.where(core == 0, qkv_half, qkv_other)
        high = jnp.where(core == 0, qkv_other, qkv_half)
        rows = taken[0]
        qkv_full = jnp.concatenate(
            [
                block[shard * rows + skip : (shard + 1) * rows]
                for shard in range(shard_count)
                for block, skip in ((low, 0), (high, 2 * rows - counts[0]))
            ],
            axis=0,
        )
        w_qkv = jnp.concatenate(
            [rows_of(qkv_full, part * width + first_row) for part in range(3)], axis=0
        )
        twice = (core == 1) & (jnp.arange(OWN) < HDIM)
        own = lax.dynamic_slice_in_dim(output_projection_weight, first_row, OWN, 1)
        (w_out,) = moves.lay([jnp.where(twice[None, :], 0, own).astype(BF16)], ())
        (w_up,), (w_down,) = moves.lay(ff_piece[:1], ()), moves.lay(ff_piece[1:], ())
        events = []
    grad_half = moves.in_half(late(grad_came, [w_qkv]))
    grad_across = moves.over_z(grad_half, 1)
    zeros = jnp.zeros((OWN,), F32)
    joined_bias = jnp.concatenate([rows_of(q_bias, first_row), zeros, rows_of(v_bias, first_row)])
    row_scale = jnp.where(jnp.arange(3 * OWN) < OWN, 0.125, 1.0).astype(F32)
    joined = product(
        w_qkv,
        normed,
        "nn",
        416,
        lambda value, at, bias, scale: (
            (value + bias[...]).astype(BF16).astype(F32) * scale[...],
        ),
        (column(joined_bias), column(row_scale)),
        name="project_qkv",
    )
    mixed, lse = attention(seg, joined, [])
    side = jnp.broadcast_to(core.astype(F32), (width, 1))
    halves = ((half_len, BF16), (half_len, BF16))

    def by_side(value, at, side_ref):
        first, second = value[:, :half_len], value[:, half_len:]
        mine = side_ref[...] == 0
        return jnp.where(mine, first, second), jnp.where(mine, second, first)

    branch, branch_sent = product(
        w_out, mixed, "nn", 400, by_side, (side,), halves, name="project_out"
    )
    events = [*events, branch_sent, grad_across]

    branch_sent, grad_half, grad_across = late([branch_sent, grad_half, grad_across], events)
    branch_came = moves.over_core(branch_sent)
    grad_other, grad_far = moves.over_core(grad_half), moves.over_core(grad_across)
    middle, norm_half = norm_mid(
        tokens, branch, branch_came, column(out_bias), column(ln2_gain), column(ln2_bias)
    )
    events = [norm_half, grad_other, grad_far]
    grad_out = [grad_half, grad_across, grad_other, grad_far]

    (norm_half,) = late([norm_half], events)
    norm_across = moves.over_z(norm_half, 1)
    norm_other = moves.over_core(norm_half)
    if moves.square:
        ff_x, ff_y = late(ff_x, events), late(ff_y, events)
        ff_low, ff_high = moves.over_x(ff_y[0]), moves.over_y(ff_x[1])
        laid = [
            lay_near(moves.places, near, 1) for near in zip(late(ff_piece, events), ff_x, ff_y)
        ]
        (w_up,) = lay_far(moves.places, (ff_low,), laid[0])
        (w_down,) = lay_far(moves.places, (ff_high,), laid[1])
        (norm_across,) = late([norm_across], [w_up, w_down])
    norm_far = moves.over_core(norm_across)
    normed_two = [norm_half, norm_across, norm_other, norm_far]

    activ, slope = product(
        w_up,
        normed_two,
        "nn",
        320,
        lambda value, at, bias: gelu_pair(value + bias[...]),
        (column(up_bias_own),),
        ((None, BF16), (None, BF16)),
        name="project_up",
        wait=grad_out,
    )

    def in_halves(value, at):
        half = value.shape[1] // 2
        return value[:, :half], value[:, half:]

    pairs = ((length, BF16), (length, BF16))

    def through_gelu(value, at, slope_ref):
        size = value.shape[1]
        slope_here = slope_ref[:, at * size : (at + 1) * size].astype(F32)
        grad = (value * slope_here).astype(BF16)
        sums = lane_sums(grad.astype(F32))
        return (grad, None, sums) if at < 2 else (None, grad, sums)

    ff_cut = 896 if width == 1600 else width // 256 * 128
    down_parts = moves.scatter_first([(grad_out, activ)], ff_cut)
    down_near = moves.scatter_near(down_parts)
    pre_here, pre_there, grad_pre_sums = product(
        w_down,
        grad_out,
        "tn",
        256,
        through_gelu,
        (slope,),
        (*pairs, (512, F32)),
        name="back_down",
        wait=down_parts[:1],
    )
    norm_there = product(w_up, pre_there, "tn", 256, name="back_up")

    norm_came = moves.over_core(norm_there)
    norm_here = product(
        w_up, pre_here, "tn", 256, name="back_up", wait=[norm_there, *down_near[1]]
    )
    events = [norm_came, norm_here]

    norm_came, norm_here = late([norm_came, norm_here], events)
    norm_last = moves.over_z(norm_here[:, half_len:] + norm_came[:, half_len:], 1)
    down_far = moves.scatter_far(down_near, events)
    down_here, down_there = product(
        w_down, activ, "nn", 320, in_halves, (), pairs, name="project_down", wait=events
    )
    up_parts = moves.scatter_first([([pre_here, pre_there], normed_two)], ff_cut, [down_there])
    events = [norm_last, *down_far[1], up_parts[0]]

    (norm_last,) = late([norm_last], events)
    grad_middle, grad_branch_half, mid_sums = norm_mid_back(
        (norm_here, norm_came, norm_last), middle, grad_half, column(ln2_gain), events
    )
    (down_part,) = late([moves.scatter_last(down_far, width)], [grad_branch_half])
    grad_branch = moves.ordered(grad_branch_half, moves.over_core(grad_branch_half))
    grad_mixed = product(w_out, grad_branch, "tn", OWN, name="back_out", wait=[down_part], share=0.01)
    upper = to_sixteen(down_part.shape[0] // 2)
    down_low, down_high = down_part[:upper], down_part[upper:]
    events = [grad_mixed, down_low, down_high]

    up_near = moves.scatter_near(up_parts, events)
    down_there, down_low, down_high = late([down_there, down_low, down_high], events)
    down_came = moves.over_core(down_there)
    down_come = [moves.alike(down_low)]
    grad_own = attention_back(seg, joined, mixed, grad_mixed, lse, events).reshape(3 * OWN, length)
    events = [*up_near[1], down_came, down_come[0], grad_own]

    (grad_own,) = late([grad_own], events)
    grad_heads = moves.over_core(grad_own)
    up_far = moves.scatter_far(up_near, events)
    (down_high,) = late([down_high], events)
    down_come.append(moves.alike(down_high))
    down_sent = down_here[:, half_len:] + down_came[:, half_len:]
    down_last = [moves.over_z(down_sent[:, : half_len // 2], 1)]
    padded = to_tiles(OWN)
    out_parts = moves.scatter_first([(grad_branch, mixed)], 512, events)
    norm_one, norm_one_sent = product(
        w_qkv, grad_own, "tn", 256, by_side, (side,), halves, name="back_qkv", wait=out_parts[:1]
    )
    events = [grad_heads, *up_far[1], down_come[1], norm_one_sent, down_last[0]]

    grad_heads, norm_one_sent = late([grad_heads, norm_one_sent], events)
    down_sum = moves.alike_sum(down_part, late(down_come, events))
    down_across = moves.over_z(down_sum, 1)
    down_sent = down_sent[:, half_len // 2 :]
    norm_one_came = moves.over_core(norm_one_sent)
    out_near = moves.scatter_near(out_parts, events)
    if moves.square:
        grad_rows = join_heads(
            moves.core_ref, grad_own, grad_heads, counts[0], taken[0], []
        )
    else:
        low = jnp.where(core == 0, grad_own, grad_heads)
        high = jnp.where(core == 0, grad_heads, grad_own)
        grad_joined = jnp.concatenate(
            [
                piece
                for part in range(3)
                for piece in (
                    low[part * OWN : (part + 1) * OWN],
                    high[part * OWN + HDIM : (part + 1) * OWN],
                )
            ],
            axis=0,
        )
        grad_rows = jnp.concatenate(
            [
                lax.dynamic_slice_in_dim(
                    grad_joined, shard * counts[0] + core * (counts[0] - taken[0]), taken[0], 0
                )
                for shard in range(shard_count)
            ],
            axis=0,
        )
    qkv_parts = moves.scatter_first([(grad_rows, normed)], ff_cut, events)
    events = [qkv_parts[0], norm_one_came, down_across, *out_near[1], down_sent]

    qkv_near = moves.scatter_near(qkv_parts, events)
    down_sent, norm_one_came = late([down_sent, norm_one_came], events)
    up_part = moves.scatter_last(up_far, width)
    (up_part,) = late([up_part], events)
    up_low, up_high = up_part[:upper], up_part[upper:]
    up_come = [moves.alike(up_low)]
    down_last.append(moves.over_z(down_sent, 1))
    input_half, in_sums = norm_in_back(
        (norm_one, norm_one_came), tokens, grad_middle, column(ln1_gain)
    )
    up_bias_grad = jnp.sum(grad_pre_sums, axis=1).reshape(shard_count, 1, strip)
    up_bias_grad = up_bias_grad * (jnp.arange(4)[None, :, None] == quarter).astype(F32)
    head_sums = jnp.sum(grad_own.astype(F32), axis=1).reshape(3, OWN)
    bias_sums = lax.dynamic_update_slice(
        jnp.zeros((3, width), F32), head_sums, (jnp.int32(0), first_row)
    )
    small = jnp.concatenate(
        [
            up_bias_grad.reshape(-1),
            jnp.sum(mid_sums, axis=2).reshape(-1),
            jnp.sum(in_sums, axis=2).reshape(-1),
            bias_sums[0],
            bias_sums[2],
        ]
    ).reshape(-1, 128)
    up_low_sum = moves.alike_sum(up_low, up_come)
    events = [*qkv_near[1], down_last[1], up_low_sum, input_half, small, up_high]

    qkv_far = moves.scatter_far(qkv_near, events)
    up_high, up_low_sum, small, *down_last = late(
        [up_high, up_low_sum, small, *down_last], events
    )
    down_last = jnp.concatenate(down_last, axis=1)
    up_come.append(moves.alike(up_high))
    up_across = [moves.over_z(up_low_sum, 1)]
    small = moves.small_cores(small)
    tokens_back = results(
        at, seqs, middle, (down_here, down_came, down_last), column(down_bias), input_half
    )
    events = [*qkv_far[1], up_come[1], up_across[0], small, *tokens_back]

    down_sum, down_across, small = late([down_sum, down_across, small], events)
    out_far = moves.scatter_far(out_near, events)
    small = moves.small_square(small)
    qkv_pair = moves.scatter_pair(qkv_far, width)
    out_part = moves.scatter_last(out_far, padded)
    down_other = moves.over_core(down_sum)
    down_far_other = moves.over_core(down_across)
    up_high_sum = moves.alike_sum(up_high, late(up_come[1:], events))
    out_halves = moves.halves(out_part) if moves.square else [out_part, out_part]
    events = [qkv_pair, *out_halves, down_other, down_far_other, up_high_sum, small]

    qkv_pair, up_high_sum, down_far_other, *out_halves = late(
        [qkv_pair, up_high_sum, down_far_other, *out_halves], events
    )
    tokens_back = late(tokens_back, events)
    qkv_full = moves.total_all(qkv_pair)
    up_across.append(moves.over_z(up_high_sum, 1))
    up_sum = jnp.concatenate([up_low_sum, up_high_sum], axis=0)
    out_pair = out_halves[0]
    if moves.square:
        out_pair = out_pair + moves.over_z(out_halves[1], 1)
    tokens_came = moves.from_chips(tokens_back)
    quarter_ref = quarter.astype(jnp.int32)[None]
    down_total = finish_down(
        quarter_ref, [down_sum, down_other, down_across, down_far_other], shard_count
    )
    events = [qkv_full, up_across[1], tokens_came, down_total, up_sum, out_pair]

    qkv_full, out_pair, up_sum, small, tokens_came, *up_across = late(
        [qkv_full, out_pair, up_sum, small, tokens_came, *up_across], events
    )
    qkv_sum = moves.total_halves(qkv_full)
    out_full = moves.total_all(out_pair)
    up_across = jnp.concatenate(up_across, axis=0)
    up_total = finish_up(
        quarter_ref, [up_sum, moves.over_core(up_sum), up_across, moves.over_core(up_across)]
    )
    result, input_grad = tokens_came[:, :width], tokens_came[:, width:].astype(F32)
    small = moves.small_columns(late([small], [up_total, input_grad])[0], 1)
    events = [*qkv_sum, out_full, small]

    (out_full,) = late([out_full], events)
    out_sum = moves.total_halves(out_full)
    small = moves.small_columns(late([small], events)[0], 2).reshape(-1)
    qkv_sum = moves.four(late(qkv_sum, events))
    qkv_total = moves.rows(qkv_sum, counts[0])
    out_sum = [*out_sum[:1], *late(out_sum[1:], [qkv_total])]
    out_total = moves.sides(moves.four(out_sum))

    up_bias_grad, rest = small[:ff], small[ff:]
    (
        ln2_gain_grad,
        ln2_bias_grad,
        down_bias_grad,
        out_bias_grad,
        ln1_gain_grad,
        ln1_bias_grad,
        q_bias_grad,
        v_bias_grad,
    ) = rest.reshape(8, width)

    return (
        result.transpose(2, 0, 1),
        input_grad.transpose(2, 0, 1),
        ln1_gain_grad,
        ln1_bias_grad,
        qkv_total,
        q_bias_grad,
        v_bias_grad,
        out_total,
        out_bias_grad,
        ln2_gain_grad,
        ln2_bias_grad,
        up_total,
        up_bias_grad,
        down_total,
        down_bias_grad,
    )


def solution(mesh):
    rows = P("shard", None)
    tokens = P("shard", "replica", None)
    in_specs = (
        tokens,
        tokens,
        P(None, "replica"),
        P(),
        P(),
        rows,
        P(),
        P(),
        rows,
        P(),
        P(),
        P(),
        rows,
        P(),
        rows,
        P(),
    )
    out_specs = (
        tokens,
        tokens,
        P(),
        P(),
        rows,
        P(),
        P(),
        rows,
        P(),
        P(),
        P(),
        rows,
        P(),
        rows,
        P(),
    )
    body = functools.partial(shards, mesh.shape["shard"], mesh.shape["replica"])
    return jax.shard_map(body, mesh=mesh, in_specs=in_specs, out_specs=out_specs, check_vma=False)
```
